32 devices in a mesh: dp: 4 (over y, x), fsdp: 8 (over z, core).
Axes of the slice: x: 2, y: 2, z: 4, core: 2. Of those that a mesh axis runs over, the one named last changes fastest.
Arguments:
- tokens: bfloat16 [2, 8192, 1024], P(None, ('dp', 'fsdp')), may hold values from -6 to 6
- lengths: int32 [2, 32, 4], P(None, ('dp', 'fsdp')), may hold values from 0 to 256, as said below
- mix_weight: bfloat16 [1024, 3072], P(('dp', 'fsdp')), may hold values from -0.1875 to 0.1875
- out_weight: bfloat16 [1024, 1024], P(('dp', 'fsdp')), may hold values from -0.5 to 0.5
- up_weight: bfloat16 [1024, 4096], P(('dp', 'fsdp')), may hold values from -0.1875 to 0.1875
- down_weight: bfloat16 [4096, 1024], P(('dp', 'fsdp')), may hold values from -0.09375 to 0.09375
- attn_gain: bfloat16 [1024], P(('dp', 'fsdp')), may hold values from 0.099609375 to 1.8984375
- attn_bias: bfloat16 [1024], P(('dp', 'fsdp')), may hold values from -3 to 3
- feed_gain: bfloat16 [1024], P(('dp', 'fsdp')), may hold values from 0.099609375 to 1.8984375
- feed_bias: bfloat16 [1024], P(('dp', 'fsdp')), may hold values from -3 to 3
- feature_freq: float32 [64, 64], replicated, may hold values from -4 to 4
- feature_scale: float32 [64], replicated, may hold values from 0.5 to 2
- cotangent: bfloat16 [2, 8192, 1024], P(None, ('dp', 'fsdp')), may hold values from -6 to 6
Outputs:
- out: bfloat16 [2, 8192, 1024], P(None, ('dp', 'fsdp'))
- grad_tokens: float32 [2, 8192, 1024], P(None, ('dp', 'fsdp'))
- grad_mix: float32 [1024, 3072], P(('dp', 'fsdp'))
- grad_out: float32 [1024, 1024], P(('dp', 'fsdp'))
- grad_up: float32 [1024, 4096], P(('dp', 'fsdp'))
- grad_down: float32 [4096, 1024], P(('dp', 'fsdp'))
- grad_attn_gain: float32 [1024], P(('dp', 'fsdp'))
- grad_attn_bias: float32 [1024], P(('dp', 'fsdp'))
- grad_feed_gain: float32 [1024], P(('dp', 'fsdp'))
- grad_feed_bias: float32 [1024], P(('dp', 'fsdp'))
The draws below stay inside these ranges and needn't reach their ends.
Inputs may be any that keep to these rules, and one draw needn't show every extreme that they name: A slot's lengths are those of its packed sequences in order, 0 for unused places; they sum to at least 192 and at most 256, the rest of the slot being padding; the first slot of each micro-batch holds one sequence of 256 tokens.
All inputs are finite; a program needn't handle non-finite values.
Results may differ from the reference program's by a relative error of at most 0.012.
The reference program's roundings to bfloat16 on the way count: a program that leaves them out, or rounds other values in their place, can miss the bound.
Values may be sent and summed in bfloat16 or wider, within the bound.
A program may use at most 256 MiB of HBM per device.

```python
import math
import jax
import jax.numpy as jnp
from jax import lax

D = 1024
FF = 4096
HEADS = 16
HEAD = 64
ROT = 16
FEAT = 64
SEGS = 4
MICRO = 2
SLOT = 256
SLOTS = 32
TOKENS = 8192


def draw_lengths(key, part):
    key = jax.random.fold_in(key, 7)
    fill_key, cut_key = jax.random.split(key)
    slot_count = MICRO * SLOTS
    padding = jax.random.randint(fill_key, (slot_count,), 0, SLOT // 4 + 1)
    filled = SLOT - padding
    cut_points = jax.random.randint(cut_key, (slot_count, SEGS - 1), 0, SLOT + 1)
    cut_points = jnp.sort(jnp.minimum(cut_points, filled[:, None]), axis=1)
    boundaries = jnp.concatenate([jnp.zeros((slot_count, 1), jnp.int32), cut_points, filled[:, None]], axis=1)
    span_table = (boundaries[:, 1:] - boundaries[:, :-1]).reshape(MICRO, SLOTS, SEGS)
    full_slot = jnp.concatenate([jnp.full((MICRO, 1, 1), SLOT, jnp.int32), jnp.zeros((MICRO, 1, SEGS - 1), jnp.int32)], axis=2)
    span_table = jnp.concatenate([full_slot, span_table[:, 1:]], axis=1)
    return span_table.astype(jnp.int32)


def shard_levels(key, extent, cuts, smallest, high):
    def one(dim, parts):
        steps = jax.random.uniform(jax.random.fold_in(jax.random.fold_in(key, 6), dim), (parts,), jnp.float32, smallest / len(cuts), high / len(cuts))
        return jnp.repeat(jnp.exp(steps), extent[dim] // parts).reshape((-1,) + (1,) * (len(extent) - dim - 1))

    loudness = one(*cuts[0])
    for cut in cuts[1:]:
        loudness = loudness * one(*cut)
    return loudness


def noise(own_key, extent, scale, bound, cuts=(), held_as=jnp.bfloat16):
    values = scale * jax.random.normal(own_key, extent, jnp.float32)
    if cuts:
        values = values * shard_levels(own_key, extent, cuts, -0.22, 0.18)
    return jnp.clip(values, -bound, bound).astype(held_as)


def setup_inputs(seed: int = 0) -> dict:
    key_list = jax.random.split(jax.random.key(seed), 14)
    tokens = noise(key_list[0], (MICRO, TOKENS, D), 1.0, 6.0, ((1, 32),))
    lengths = draw_lengths(jax.random.fold_in(key_list[13], 71), 0)
    mix_weight = noise(key_list[2], (D, 3 * D), D ** -0.5, 0.1875, ((0, 32),))
    out_weight = noise(key_list[3], (D, D), (D // 8) ** -0.5, 0.5, ((0, 32),))
    up_weight = noise(key_list[4], (D, FF), D ** -0.5, 0.1875, ((0, 32),))
    down_weight = noise(key_list[5], (FF, D), FF ** -0.5, 0.09375, ((0, 32),))
    attn_gain = jnp.clip(1.0 + 0.18 * jax.random.normal(key_list[6], (D,), jnp.float32), 0.099609375, 1.8984375).astype(jnp.bfloat16)
    attn_bias = noise(key_list[7], (D,), 0.5, 3.0, ((0, 32),))
    feed_gain = jnp.clip(1.0 + 0.18 * jax.random.normal(key_list[8], (D,), jnp.float32), 0.099609375, 1.8984375).astype(jnp.bfloat16)
    feed_bias = noise(key_list[9], (D,), 0.5, 3.0, ((0, 32),))
    feature_freq = noise(key_list[10], (FEAT, HEAD), 1.0, 4.0, (), jnp.float32)
    feature_scale = jnp.clip(jnp.exp(jax.random.uniform(key_list[11], (FEAT,), jnp.float32, math.log(0.5), math.log(2.0))), 0.5, 2.0)
    cotangent = noise(key_list[12], (MICRO, TOKENS, D), 1.0, 6.0, ((1, 32),))
    return {"tokens": tokens, "lengths": lengths, "mix_weight": mix_weight, "out_weight": out_weight, "up_weight": up_weight, "down_weight": down_weight, "attn_gain": attn_gain, "attn_bias": attn_bias, "feed_gain": feed_gain, "feed_bias": feed_bias, "feature_freq": feature_freq, "feature_scale": feature_scale, "cotangent": cotangent}


epsilon = 1e-05
exact_precision = lax.Precision.HIGHEST

@jax.custom_vjp
def low(v):
    return lax.optimization_barrier(v.astype(jnp.bfloat16)).astype(jnp.float32)

@jax.custom_vjp
def low_back(v):
    return v

def low_keep(v):
    return (low(v), None)

def low_pass(kept, grad):
    return (grad,)

def back_keep(v):
    return (v, None)

def back_low(kept, grad):
    return (low(grad),)
low.defvjp(low_keep, low_pass)
low_back.defvjp(back_keep, back_low)

def dct_matrix(width):
    order = jnp.arange(width, dtype=jnp.float32)[:, None]
    sample = jnp.arange(width, dtype=jnp.float32)[None, :]
    factor = jnp.where(order == 0, jnp.sqrt(1.0 / width), jnp.sqrt(2.0 / width))
    return factor * jnp.cos(math.pi * (2.0 * sample + 1.0) * order / (2.0 * width))

def feature_table(feature_freq):
    return low(jnp.dot(dct_matrix(HEAD).T, feature_freq.T, precision=exact_precision) / math.sqrt(HEAD))

def slot_layout(span_table, slot_len):
    seg_ends = jnp.cumsum(span_table, axis=-1).astype(jnp.int32)
    seg_starts = seg_ends - span_table
    places = jnp.arange(slot_len, dtype=jnp.int32)
    segment = lax.optimization_barrier(jnp.sum((places[:, None] >= seg_ends[..., None, :]).astype(jnp.int32), axis=-1))
    numbers = jnp.arange(span_table.shape[-1], dtype=jnp.int32)
    matched = segment[..., None] == numbers
    begin_at = lax.optimization_barrier(jnp.sum(jnp.where(matched, seg_starts[..., None, :], 0), axis=-1))
    begin_at = begin_at + jnp.where(segment == span_table.shape[-1], seg_ends[..., -1:], 0)
    position = (places - begin_at).astype(jnp.float32)
    valid = (segment < span_table.shape[-1]).astype(jnp.float32)
    return (segment, position, valid)

def rotate(raw_heads, position):
    half_rot = ROT // 2
    inverse = 10000.0 ** (-2.0 * jnp.arange(half_rot, dtype=jnp.float32) / ROT)
    angle = position[..., None] * inverse
    cosine_wave = jnp.cos(angle)[..., None, :]
    sine = jnp.sin(angle)[..., None, :]
    first = raw_heads[..., :half_rot]
    second = raw_heads[..., half_rot:ROT]
    return jnp.concatenate([first * cosine_wave - second * sine, second * cosine_wave + first * sine, raw_heads[..., ROT:]], axis=-1)

def feature_map(raw_heads, position, table, feature_scale):
    rotated_rows = low(rotate(raw_heads, position))
    pre = low_back(jnp.einsum('...hd,df->...hf', rotated_rows, table, precision=exact_precision))
    return feature_scale * jnp.exp(pre)

def norm_apply(inputs, gain, shift):
    center = inputs - lax.optimization_barrier(jnp.mean(inputs, axis=-1, keepdims=True))
    spread = lax.optimization_barrier(jnp.mean(center * center, axis=-1, keepdims=True))
    return center * lax.rsqrt(spread + epsilon) * gain + shift

def slot_attention(pieces):
    mapped_query, mapped_key, value_rows, segment = pieces
    places = jnp.arange(segment.shape[0], dtype=jnp.int32)
    allowed = (segment[:, None] == segment[None, :]) & (places[None, :] <= places[:, None])
    score_matrix = jnp.einsum('tnl,vnl->ntv', mapped_query, mapped_key, precision=exact_precision)
    score_matrix = low_back(jnp.where(allowed[None], score_matrix, 0.0))
    totals = lax.optimization_barrier(jnp.sum(score_matrix, axis=2))
    numerator = low_back(jnp.einsum('hqk,khd->qhd', low(score_matrix), value_rows, precision=exact_precision))
    return numerator / totals.T[:, :, None]

def forward_layer_pass(inputs, span_table, feature_freq, feature_scale, mix_weight, out_weight, up_weight, down_weight, attn_gain, attn_bias, feed_gain, feed_bias):
    table = feature_table(feature_freq)
    group_count = inputs.shape[0]
    segment, position, valid = slot_layout(span_table, SLOT)
    normed_attn = low(norm_apply(inputs, attn_gain, attn_bias))
    normed_feed = low(norm_apply(inputs, feed_gain, feed_bias))
    mixed = low_back(jnp.einsum('gsd,de->gse', normed_attn, mix_weight, precision=exact_precision))
    split_heads = mixed.reshape(group_count, SLOT, 3, HEADS, HEAD)
    mapped_query = low(feature_map(split_heads[:, :, 0], position, table, feature_scale))
    mapped_key = low(feature_map(split_heads[:, :, 1], position, table, feature_scale))
    value_rows = low(split_heads[:, :, 2])
    attended = lax.map(jax.checkpoint(slot_attention), (mapped_query, mapped_key, value_rows, segment))
    attended = low(attended.reshape(group_count, SLOT, D))
    attn_rows = jnp.einsum('gsd,de->gse', attended, out_weight, precision=exact_precision)
    hidden = low_back(jnp.einsum('gsd,df->gsf', normed_feed, up_weight, precision=exact_precision))
    active = low(jax.nn.gelu(hidden, approximate=False))
    feed_rows = jnp.einsum('gsf,fd->gsd', active, down_weight, precision=exact_precision)
    return inputs + valid[..., None] * (attn_rows + feed_rows)

def reference(tokens, lengths, mix_weight, out_weight, up_weight, down_weight, attn_gain, attn_bias, feed_gain, feed_bias, feature_freq, feature_scale, cotangent):
    group_slots = 1
    while group_slots * 2 * SLOT <= 4096 and SLOTS % (group_slots * 2) == 0:
        group_slots = group_slots * 2
    groups = MICRO * SLOTS // group_slots
    inputs = tokens.reshape(groups, group_slots, SLOT, D)
    span_groups = lengths.reshape(groups, group_slots, SEGS)
    cot_groups = cotangent.reshape(groups, group_slots, SLOT, D)
    weights = tuple((member.astype(jnp.float32) for member in (mix_weight, out_weight, up_weight, down_weight, attn_gain, attn_bias, feed_gain, feed_bias)))

    def step_group(running, pieces):
        group_rows, group_spans, group_cot = pieces

        def forward(rows_in, *params):
            return forward_layer_pass(rows_in, group_spans, feature_freq, feature_scale, *params)
        result, pullback = jax.vjp(forward, group_rows.astype(jnp.float32), *weights)
        gradients = pullback(group_cot.astype(jnp.float32))
        running = tuple((total_sum + update for total_sum, update in zip(running, gradients[1:])))
        return (running, (result.astype(jnp.bfloat16), gradients[0]))
    zero_grads = tuple((jnp.zeros(member.shape, jnp.float32) for member in weights))
    weight_grads, (output_rows, grad_inputs) = lax.scan(step_group, zero_grads, (inputs, span_groups, cot_groups))
    return (output_rows.reshape(MICRO, TOKENS, D), grad_inputs.reshape(MICRO, TOKENS, D), weight_grads[0], weight_grads[1], weight_grads[2], weight_grads[3], weight_grads[4], weight_grads[5], weight_grads[6], weight_grads[7])
```

```python
from functools import partial
import math

import jax
import jax.numpy as jnp
from jax import lax
from jax.experimental import pallas as pl
from jax.experimental.pallas import tpu as pltpu
from jax.sharding import PartitionSpec as P

D = 1024
HEAD = 64
ROT = 16


epsilon = 1e-05
exact_precision = lax.Precision.HIGHEST


def dct_matrix(width):
    order = jnp.arange(width, dtype=jnp.float32)[:, None]
    sample = jnp.arange(width, dtype=jnp.float32)[None, :]
    factor = jnp.where(order == 0, jnp.sqrt(1.0 / width), jnp.sqrt(2.0 / width))
    return factor * jnp.cos(math.pi * (2.0 * sample + 1.0) * order / (2.0 * width))


def feature_table(feature_freq):
    table = jnp.dot(dct_matrix(HEAD).T, feature_freq.T, precision=exact_precision) / math.sqrt(HEAD)
    return table.astype(jnp.bfloat16)


def slot_layout(span_table, slot_len):
    seg_ends = jnp.cumsum(span_table, axis=-1)
    seg_starts = seg_ends - span_table
    places = jnp.arange(slot_len, dtype=jnp.int32)
    segment = jnp.sum((places[:, None] >= seg_ends[..., None, :]).astype(jnp.int32), axis=-1)
    numbers = jnp.arange(span_table.shape[-1], dtype=jnp.int32)
    matched = segment[..., None] == numbers
    begin_at = jnp.sum(jnp.where(matched, seg_starts[..., None, :], 0), axis=-1)
    begin_at = begin_at + jnp.where(segment == span_table.shape[-1], seg_ends[..., -1:], 0)
    position = (places - begin_at).astype(jnp.float32)
    valid = (segment < span_table.shape[-1]).astype(jnp.float32)
    return (segment, position, valid)


def rotate(raw_heads, position):
    half_rot = ROT // 2
    inverse = 10000.0 ** (-2.0 * jnp.arange(half_rot, dtype=jnp.float32) / ROT)
    angle = position[..., None] * inverse
    cosine_wave = jnp.cos(angle)[..., None, :]
    sine = jnp.sin(angle)[..., None, :]
    first = raw_heads[..., :half_rot]
    second = raw_heads[..., half_rot:ROT]
    return jnp.concatenate(
        [
            first * cosine_wave - second * sine,
            second * cosine_wave + first * sine,
            raw_heads[..., ROT:],
        ],
        axis=-1,
    )


def feature_map(raw_heads, position, table, feature_scale):
    rotated_rows = rotate(raw_heads, position).astype(jnp.bfloat16)
    pre = jnp.einsum("shd,df->shf", rotated_rows, table, preferred_element_type=jnp.float32)
    return feature_scale * jnp.exp(pre)


def feature_back(raw_heads, grad_phi, position, table, feature_scale):
    phi = feature_map(raw_heads, position, table, feature_scale)
    grad_pre = (grad_phi * phi).astype(jnp.bfloat16)
    grad_turned = jnp.einsum("shf,df->shd", grad_pre, table, preferred_element_type=jnp.float32)
    _, turn_pull = jax.vjp(lambda values: rotate(values, position), raw_heads)
    return turn_pull(grad_turned)[0]


def norm_apply(inputs, gain, shift):
    center = inputs - jnp.mean(inputs, axis=-1, keepdims=True)
    spread = jnp.mean(center * center, axis=-1, keepdims=True)
    return center * lax.rsqrt(spread + epsilon) * gain + shift


def head_major(values):
    return jnp.swapaxes(values, 0, 1)


def attend_head(allowed, pieces):
    mapped_query, mapped_key, value_rows = pieces
    score_matrix = jnp.einsum(
        "qf,kf->qk", mapped_query, mapped_key, preferred_element_type=jnp.float32
    )
    score_matrix = jnp.where(allowed, score_matrix, 0.0)
    totals = jnp.sum(score_matrix, axis=1)
    numerator = jnp.dot(
        score_matrix.astype(jnp.bfloat16), value_rows, preferred_element_type=jnp.float32
    )
    return numerator / totals[:, None]


def attend_back(allowed, pieces):
    mapped_query, mapped_key, value_rows, grad_heads = pieces
    score_matrix = jnp.einsum(
        "qf,kf->qk", mapped_query, mapped_key, preferred_element_type=jnp.float32
    )
    score_matrix = jnp.where(allowed, score_matrix, 0.0)
    totals = jnp.sum(score_matrix, axis=1)
    scores_low = score_matrix.astype(jnp.bfloat16)
    numerator = jnp.dot(scores_low, value_rows, preferred_element_type=jnp.float32)
    grad_numer = (grad_heads / totals[:, None]).astype(jnp.bfloat16)
    grad_totals = -jnp.sum(grad_heads * numerator, axis=1) / (totals * totals)
    grad_scores = jnp.einsum(
        "qd,kd->qk", grad_numer, value_rows, preferred_element_type=jnp.float32
    )
    grad_scores = jnp.where(allowed, grad_scores + grad_totals[:, None], 0.0).astype(jnp.bfloat16)
    grad_query = jnp.dot(grad_scores, mapped_key, preferred_element_type=jnp.float32)
    grad_key = jnp.einsum(
        "qk,qf->kf", grad_scores, mapped_query, preferred_element_type=jnp.float32
    )
    grad_value = jnp.einsum("qk,qd->kd", scores_low, grad_numer, preferred_element_type=jnp.float32)
    return (grad_query, grad_key, grad_value)


def fetch_attention(shards):
    return (
        lax.all_gather(shards[0], ("dp", "fsdp"), axis=0, tiled=True),
        lax.all_gather(shards[1], ("dp", "fsdp"), axis=0, tiled=True),
        lax.all_gather(shards[2], ("dp", "fsdp"), axis=0, tiled=True),
        lax.all_gather(shards[3], ("dp", "fsdp"), axis=0, tiled=True),
    )


def fetch_feed(shards):
    return (
        lax.all_gather(shards[0], ("dp", "fsdp"), axis=0, tiled=True),
        lax.all_gather(shards[1], ("dp", "fsdp"), axis=0, tiled=True),
        lax.all_gather(shards[2], ("dp", "fsdp"), axis=0, tiled=True),
        lax.all_gather(shards[3], ("dp", "fsdp"), axis=0, tiled=True),
    )


def reduce_attention(grads):
    return (
        lax.psum_scatter(grads[0], ("dp", "fsdp"), scatter_dimension=0, tiled=True),
        lax.psum_scatter(grads[1], ("dp", "fsdp"), scatter_dimension=0, tiled=True),
        lax.psum_scatter(grads[2], ("dp", "fsdp"), scatter_dimension=0, tiled=True),
        lax.psum_scatter(grads[3], ("dp", "fsdp"), scatter_dimension=0, tiled=True),
    )


def reduce_feed(grads):
    return (
        lax.psum_scatter(grads[0], ("dp", "fsdp"), scatter_dimension=0, tiled=True),
        lax.psum_scatter(grads[1], ("dp", "fsdp"), scatter_dimension=0, tiled=True),
        lax.psum_scatter(grads[2], ("dp", "fsdp"), scatter_dimension=0, tiled=True),
        lax.psum_scatter(grads[3], ("dp", "fsdp"), scatter_dimension=0, tiled=True),
    )


def add_tuples(running, update):
    if running is None:
        return tuple(update)
    return tuple(jax.tree.map(jnp.add, tuple(running), tuple(update)))


def per_device_plain(
    tokens,
    lengths,
    mix_weight,
    out_weight,
    up_weight,
    down_weight,
    attn_gain,
    attn_bias,
    feed_gain,
    feed_bias,
    feature_freq,
    feature_scale,
    cotangent,
):
    table = feature_table(feature_freq)
    slot_len = tokens.shape[1]
    head_count = D // HEAD
    attn_shards = (mix_weight, out_weight, attn_gain, attn_bias)
    feed_shards = (up_weight, down_weight, feed_gain, feed_bias)
    places = jnp.arange(slot_len, dtype=jnp.int32)
    output_rows = []
    grad_inputs = []
    attn_total = None
    feed_total = None
    for micro_index in range(tokens.shape[0]):
        attn_full = fetch_attention(attn_shards)
        feed_full = fetch_feed(feed_shards)
        mix_full, out_full, gain_one, bias_one = attn_full
        up_full, down_full, gain_two, bias_two = feed_full
        gain_attn = gain_one.astype(jnp.float32)
        shift_attn = bias_one.astype(jnp.float32)
        gain_feed = gain_two.astype(jnp.float32)
        shift_feed = bias_two.astype(jnp.float32)
        inputs = tokens[micro_index].astype(jnp.float32)
        segment, position, valid = slot_layout(lengths[micro_index, 0], slot_len)
        allowed = (segment[:, None] == segment[None, :]) & (places[None, :] <= places[:, None])
        normed_attn = norm_apply(inputs, gain_attn, shift_attn).astype(jnp.bfloat16)
        normed_feed = norm_apply(inputs, gain_feed, shift_feed).astype(jnp.bfloat16)
        mixed = jnp.dot(normed_attn, mix_full, preferred_element_type=jnp.float32)
        mixed = mixed.reshape(slot_len, 3, head_count, HEAD)
        query_raw = mixed[:, 0]
        key_raw = mixed[:, 1]
        value_rows = mixed[:, 2].astype(jnp.bfloat16)
        mapped_query = feature_map(query_raw, position, table, feature_scale).astype(jnp.bfloat16)
        mapped_key = feature_map(key_raw, position, table, feature_scale).astype(jnp.bfloat16)
        attended = lax.map(
            partial(attend_head, allowed),
            (head_major(mapped_query), head_major(mapped_key), head_major(value_rows)),
        )
        attended = head_major(attended).reshape(slot_len, D).astype(jnp.bfloat16)
        attn_rows = jnp.dot(attended, out_full, preferred_element_type=jnp.float32)
        hidden = jnp.dot(normed_feed, up_full, preferred_element_type=jnp.float32)
        active = jax.nn.gelu(hidden, approximate=False).astype(jnp.bfloat16)
        feed_rows = jnp.dot(active, down_full, preferred_element_type=jnp.float32)
        result = inputs + valid[:, None] * (attn_rows + feed_rows)
        output_rows.append(result.astype(jnp.bfloat16))
        attn_full = fetch_attention(attn_shards)
        feed_full = fetch_feed(feed_shards)
        mix_full, out_full, gain_one, bias_one = attn_full
        up_full, down_full, gain_two, bias_two = feed_full
        grad_rows = cotangent[micro_index]
        grad_branch = jnp.where(valid[:, None] > 0.0, grad_rows, jnp.zeros_like(grad_rows))
        grad_down = jnp.einsum("sf,sd->fd", active, grad_branch, preferred_element_type=jnp.float32)
        grad_out = jnp.einsum(
            "sd,se->de", attended, grad_branch, preferred_element_type=jnp.float32
        )
        grad_active = jnp.einsum(
            "sd,fd->sf", grad_branch, down_full, preferred_element_type=jnp.float32
        )
        _, gelu_pull = jax.vjp(partial(jax.nn.gelu, approximate=False), hidden)
        grad_hidden = gelu_pull(grad_active)[0].astype(jnp.bfloat16)
        grad_up = jnp.einsum(
            "sd,sf->df", normed_feed, grad_hidden, preferred_element_type=jnp.float32
        )
        grad_normed_feed = jnp.einsum(
            "sf,df->sd", grad_hidden, up_full, preferred_element_type=jnp.float32
        )
        grad_attended = jnp.einsum(
            "sd,ed->se", grad_branch, out_full, preferred_element_type=jnp.float32
        )
        grad_attended = grad_attended.reshape(slot_len, head_count, HEAD)
        grad_phi_q, grad_phi_k, grad_value = lax.map(
            partial(attend_back, allowed),
            (
                head_major(mapped_query),
                head_major(mapped_key),
                head_major(value_rows),
                head_major(grad_attended),
            ),
        )
        grad_query = feature_back(query_raw, head_major(grad_phi_q), position, table, feature_scale)
        grad_key = feature_back(key_raw, head_major(grad_phi_k), position, table, feature_scale)
        grad_mixed = jnp.stack([grad_query, grad_key, head_major(grad_value)], axis=1)
        grad_mixed = grad_mixed.reshape(slot_len, 3 * D).astype(jnp.bfloat16)
        grad_mix = jnp.einsum(
            "sd,se->de", normed_attn, grad_mixed, preferred_element_type=jnp.float32
        )
        grad_normed_attn = jnp.einsum(
            "se,de->sd", grad_mixed, mix_full, preferred_element_type=jnp.float32
        )
        _, attn_norm_pull = jax.vjp(norm_apply, inputs, gain_attn, shift_attn)
        grad_in_one, grad_gain_one, grad_bias_one = attn_norm_pull(grad_normed_attn)
        _, feed_norm_pull = jax.vjp(norm_apply, inputs, gain_feed, shift_feed)
        grad_in_two, grad_gain_two, grad_bias_two = feed_norm_pull(grad_normed_feed)
        grad_inputs.append(grad_rows.astype(jnp.float32) + grad_in_one + grad_in_two)
        attn_grads = (grad_mix, grad_out, grad_gain_one, grad_bias_one)
        feed_grads = (grad_up, grad_down, grad_gain_two, grad_bias_two)
        attn_grads = reduce_attention(attn_grads)
        feed_grads = reduce_feed(feed_grads)
        attn_total = add_tuples(attn_total, attn_grads)
        feed_total = add_tuples(feed_total, feed_grads)
    return (
        jnp.stack(output_rows),
        jnp.stack(grad_inputs),
        attn_total[0],
        attn_total[1],
        feed_total[0],
        feed_total[1],
        attn_total[2],
        attn_total[3],
        feed_total[2],
        feed_total[3],
    )


MESH_ID = pl.DeviceIdType.MESH
LOW = jnp.bfloat16
WIDE = jnp.float32


def here(nz):
    dp = lax.axis_index("dp")
    fs = lax.axis_index("fsdp")
    return dp // 2, dp % 2, fs // 2, fs % 2


class Places:
    def __init__(self, ny, nz):
        self.ny, self.nz = ny, nz
        self.y, self.x, self.z, self.c = here(nz)

    def at(self, y, x, z, c):
        return (y * 2 + x, z * 2 + c)

    def member(self, r):
        x = 1 - self.x if r & 2 else self.x
        c = 1 - self.c if r & 1 else self.c
        return x, c

    def member_id(self, r):
        x, c = self.member(r)
        return self.at(self.y, x, self.z, c)

    def yid(self):
        return self.at(1 - self.y, self.x, self.z, self.c)

    def zid(self, step):
        return self.at(self.y, self.x, (self.z + step) % self.nz, self.c)

    def zsrc(self, step):
        return (self.z + self.nz - step) % self.nz

    def greet(self):
        barrier = pltpu.get_barrier_semaphore()
        ids = [self.member_id(r) for r in (1, 2, 3)] + [self.yid()]
        ids += [self.zid(step) for step in range(1, self.nz)]
        for one in ids:
            pl.semaphore_signal(barrier, inc=1, device_id=one, device_id_type=MESH_ID)
        pl.semaphore_wait(barrier, len(ids))


class Copy:
    def __init__(self, describe):
        self.describe = describe

    def start(self):
        self.describe().start()

    def wait_recv(self):
        self.describe().wait_recv()

    def wait_send(self):
        self.describe().wait_send()


class Links:
    def __init__(self, send, recv):
        self.send, self.recv, self.count, self.open = send, recv, 0, []

    def plan(self, src, dst, device):
        i = self.count
        self.count += 1

        def describe():
            return pltpu.make_async_remote_copy(
                src() if callable(src) else src,
                dst() if callable(dst) else dst,
                self.send.at[i],
                self.recv.at[i],
                device_id=device() if callable(device) else device,
                device_id_type=MESH_ID,
            )

        copy = Copy(describe)
        self.open.append(copy)
        return copy

    def start(self, src, dst, device):
        copy = self.plan(src, dst, device)
        copy.start()
        return copy


class Locals:
    def __init__(self, sems):
        self.sems, self.count = sems, 0

    def start(self, src, dst):
        copy = pltpu.make_async_copy(src, dst, self.sems.at[self.count])
        self.count += 1
        copy.start()
        return copy


class Gather:
    def __init__(self, links, place, block):
        self.links, self.place, self.block = links, place, block

    def begin(self, own=None):
        place = self.place
        target = self.block(place.y, place.z)
        own = target if own is None else own
        self.zs = [
            self.links.start(own, target, place.zid(step)) for step in range(1, place.nz)
        ]
        self.ys = [self.links.start(own, target, place.yid())]

    def forward(self):
        place = self.place
        for step in range(1, place.nz):
            self.zs[step - 1].wait_recv()
            held = self.block(place.y, place.zsrc(step))
            self.ys.append(self.links.start(held, held, place.yid()))

    def finish(self):
        for copy in self.ys:
            copy.wait_recv()


def dot_nn(a, b):
    return jnp.dot(a, b, preferred_element_type=WIDE)


def dot_nt(a, b):
    return lax.dot_general(a, b, (((1,), (1,)), ((), ())), preferred_element_type=WIDE)


def dot_tn(a, b):
    return lax.dot_general(a, b, (((0,), (0,)), ((), ())), preferred_element_type=WIDE)


def fold_rows(values):
    rows, cols = values.shape
    return jnp.sum(values.reshape(rows // 8, 8, cols), axis=0)


def gather_kernel(
    ny, nz,
    tok, cot, meta, up_own, mix_own, down_own, out_own, small_own,
    mix_all, out_all, na_out, xh_out, cot_out, feed_out, gxf_out, gdown_out, gup_out,
    meta_all, gains, gains_feed,
    xs, gs, nf, na, act, gp, feed, gxf, up, down, gup, gdown, small,
    send, recv, sems, sems_out,
):
    place = Places(ny, nz)
    y, x, z, c = place.y, place.x, place.z, place.c
    me = x * 2 + c
    rows = xs.shape[1]
    width = xs.shape[2]
    half = up.shape[-1]
    place.greet()
    links = Links(send, recv)
    local = Locals(sems)
    tile = 256
    per = rows // tile

    up_mine = local.start(up_own.at[:, me], up.at[:, y, x, z, c])
    mix_mine = local.start(mix_own.at[me], mix_all.at[y, x, z, c])
    tok_mine = local.start(tok, xs.at[0])
    cot_mine = local.start(cot, gs.at[0])
    small_mine = local.start(small_own, small.at[y, x, z, c])
    meta_mine = local.start(meta, meta_all.at[0])
    down_mine = [
        local.start(down_own.at[:, pl.ds(k * half, half)], down.at[k, y, z]) for k in range(2)
    ]
    out_mine = local.start(out_own, out_all.at[y, z // 2, z % 2, c])

    up_swaps, small_swaps, mix_swaps, meta_swaps = [], [], [], []
    for r in (1, 2, 3):
        mx, mc = place.member(r)
        to = place.member_id(r)
        small_swaps.append(links.start(small_own, small.at[y, x, z, c], to))
        up_swaps.append(links.start(up_own.at[:, mx * 2 + mc], up.at[:, y, x, z, c], to))
    tok_sib = links.start(tok, xs.at[1], place.member_id(1))
    tok_far = links.start(tok, xs.at[2], place.member_id(2))
    out_gather = Gather(links, place, lambda by, bz: out_all.at[by, bz // 2, bz % 2, c])
    out_gather.begin(out_own)

    small_mine.wait()
    for copy in small_swaps:
        copy.wait_recv()
    small_gather = Gather(links, place, lambda by, bz: small.at[by, :, bz])
    small_gather.begin()
    up_mine.wait()
    for copy in up_swaps:
        copy.wait_recv()
    up_gather = [Gather(links, place, lambda by, bz, k=k: up.at[k, by, :, bz]) for k in range(2)]
    up_gather[0].begin()
    up_gather[1].begin()
    for r in (1, 2, 3):
        mx, mc = place.member(r)
        to = place.member_id(r)
        mix_swaps.append(links.start(mix_own.at[mx * 2 + mc], mix_all.at[y, x, z, c], to))
        meta_swaps.append(links.start(meta, meta_all.at[r], to))
    small_gather.forward()
    small_gather.finish()
    count = ny * 2 * nz * 2
    packed = jnp.sum(small[...].reshape(count, 8, 128), axis=1).astype(LOW)
    each = width // count
    lane = lax.broadcasted_iota(jnp.int32, (128, width), 0)
    col = lax.broadcasted_iota(jnp.int32, (128, width), 1)
    owner = lax.broadcasted_iota(jnp.int32, (count, width), 0)
    owned = lax.broadcasted_iota(jnp.int32, (count, width), 1)
    for k in range(4):
        pick = jnp.where(lane == k * each + col % each, 1.0, 0.0).astype(LOW)
        spread = jnp.where(owned // each == owner, dot_nn(packed, pick), 0.0)
        gains[k : k + 1, :] = jnp.sum(spread, axis=0, keepdims=True)
    gains[4:8, :] = jnp.zeros((4, width), WIDE)
    gains_feed[...] = jnp.zeros_like(gains_feed)

    def norm(j):
        def body(i, carry):
            rs = pl.ds(pl.multiple_of(i * 128, 128), 128)
            values = xs[j, rs, :].astype(WIDE)
            center = values - jnp.mean(values, axis=1, keepdims=True)
            spread = jnp.mean(center * center, axis=1, keepdims=True)
            hat = center * lax.rsqrt(spread + epsilon)
            na[j, rs, :] = (hat * gains[0:1, :] + gains[1:2, :]).astype(LOW)
            nf[j, rs, :] = (hat * gains[2:3, :] + gains[3:4, :]).astype(LOW)
            xs[j, rs, :] = hat.astype(LOW)
            return carry

        lax.fori_loop(0, rows // 128, body, 0)

    def hidden(first, last, k):
        weight = up.at[k]

        def body(i, carry):
            j = i // per
            rs = pl.ds(pl.multiple_of((i % per) * tile, tile), tile)
            h = dot_nn(nf[j, rs, :], weight[...].reshape(width, half))
            cdf = 0.5 * (1.0 + lax.erf(h * math.sqrt(0.5)))
            pdf = jnp.exp(-0.5 * h * h) * (1.0 / math.sqrt(2.0 * math.pi))
            act[j, rs, pl.ds(k * half, half)] = (h * cdf).astype(LOW)
            gp[j, rs, pl.ds(k * half, half)] = (cdf + h * pdf).astype(LOW)
            return carry

        lax.fori_loop(first * per, last * per, body, 0)

    def back(first, last):
        def body(i, carry):
            j = i // per
            rs = pl.ds(pl.multiple_of((i % per) * tile, tile), tile)
            ga = jnp.zeros((tile, 2 * half), WIDE)
            for k in range(2):
                d = down[k].reshape(2 * half, half)
                feed[j, rs, pl.ds(k * half, half)] = dot_nn(act[j, rs, :], d).astype(LOW)
                ga += dot_nt(gs[j, rs, pl.ds(k * half, half)], d)
            gh = (ga * gp[j, rs, :].astype(WIDE)).astype(LOW)
            gp[j, rs, :] = gh
            gn = jnp.zeros((tile, width), WIDE)
            for k in range(2):
                gn += dot_nt(gh[:, k * half : (k + 1) * half], up[k].reshape(width, half))
            gains_feed[0:8, :] += fold_rows(gn * xs[j, rs, :].astype(WIDE))
            gains_feed[8:16, :] += fold_rows(gn)
            gxf[j, rs, :] = (gn * gains[2:3, :]).astype(LOW)
            return carry

        lax.fori_loop(first * per, last * per, body, 0)

    def outer(a, b, dst):
        whole = a.shape[0] * a.shape[1]

        def body(i, carry):
            cols = pl.ds(pl.multiple_of(i * 256, 256), 256)
            part = dot_tn(a[:, :, cols].reshape(whole, 256), b[...].reshape(whole, width))
            dst[pl.ds(pl.multiple_of(i * 256, 256), 256), :] = part.astype(LOW)
            return carry

        lax.fori_loop(0, width // 256, body, 0)

    stores = Locals(sems_out)
    written = []

    tok_mine.wait()
    norm(0)
    tok_sib.wait_recv()
    norm(1)
    cot_sib = links.start(cot, gs.at[1], place.member_id(1))
    cot_far = links.start(cot, gs.at[2], place.member_id(2))
    out_gather.forward()
    mix_mine.wait()
    for copy in mix_swaps:
        copy.wait_recv()
    for copy in down_mine:
        copy.wait()
    down_gather = [Gather(links, place, lambda by, bz, k=k: down.at[k, by, bz]) for k in range(2)]
    mix_gather = Gather(links, place, lambda by, bz: mix_all.at[by, :, bz])
    up_gather[0].forward()
    down_gather[0].begin()
    up_gather[1].forward()
    down_gather[1].begin()
    up_gather[0].finish()
    hidden(0, 2, 0)
    tok_far.wait_recv()
    tok_fwd = links.start(xs.at[2], xs.at[3], place.member_id(1))
    up_gather[1].finish()
    hidden(0, 2, 1)
    down_gather[0].forward()
    mix_gather.begin()
    tok_fwd.wait_recv()
    tok_fwd.wait_send()
    norm(2)
    norm(3)
    for j in range(4):
        written.append(stores.start(na.at[j], na_out.at[j]))
        written.append(stores.start(xs.at[j], xh_out.at[j]))
    hidden(2, 4, 0)
    hidden(2, 4, 1)
    down_gather[1].forward()
    cot_far.wait_recv()
    cot_fwd = links.start(gs.at[2], gs.at[3], place.member_id(1))
    cot_mine.wait()
    cot_sib.wait_recv()
    down_gather[0].finish()
    down_gather[1].finish()
    back(0, 2)
    mix_gather.forward()
    cot_fwd.wait_recv()
    for j in range(4):
        written.append(stores.start(gs.at[j], cot_out.at[j]))
    back(2, 4)
    for j in range(4):
        written.append(stores.start(feed.at[j], feed_out.at[j]))
        written.append(stores.start(gxf.at[j], gxf_out.at[j]))
    outer(act, gs, gdown)
    written.append(stores.start(gdown, gdown_out))
    outer(nf, gp, gup)
    written.append(stores.start(gup, gup_out))
    out_mine.wait()
    out_gather.finish()
    out_swap = links.start(
        out_all.at[:, :, 1 - c, c], out_all.at[:, :, 1 - c, c], place.member_id(1)
    )
    mix_gather.finish()
    meta_mine.wait()
    for copy in meta_swaps:
        copy.wait_recv()
    out_swap.wait_recv()
    for copy in written:
        copy.wait()
    links.open.remove(tok_fwd)
    for copy in links.open:
        copy.wait_send()


class Scatter:
    def __init__(self, links, place, theirs, mine, ybuf, zbuf):
        self.links, self.place = links, place
        self.theirs, self.mine, self.ybuf, self.zbuf = theirs, mine, ybuf, zbuf
        self.ys = [self.plan_y(step) for step in range(place.nz)]
        self.zs = [None] + [self.plan_z(step) for step in range(1, place.nz)]

    def at(self, step):
        return (self.place.z + step) % self.place.nz

    def plan_y(self, step):
        return self.links.plan(
            lambda: self.theirs(self.at(step)), lambda: self.ybuf(self.at(step)), self.place.yid
        )

    def plan_z(self, step):
        return self.links.plan(
            lambda: self.ybuf(self.at(step)),
            lambda: self.zbuf(step - 1),
            lambda: self.place.zid(step),
        )

    def begin(self, step):
        self.ys[step].start()

    def turn(self, step):
        self.ys[step].wait_recv()
        if step:
            at = self.at(step)
            land = self.ybuf(at)
            land[...] = (land[...].astype(WIDE) + self.mine(at)[...].astype(WIDE)).astype(LOW)
            self.zs[step].start()

    def total(self):
        at = self.place.z
        total = self.ybuf(at)[...].astype(WIDE) + self.mine(at)[...].astype(WIDE)
        for step in range(1, self.place.nz):
            self.zs[step].wait_recv()
            total += self.zbuf(step - 1)[...].astype(WIDE)
        return total


def scatter_kernel(
    ny, nz,
    na_in, xh_in, cot_in, feed_in, gxf_in, mix_in, out_in, gdown_in, gup_in, meta_in,
    gains, gains_feed, table, scale, spread, tok, cot,
    out_rows, grad_rows, gmix_out, gout_out, gup_out, gdown_out, gains_out,
    na, xh, gs, feed, gxf, mix, outw, down_own, up_own, meta, gmixed, attended, gmix, gout, gout_by,
    ydown, zdown, yup, zup, ymix, zmix, yout, zout, up_send, up_recv, mix_send, mix_recv,
    sib_out, sib_gx, own_out, own_gx, far_out, far_gx, gacc, gsum, gy, g2, gz, g3, gm,
    send, recv, sems, sib_sems, own_sems, far_sems,
):
    place = Places(ny, nz)
    y, x, z, c = place.y, place.x, place.z, place.c
    width = na.shape[-1]
    span = na.shape[2]
    heads = 4
    group = heads * HEAD
    local = Locals(sems)
    up_half = local.start(gup_in.at[y], up_own)
    down_half = local.start(gdown_in.at[y], down_own)
    meta_load = local.start(meta_in, meta)
    mix_load = local.start(mix_in, mix)
    out_load = local.start(out_in.at[:, :, c], outw)
    loads = {}
    for j in (3, 2, 1, 0):
        loads[j] = [
            local.start(src.at[j], dst.at[j])
            for src, dst in ((na_in, na), (feed_in, feed), (gxf_in, gxf), (xh_in, xh), (cot_in, gs))
        ]
    place.greet()
    links = Links(send, recv)

    down_sum = Scatter(
        links, place, lambda at: gdown_in.at[1 - y, at], lambda at: down_own.at[at],
        lambda at: ydown.at[at], lambda k: zdown.at[k],
    )
    up_sum = Scatter(
        links, place, lambda at: gup_in.at[1 - y, :, at], lambda at: up_own.at[:, at],
        lambda at: yup.at[:, at], lambda k: zup.at[k],
    )
    mix_sum = Scatter(
        links, place, lambda at: gmix.at[1 - y, :, at], lambda at: gmix.at[y, :, at],
        lambda at: ymix.at[:, at], lambda k: zmix.at[k],
    )
    out_sum = Scatter(
        links, place, lambda at: gout_by.at[1 - y, at // 2, at % 2], lambda at: gout_by.at[y, at // 2, at % 2],
        lambda at: yout.at[at], lambda k: zout.at[k],
    )
    steps = list(range(1, nz)) + [0]
    for step in steps:
        down_sum.begin(step)
    gacc[...] = jnp.zeros_like(gacc)
    meta_load.wait()
    mix_load.wait()
    out_load.wait()
    for copy in loads[3]:
        copy.wait()

    lane = lax.broadcasted_iota(jnp.int32, (1, group), 1)
    of_head = [lane // HEAD == h for h in range(heads)]
    low_lane = lax.broadcasted_iota(jnp.int32, (1, 128), 1) % HEAD < ROT // 2
    key_at = lax.broadcasted_iota(jnp.int32, (span, span), 1)
    query_at = lax.broadcasted_iota(jnp.int32, (span, span), 0)
    causal = key_at <= query_at
    wide_mix = mix.shape[-1]

    def turn(values, cosine, sine):
        parts = []
        for first in range(0, group, 128):
            part = values[:, first : first + 128]
            other = jnp.where(
                low_lane, pltpu.roll(part, 128 - ROT // 2, 1), pltpu.roll(part, ROT // 2, 1)
            )
            parts.append(part * cosine + other * sine)
        return jnp.concatenate(parts, axis=1)

    def spread_meta(j, s, first, last):
        return lax.dot_general(
            meta[j, s], spread[:, first:last], (((0,), (0,)), ((), ())),
            precision=lax.Precision.HIGHEST, preferred_element_type=WIDE,
        )

    def sib_copy(s, kind):
        buf, dst = ((feed, sib_out), (gxf, sib_gx))[kind]
        return pltpu.make_async_remote_copy(
            buf.at[3, s], dst.at[s], sib_sems.at[0, kind, s], sib_sems.at[1, kind, s],
            device_id=place.member_id(1), device_id_type=MESH_ID,
        )

    def far_copy(s, kind):
        buf, dst = ((feed, far_out), (gxf, far_gx))[kind]
        return pltpu.make_async_remote_copy(
            buf.at[2, s], dst.at[s], far_sems.at[0, kind, s], far_sems.at[1, kind, s],
            device_id=place.member_id(2), device_id_type=MESH_ID,
        )

    def own_copy(s, kind):
        buf, dst = ((feed, own_out), (gxf, own_gx))[kind]
        return pltpu.make_async_remote_copy(
            buf.at[1, s], dst.at[s], own_sems.at[0, kind, s], own_sems.at[1, kind, s],
            device_id=place.member_id(1), device_id_type=MESH_ID,
        )

    def hand_on(j, s, value, kind):
        buf = (feed, gxf)[kind]
        landed = (sib_out, sib_gx)[kind]

        @pl.when(j != 2)
        def _():
            buf[j, s] = value.astype(LOW)

        @pl.when(j == 3)
        def _():
            sib_copy(s, kind).start()

        @pl.when(j == 2)
        def _():
            sib_copy(s, kind).wait_recv()
            buf[j, s] = (value + landed[s].astype(WIDE)).astype(LOW)
            far_copy(s, kind).start()

        @pl.when(j == 1)
        def _():
            own_copy(s, kind).start()

    events = {}

    def pump(i, place_in):
        for at, event in events.items():
            if at[1] == place_in:
                pl.when(i == at[0])(event)

    def slot(i, carry):
        j = 3 - i // 2
        s = i % 2
        pump(i, 0)
        rows = na[j, s]
        mixed = dot_nn(rows, mix[...].reshape(width, wide_mix))
        turns = spread_meta(j, s, 0, 384)
        cosine, sine, owner = turns[:, :128], turns[:, 128:256], turns[:, 256:384]
        owner = jnp.concatenate([owner, owner], axis=1)
        allowed = (owner == meta[j, s, 16:17, :]) & causal
        query = turn(mixed[:, :group], cosine, sine).astype(LOW)
        key = turn(mixed[:, group : 2 * group], cosine, sine).astype(LOW)
        value = mixed[:, 2 * group : 3 * group].astype(LOW)
        raised_query = scale[0:1, :] * jnp.exp(dot_nn(query, table[...]))
        raised_key = scale[0:1, :] * jnp.exp(dot_nn(key, table[...]))
        phi_query = raised_query.astype(LOW)
        phi_key = raised_key.astype(LOW)
        none = jnp.zeros((), LOW)
        scores, totals = [], []
        numer = jnp.zeros((span, group), WIDE)
        total = jnp.zeros((span, group), WIDE)
        for h in range(heads):
            score = dot_nt(jnp.where(of_head[h], phi_query, none), phi_key)
            score = jnp.where(allowed, score, 0.0)
            totals.append(jnp.sum(score, axis=1, keepdims=True))
            scores.append(score.astype(LOW))
            numer += dot_nn(scores[h], jnp.where(of_head[h], value, none))
            total = jnp.where(of_head[h], totals[h], total)
        att = (numer / total).astype(LOW)
        attended[j, s] = att
        attn_rows = dot_nn(att, outw[...].reshape(group, width))
        hand_on(j, s, attn_rows + feed[j, s].astype(WIDE), 0)
        pump(i, 1)
        grad_att = dot_nt(gs[j, s], outw[...].reshape(group, width))
        grad_numer = (grad_att / total).astype(LOW)
        product = grad_att * numer
        grad_query = jnp.zeros((span, group), WIDE)
        grad_key = jnp.zeros((span, group), WIDE)
        grad_value = jnp.zeros((span, group), WIDE)
        for h in range(heads):
            grad_total = -jnp.sum(jnp.where(of_head[h], product, 0.0), axis=1, keepdims=True)
            grad_total = grad_total / (totals[h] * totals[h])
            numer_h = jnp.where(of_head[h], grad_numer, none)
            grad_score = dot_nt(numer_h, value) + grad_total
            grad_score = jnp.where(allowed, grad_score, 0.0).astype(LOW)
            grad_query += dot_nn(grad_score, jnp.where(of_head[h], phi_key, none))
            grad_key += dot_tn(grad_score, jnp.where(of_head[h], phi_query, none))
            grad_value += dot_tn(scores[h], numer_h)
        back_query = turn(
            dot_nt((grad_query * raised_query).astype(LOW), table[...]), cosine, -sine
        )
        back_key = turn(dot_nt((grad_key * raised_key).astype(LOW), table[...]), cosine, -sine)
        grad_mixed = jnp.concatenate(
            [back_query.astype(LOW), back_key.astype(LOW), grad_value.astype(LOW)], axis=1
        )
        gmixed[j, s] = grad_mixed
        grad_normed = dot_nt(grad_mixed, mix[...].reshape(width, wide_mix))
        gacc[0:8, :] += fold_rows(grad_normed * xh[j, s].astype(WIDE))
        gacc[8:16, :] += fold_rows(grad_normed)
        hand_on(j, s, grad_normed * gains[0:1, :] + gxf[j, s].astype(WIDE), 1)
        return carry

    def waits(j):
        def event():
            for copy in loads[j]:
                copy.wait()

        return event

    def both(*fns):
        def event():
            for fn in fns:
                fn()

        return event

    def begin_up():
        up_half.wait()
        down_half.wait()
        for step in steps:
            up_sum.begin(step)

    events[(0, 1)] = begin_up
    events[(1, 1)] = lambda: down_sum.turn(steps[0])
    events[(2, 0)] = waits(2)
    events[(2, 1)] = lambda: down_sum.turn(steps[1])
    events[(4, 0)] = both(waits(1), lambda: down_sum.turn(steps[2]))
    events[(5, 1)] = lambda: down_sum.turn(steps[3])
    events[(6, 0)] = both(waits(0), lambda: up_sum.turn(steps[0]))
    events[(7, 1)] = lambda: up_sum.turn(steps[1])
    lax.fori_loop(0, 8, slot, 0)

    rest = 4 * 2 * span
    part = dot_tn(attended[...].reshape(rest, group), gs[...].reshape(rest, width))
    gout[...] = part.astype(LOW).reshape(gout.shape)
    out_swap = links.start(gout.at[:, :, 1 - c], gout_by.at[:, :, c], place.member_id(1))
    gout_by[:, :, c] = gout[:, :, c]

    gsum[...] = jnp.zeros_like(gsum)
    gsum[0:1, :] = jnp.sum(gacc[0:8, :], axis=0, keepdims=True)
    gsum[1:2, :] = jnp.sum(gacc[8:16, :], axis=0, keepdims=True)
    gsum[2:3, :] = jnp.sum(gains_feed[0:8, :], axis=0, keepdims=True)
    gsum[3:4, :] = jnp.sum(gains_feed[8:16, :], axis=0, keepdims=True)
    gain_y = links.start(gsum, gy, place.yid())

    def outer_mix(first):
        def body(i, carry):
            at_y = (y + 1 + i // 2) % ny
            cols = pl.ds(pl.multiple_of((at_y * 2 + i % 2) * 256, 256), 256)
            part = dot_tn(na[:, :, :, cols].reshape(rest, 256), gmixed[...].reshape(rest, wide_mix))
            gmix[at_y, i % 2] = part.astype(LOW).reshape(gmix.shape[2:])
            return carry

        lax.fori_loop(first, first + 2, body, 0)

    outer_mix(0)
    out_swap.wait_recv()
    for step in steps:
        out_sum.begin(step)
    for step in steps:
        mix_sum.begin(step)
    up_sum.turn(steps[2])
    gain_y.wait_recv()
    g2[...] = gsum[...] + gy[...]
    gain_zs = [links.start(g2, gz.at[step - 1], place.zid(step)) for step in range(1, nz)]
    outer_mix(2)
    up_sum.turn(steps[3])
    gdown_out[...] = down_sum.total()

    def finish(s, carry):
        for kind in (0, 1):
            own_copy(s, kind).wait_recv()
            far_copy(s, kind).wait_recv()
        keep = spread_meta(0, s, 384, 512)[:, :1]
        values = tok[s].astype(WIDE)
        added = feed[0, s].astype(WIDE) + own_out[s].astype(WIDE) + far_out[s].astype(WIDE)
        out_rows[s] = (values + keep * added).astype(LOW)
        grad = gxf[0, s].astype(WIDE) + own_gx[s].astype(WIDE) + far_gx[s].astype(WIDE)
        center = values - jnp.mean(values, axis=1, keepdims=True)
        rate = lax.rsqrt(jnp.mean(center * center, axis=1, keepdims=True) + epsilon)
        hat = center * rate
        inner = jnp.mean(grad * hat, axis=1, keepdims=True)
        grad = grad - jnp.mean(grad, axis=1, keepdims=True) - hat * inner
        grad_rows[s] = cot[s].astype(WIDE) + rate * grad
        return carry

    lax.fori_loop(0, 2, finish, 0)
    for step in steps:
        out_sum.turn(step)
    for step in range(1, nz):
        gain_zs[step - 1].wait_recv()
    g3[...] = g2[...] + sum(gz[step - 1] for step in range(1, nz))
    gain_ms = [links.start(g3, gm.at[r - 1], place.member_id(r)) for r in (1, 2, 3)]
    for step in steps:
        mix_sum.turn(step)

    def share(total, hold, land):
        hold[...] = total.astype(LOW).reshape(hold.shape)
        copies = []
        for r in (1, 2, 3):
            mx, mc = place.member(r)
            copies.append(links.start(hold.at[mx, mc], land.at[r - 1], place.member_id(r)))
        return copies

    def collect(copies, hold, land, dst):
        dst[x * 2 + c] = hold[x, c].astype(WIDE)
        for r in (1, 2, 3):
            mx, mc = place.member(r)
            copies[r - 1].wait_recv()
            dst[mx * 2 + mc] = land[r - 1].astype(WIDE)

    up_shares = share(up_sum.total(), up_send, up_recv)
    gout_out[...] = out_sum.total()
    for copy in gain_ms:
        copy.wait_recv()
    gains_out[...] = g3[...] + gm[0] + gm[1] + gm[2]
    mix_shares = share(mix_sum.total(), mix_send, mix_recv)
    collect(up_shares, up_send, up_recv, gup_out)
    collect(mix_shares, mix_send, mix_recv, gmix_out)
    for copy in links.open:
        copy.wait_send()
    for kind in (0, 1):
        for s in (0, 1):
            sib_copy(s, kind).wait_send()
            far_copy(s, kind).wait_send()
            own_copy(s, kind).wait_send()


VMEM = pl.BlockSpec(memory_space=pltpu.VMEM)
ANY = pl.BlockSpec(memory_space=pl.ANY)
SHAPE = jax.ShapeDtypeStruct
LIMIT = 60 * 2**20


def turn_table(position):
    half = ROT // 2
    inverse = 10000.0 ** (-2.0 * jnp.arange(half, dtype=WIDE) / ROT)
    angle = position[..., None] * inverse
    return jnp.cos(angle), jnp.sin(angle)


def spread_rows():
    row = jnp.arange(24)[:, None]
    lane = jnp.arange(512)[None, :]
    part, dim = lane // 128, lane % HEAD
    half = ROT // 2
    cosine = (part == 0) & (dim < ROT) & (row == dim % half)
    cosine = cosine | ((part == 0) & (dim >= ROT) & (row == 17))
    sine = (part == 1) & (dim < ROT) & (row == half + dim % half)
    rest = ((part == 2) & (row == 16)) | ((part == 3) & (row == 18))
    sign = jnp.where((part == 1) & (dim < half), -1.0, 1.0)
    return jnp.where(cosine | sine | rest, sign, 0.0).astype(WIDE)


def per_device_group(
    ny,
    nz,
    tokens,
    lengths,
    mix_weight,
    out_weight,
    up_weight,
    down_weight,
    attn_gain,
    attn_bias,
    feed_gain,
    feed_bias,
    feature_freq,
    feature_scale,
    cotangent,
):
    micro, span, width = tokens.shape
    rows = micro * span
    shard = mix_weight.shape[0]
    feed_shard = down_weight.shape[0]
    count = ny * 2 * nz * 2
    heads = width // HEAD // 4
    group = heads * HEAD
    hidden = feed_shard * ny * nz
    half = hidden // 2

    segment, position, valid = slot_layout(lengths[:, 0], span)
    cosine, sine = turn_table(position)
    facts = jnp.concatenate(
        [
            cosine,
            sine,
            segment.astype(WIDE)[..., None],
            jnp.ones((micro, span, 1), WIDE),
            valid[..., None],
            jnp.zeros((micro, span, 5), WIDE),
        ],
        axis=-1,
    )
    meta = jnp.swapaxes(facts, 1, 2)
    table = feature_table(feature_freq)
    table_wide = jnp.kron(jnp.eye(heads, dtype=LOW), table)
    scale = jnp.broadcast_to(jnp.tile(feature_scale, heads)[None], (8, group))
    branch = jnp.where(valid[..., None] > 0.0, cotangent, jnp.zeros_like(cotangent))
    up_own = up_weight.reshape(shard, ny, 2, nz, 2, feed_shard).transpose(2, 4, 0, 1, 3, 5)
    up_own = up_own.reshape(4, shard, 2, half).transpose(2, 0, 1, 3)
    mix_own = mix_weight.reshape(shard, 3, ny, 2, nz // 2, 2, HEAD).transpose(3, 5, 0, 1, 2, 4, 6)
    mix_own = mix_own.reshape(4, shard, 3 * group)
    small = jnp.concatenate([attn_gain, attn_bias, feed_gain, feed_bias]).astype(WIDE)
    small = jnp.pad(small[None], ((0, 7), (0, 0)))

    dma = pltpu.SemaphoreType.DMA
    names = [
        ("mix_all", (ny, 2, nz, 2, shard, 3 * group), LOW),
        ("out_all", (ny, nz // 2, 2, 2, shard, width), LOW),
        ("na", (4, rows, width), LOW),
        ("xh", (4, rows, width), LOW),
        ("cot", (4, rows, width), LOW),
        ("feed", (4, rows, width), LOW),
        ("gxf", (4, rows, width), LOW),
        ("gdown", (hidden, width), LOW),
        ("gup", (width, hidden), LOW),
        ("meta", (4, micro, 24, span), WIDE),
        ("gains", (8, width), WIDE),
        ("gains_feed", (16, width), WIDE),
    ]
    full = pltpu.VMEM((4, rows, width), LOW)
    first = pl.pallas_call(
        partial(gather_kernel, ny, nz),
        out_shape=[SHAPE(shape, kind) for _, shape, kind in names],
        in_specs=[ANY] * 8,
        out_specs=[ANY] * 10 + [VMEM] * 2,
        scratch_shapes=[full] * 8
        + [
            pltpu.VMEM((2, ny, 2, nz, 2, shard, half), LOW),
            pltpu.VMEM((2, ny, nz, feed_shard, half), LOW),
            pltpu.VMEM((width, hidden), LOW),
            pltpu.VMEM((hidden, width), LOW),
            pltpu.VMEM((ny, 2, nz, 2, 8, 128), WIDE),
            dma((80,)),
            dma((80,)),
            dma((12,)),
            dma((24,)),
        ],
        name="gather_feed",
        cost_estimate=pl.CostEstimate(flops=25 * 10**9, bytes_accessed=40 * 10**6, transcendentals=0),
        compiler_params=pltpu.CompilerParams(
            collective_id=0, has_side_effects=True, vmem_limit_bytes=LIMIT
        ),
    )(
        tokens.reshape(rows, width), branch.reshape(rows, width), meta, up_own, mix_own,
        down_weight, out_weight, small,
    )
    mix_all, out_all, na, xh, cot, feed, gxf, gdown, gup, meta_all, gains, gains_feed = first

    by_slot = (4, micro, span, width)
    slots = pltpu.VMEM(by_slot, LOW)
    landing = pltpu.VMEM((micro, span, width), LOW)
    pair = 2 * shard
    results = [
        SHAPE((micro, span, width), LOW),
        SHAPE((micro, span, width), WIDE),
        SHAPE((4, shard, 3 * group), WIDE),
        SHAPE((shard, width), WIDE),
        SHAPE((4, shard, hidden), WIDE),
        SHAPE((feed_shard, width), WIDE),
        SHAPE((8, width), WIDE),
    ]
    second = pl.pallas_call(
        partial(scatter_kernel, ny, nz),
        out_shape=results,
        in_specs=[ANY] * 10 + [VMEM] * 7,
        out_specs=[VMEM] * 7,
        scratch_shapes=[slots] * 5
        + [
            pltpu.VMEM((ny, 2, nz, 2, shard, 3 * group), LOW),
            pltpu.VMEM((ny, nz // 2, 2, shard, width), LOW),
            pltpu.VMEM((nz, feed_shard, width), LOW),
            pltpu.VMEM((2, nz, pair, hidden), LOW),
            pltpu.VMEM((4, micro, 24, span), WIDE),
            pltpu.VMEM((4, micro, span, 3 * group), LOW),
            pltpu.VMEM((4, micro, span, group), LOW),
            pltpu.VMEM((ny, 2, nz, pair, 3 * group), LOW),
            pltpu.VMEM((ny, nz // 2, 2, shard, width), LOW),
            pltpu.VMEM((ny, nz // 2, 2, shard, width), LOW),
            pltpu.VMEM((nz, feed_shard, width), LOW),
            pltpu.VMEM((nz - 1, feed_shard, width), LOW),
            pltpu.VMEM((2, nz, pair, hidden), LOW),
            pltpu.VMEM((nz - 1, 2, pair, hidden), LOW),
            pltpu.VMEM((2, nz, pair, 3 * group), LOW),
            pltpu.VMEM((nz - 1, 2, pair, 3 * group), LOW),
            pltpu.VMEM((nz, shard, width), LOW),
            pltpu.VMEM((nz - 1, shard, width), LOW),
            pltpu.VMEM((2, 2, shard, hidden), LOW),
            pltpu.VMEM((3, shard, hidden), LOW),
            pltpu.VMEM((2, 2, shard, 3 * group), LOW),
            pltpu.VMEM((3, shard, 3 * group), LOW),
        ]
        + [landing] * 6
        + [
            pltpu.VMEM((16, width), WIDE),
            pltpu.VMEM((8, width), WIDE),
            pltpu.VMEM((8, width), WIDE),
            pltpu.VMEM((8, width), WIDE),
            pltpu.VMEM((nz - 1, 8, width), WIDE),
            pltpu.VMEM((8, width), WIDE),
            pltpu.VMEM((3, 8, width), WIDE),
            dma((80,)),
            dma((80,)),
            dma((28,)),
            dma((2, 2, 2)),
            dma((2, 2, 2)),
            dma((2, 2, 2)),
        ],
        name="attend_scatter",
        cost_estimate=pl.CostEstimate(flops=25 * 10**9, bytes_accessed=40 * 10**6, transcendentals=0),
        compiler_params=pltpu.CompilerParams(
            collective_id=1, has_side_effects=True, vmem_limit_bytes=LIMIT
        ),
    )(
        na.reshape(by_slot), xh.reshape(by_slot), cot.reshape(by_slot), feed.reshape(by_slot),
        gxf.reshape(by_slot), mix_all, out_all,
        gdown.reshape(ny, nz, feed_shard, width), gup.reshape(ny, 2, nz, pair, hidden), meta_all,
        gains, gains_feed, table_wide, scale, spread_rows(), tokens, cotangent,
    )
    out_rows, grad_rows, gmix, gout, gup, gdown, gains_out = second
    gmix = gmix.reshape(2, 2, shard, 3, ny, nz // 2, HEAD).transpose(2, 3, 4, 0, 5, 1, 6)
    gup = gup.reshape(2, 2, shard, ny, nz, feed_shard).transpose(2, 3, 0, 4, 1, 5)
    index = lax.axis_index("dp") * (2 * nz) + lax.axis_index("fsdp")
    gains_out = lax.dynamic_slice_in_dim(gains_out, index * shard, shard, 1)
    return (
        out_rows,
        grad_rows,
        gmix.reshape(mix_weight.shape),
        gout,
        gup.reshape(up_weight.shape),
        gdown,
        gains_out[0],
        gains_out[1],
        gains_out[2],
        gains_out[3],
    )


def solution(mesh):
    ny, nz = mesh.shape["dp"] // 2, mesh.shape["fsdp"] // 2
    grouped = ny == 2 and nz % 2 == 0 and D // mesh.size % 32 == 0
    body = partial(per_device_group, ny, nz) if grouped else per_device_plain
    rows = P(("dp", "fsdp"), None)
    vector = P(("dp", "fsdp"))
    slots = P(None, ("dp", "fsdp"), None)
    return jax.shard_map(
        body,
        mesh=mesh,
        in_specs=(slots, slots, *[rows] * 4, *[vector] * 4, P(), P(), slots),
        out_specs=(slots, slots, *[rows] * 4, *[vector] * 4),
        check_vma=False,
    )
```

```python
from functools import partial
import math

import jax
import jax.numpy as jnp
import numpy as np
from jax import lax
from jax.experimental import pallas as pl
from jax.experimental.pallas import tpu as pltpu
from jax.sharding import PartitionSpec as P

D = 1024
HEAD = 64
ROT = 16


epsilon = 1e-05
exact_precision = lax.Precision.HIGHEST


def dct_matrix(width):
    order = jnp.arange(width, dtype=jnp.float32)[:, None]
    sample = jnp.arange(width, dtype=jnp.float32)[None, :]
    factor = jnp.where(order == 0, jnp.sqrt(1.0 / width), jnp.sqrt(2.0 / width))
    return factor * jnp.cos(math.pi * (2.0 * sample + 1.0) * order / (2.0 * width))


def feature_table(feature_freq):
    table = jnp.dot(dct_matrix(HEAD).T, feature_freq.T, precision=exact_precision) / math.sqrt(HEAD)
    return table.astype(jnp.bfloat16)


def slot_layout(span_table, slot_len):
    seg_ends = jnp.cumsum(span_table, axis=-1)
    seg_starts = seg_ends - span_table
    places = jnp.arange(slot_len, dtype=jnp.int32)
    segment = jnp.sum((places[:, None] >= seg_ends[..., None, :]).astype(jnp.int32), axis=-1)
    numbers = jnp.arange(span_table.shape[-1], dtype=jnp.int32)
    matched = segment[..., None] == numbers
    begin_at = jnp.sum(jnp.where(matched, seg_starts[..., None, :], 0), axis=-1)
    begin_at = begin_at + jnp.where(segment == span_table.shape[-1], seg_ends[..., -1:], 0)
    position = (places - begin_at).astype(jnp.float32)
    valid = (segment < span_table.shape[-1]).astype(jnp.float32)
    return (segment, position, valid)


def rotate(raw_heads, position):
    half_rot = ROT // 2
    inverse = 10000.0 ** (-2.0 * jnp.arange(half_rot, dtype=jnp.float32) / ROT)
    angle = position[..., None] * inverse
    cosine_wave = jnp.cos(angle)[..., None, :]
    sine = jnp.sin(angle)[..., None, :]
    first = raw_heads[..., :half_rot]
    second = raw_heads[..., half_rot:ROT]
    return jnp.concatenate(
        [
            first * cosine_wave - second * sine,
            second * cosine_wave + first * sine,
            raw_heads[..., ROT:],
        ],
        axis=-1,
    )


def feature_map(raw_heads, position, table, feature_scale):
    rotated_rows = rotate(raw_heads, position).astype(jnp.bfloat16)
    pre = jnp.einsum("shd,df->shf", rotated_rows, table, preferred_element_type=jnp.float32)
    return feature_scale * jnp.exp(pre)


def feature_back(raw_heads, grad_phi, position, table, feature_scale):
    phi = feature_map(raw_heads, position, table, feature_scale)
    grad_pre = (grad_phi * phi).astype(jnp.bfloat16)
    grad_turned = jnp.einsum("shf,df->shd", grad_pre, table, preferred_element_type=jnp.float32)
    _, turn_pull = jax.vjp(lambda values: rotate(values, position), raw_heads)
    return turn_pull(grad_turned)[0]


def norm_apply(inputs, gain, shift):
    center = inputs - jnp.mean(inputs, axis=-1, keepdims=True)
    spread = jnp.mean(center * center, axis=-1, keepdims=True)
    return center * lax.rsqrt(spread + epsilon) * gain + shift


def head_major(values):
    return jnp.swapaxes(values, 0, 1)


def attend_head(allowed, pieces):
    mapped_query, mapped_key, value_rows = pieces
    score_matrix = jnp.einsum(
        "qf,kf->qk", mapped_query, mapped_key, preferred_element_type=jnp.float32
    )
    score_matrix = jnp.where(allowed, score_matrix, 0.0)
    totals = jnp.sum(score_matrix, axis=1)
    numerator = jnp.dot(
        score_matrix.astype(jnp.bfloat16), value_rows, preferred_element_type=jnp.float32
    )
    return numerator / totals[:, None]


def attend_back(allowed, pieces):
    mapped_query, mapped_key, value_rows, grad_heads = pieces
    score_matrix = jnp.einsum(
        "qf,kf->qk", mapped_query, mapped_key, preferred_element_type=jnp.float32
    )
    score_matrix = jnp.where(allowed, score_matrix, 0.0)
    totals = jnp.sum(score_matrix, axis=1)
    scores_low = score_matrix.astype(jnp.bfloat16)
    numerator = jnp.dot(scores_low, value_rows, preferred_element_type=jnp.float32)
    grad_numer = (grad_heads / totals[:, None]).astype(jnp.bfloat16)
    grad_totals = -jnp.sum(grad_heads * numerator, axis=1) / (totals * totals)
    grad_scores = jnp.einsum(
        "qd,kd->qk", grad_numer, value_rows, preferred_element_type=jnp.float32
    )
    grad_scores = jnp.where(allowed, grad_scores + grad_totals[:, None], 0.0).astype(jnp.bfloat16)
    grad_query = jnp.dot(grad_scores, mapped_key, preferred_element_type=jnp.float32)
    grad_key = jnp.einsum(
        "qk,qf->kf", grad_scores, mapped_query, preferred_element_type=jnp.float32
    )
    grad_value = jnp.einsum("qk,qd->kd", scores_low, grad_numer, preferred_element_type=jnp.float32)
    return (grad_query, grad_key, grad_value)


def fetch_attention(shards):
    return (
        lax.all_gather(shards[0], ("dp", "fsdp"), axis=0, tiled=True),
        lax.all_gather(shards[1], ("dp", "fsdp"), axis=0, tiled=True),
        lax.all_gather(shards[2], ("dp", "fsdp"), axis=0, tiled=True),
        lax.all_gather(shards[3], ("dp", "fsdp"), axis=0, tiled=True),
    )


def fetch_feed(shards):
    return (
        lax.all_gather(shards[0], ("dp", "fsdp"), axis=0, tiled=True),
        lax.all_gather(shards[1], ("dp", "fsdp"), axis=0, tiled=True),
        lax.all_gather(shards[2], ("dp", "fsdp"), axis=0, tiled=True),
        lax.all_gather(shards[3], ("dp", "fsdp"), axis=0, tiled=True),
    )


def reduce_attention(grads):
    return (
        lax.psum_scatter(grads[0], ("dp", "fsdp"), scatter_dimension=0, tiled=True),
        lax.psum_scatter(grads[1], ("dp", "fsdp"), scatter_dimension=0, tiled=True),
        lax.psum_scatter(grads[2], ("dp", "fsdp"), scatter_dimension=0, tiled=True),
        lax.psum_scatter(grads[3], ("dp", "fsdp"), scatter_dimension=0, tiled=True),
    )


def reduce_feed(grads):
    return (
        lax.psum_scatter(grads[0], ("dp", "fsdp"), scatter_dimension=0, tiled=True),
        lax.psum_scatter(grads[1], ("dp", "fsdp"), scatter_dimension=0, tiled=True),
        lax.psum_scatter(grads[2], ("dp", "fsdp"), scatter_dimension=0, tiled=True),
        lax.psum_scatter(grads[3], ("dp", "fsdp"), scatter_dimension=0, tiled=True),
    )


def add_tuples(running, update):
    if running is None:
        return tuple(update)
    return tuple(jax.tree.map(jnp.add, tuple(running), tuple(update)))


def per_device_plain(
    tokens,
    lengths,
    mix_weight,
    out_weight,
    up_weight,
    down_weight,
    attn_gain,
    attn_bias,
    feed_gain,
    feed_bias,
    feature_freq,
    feature_scale,
    cotangent,
):
    table = feature_table(feature_freq)
    slot_len = tokens.shape[1]
    head_count = D // HEAD
    attn_shards = (mix_weight, out_weight, attn_gain, attn_bias)
    feed_shards = (up_weight, down_weight, feed_gain, feed_bias)
    places = jnp.arange(slot_len, dtype=jnp.int32)
    output_rows = []
    grad_inputs = []
    attn_total = None
    feed_total = None
    for micro_index in range(tokens.shape[0]):
        attn_full = fetch_attention(attn_shards)
        feed_full = fetch_feed(feed_shards)
        mix_full, out_full, gain_one, bias_one = attn_full
        up_full, down_full, gain_two, bias_two = feed_full
        gain_attn = gain_one.astype(jnp.float32)
        shift_attn = bias_one.astype(jnp.float32)
        gain_feed = gain_two.astype(jnp.float32)
        shift_feed = bias_two.astype(jnp.float32)
        inputs = tokens[micro_index].astype(jnp.float32)
        segment, position, valid = slot_layout(lengths[micro_index, 0], slot_len)
        allowed = (segment[:, None] == segment[None, :]) & (places[None, :] <= places[:, None])
        normed_attn = norm_apply(inputs, gain_attn, shift_attn).astype(jnp.bfloat16)
        normed_feed = norm_apply(inputs, gain_feed, shift_feed).astype(jnp.bfloat16)
        mixed = jnp.dot(normed_attn, mix_full, preferred_element_type=jnp.float32)
        mixed = mixed.reshape(slot_len, 3, head_count, HEAD)
        query_raw = mixed[:, 0]
        key_raw = mixed[:, 1]
        value_rows = mixed[:, 2].astype(jnp.bfloat16)
        mapped_query = feature_map(query_raw, position, table, feature_scale).astype(jnp.bfloat16)
        mapped_key = feature_map(key_raw, position, table, feature_scale).astype(jnp.bfloat16)
        attended = lax.map(
            partial(attend_head, allowed),
            (head_major(mapped_query), head_major(mapped_key), head_major(value_rows)),
        )
        attended = head_major(attended).reshape(slot_len, D).astype(jnp.bfloat16)
        attn_rows = jnp.dot(attended, out_full, preferred_element_type=jnp.float32)
        hidden = jnp.dot(normed_feed, up_full, preferred_element_type=jnp.float32)
        active = jax.nn.gelu(hidden, approximate=False).astype(jnp.bfloat16)
        feed_rows = jnp.dot(active, down_full, preferred_element_type=jnp.float32)
        result = inputs + valid[:, None] * (attn_rows + feed_rows)
        output_rows.append(result.astype(jnp.bfloat16))
        attn_full = fetch_attention(attn_shards)
        feed_full = fetch_feed(feed_shards)
        mix_full, out_full, gain_one, bias_one = attn_full
        up_full, down_full, gain_two, bias_two = feed_full
        grad_rows = cotangent[micro_index]
        grad_branch = jnp.where(valid[:, None] > 0.0, grad_rows, jnp.zeros_like(grad_rows))
        grad_down = jnp.einsum("sf,sd->fd", active, grad_branch, preferred_element_type=jnp.float32)
        grad_out = jnp.einsum(
            "sd,se->de", attended, grad_branch, preferred_element_type=jnp.float32
        )
        grad_active = jnp.einsum(
            "sd,fd->sf", grad_branch, down_full, preferred_element_type=jnp.float32
        )
        _, gelu_pull = jax.vjp(partial(jax.nn.gelu, approximate=False), hidden)
        grad_hidden = gelu_pull(grad_active)[0].astype(jnp.bfloat16)
        grad_up = jnp.einsum(
            "sd,sf->df", normed_feed, grad_hidden, preferred_element_type=jnp.float32
        )
        grad_normed_feed = jnp.einsum(
            "sf,df->sd", grad_hidden, up_full, preferred_element_type=jnp.float32
        )
        grad_attended = jnp.einsum(
            "sd,ed->se", grad_branch, out_full, preferred_element_type=jnp.float32
        )
        grad_attended = grad_attended.reshape(slot_len, head_count, HEAD)
        grad_phi_q, grad_phi_k, grad_value = lax.map(
            partial(attend_back, allowed),
            (
                head_major(mapped_query),
                head_major(mapped_key),
                head_major(value_rows),
                head_major(grad_attended),
            ),
        )
        grad_query = feature_back(query_raw, head_major(grad_phi_q), position, table, feature_scale)
        grad_key = feature_back(key_raw, head_major(grad_phi_k), position, table, feature_scale)
        grad_mixed = jnp.stack([grad_query, grad_key, head_major(grad_value)], axis=1)
        grad_mixed = grad_mixed.reshape(slot_len, 3 * D).astype(jnp.bfloat16)
        grad_mix = jnp.einsum(
            "sd,se->de", normed_attn, grad_mixed, preferred_element_type=jnp.float32
        )
        grad_normed_attn = jnp.einsum(
            "se,de->sd", grad_mixed, mix_full, preferred_element_type=jnp.float32
        )
        _, attn_norm_pull = jax.vjp(norm_apply, inputs, gain_attn, shift_attn)
        grad_in_one, grad_gain_one, grad_bias_one = attn_norm_pull(grad_normed_attn)
        _, feed_norm_pull = jax.vjp(norm_apply, inputs, gain_feed, shift_feed)
        grad_in_two, grad_gain_two, grad_bias_two = feed_norm_pull(grad_normed_feed)
        grad_inputs.append(grad_rows.astype(jnp.float32) + grad_in_one + grad_in_two)
        attn_grads = (grad_mix, grad_out, grad_gain_one, grad_bias_one)
        feed_grads = (grad_up, grad_down, grad_gain_two, grad_bias_two)
        attn_grads = reduce_attention(attn_grads)
        feed_grads = reduce_feed(feed_grads)
        attn_total = add_tuples(attn_total, attn_grads)
        feed_total = add_tuples(feed_total, feed_grads)
    return (
        jnp.stack(output_rows),
        jnp.stack(grad_inputs),
        attn_total[0],
        attn_total[1],
        feed_total[0],
        feed_total[1],
        attn_total[2],
        attn_total[3],
        feed_total[2],
        feed_total[3],
    )


MESH_ID = pl.DeviceIdType.MESH
LOW = jnp.bfloat16
WIDE = jnp.float32


def here(nz):
    dp = lax.axis_index("dp")
    fs = lax.axis_index("fsdp")
    return dp // 2, dp % 2, fs // 2, fs % 2


class Places:
    def __init__(self, ny, nz):
        self.ny, self.nz = ny, nz
        self.y, self.x, self.z, self.c = here(nz)

    def at(self, y, x, z, c):
        return (y * 2 + x, z * 2 + c)

    def member(self, r):
        x = 1 - self.x if r & 2 else self.x
        c = 1 - self.c if r & 1 else self.c
        return x, c

    def member_id(self, r):
        x, c = self.member(r)
        return self.at(self.y, x, self.z, c)

    def yid(self):
        return self.at(1 - self.y, self.x, self.z, self.c)

    def zid(self, step):
        return self.at(self.y, self.x, (self.z + step) % self.nz, self.c)

    def zsrc(self, step):
        return (self.z + self.nz - step) % self.nz

    def signal(self):
        barrier = pltpu.get_barrier_semaphore()
        ids = [self.member_id(r) for r in (1, 2, 3)] + [self.yid()]
        ids += [self.zid(step) for step in range(1, self.nz)]
        for one in ids:
            pl.semaphore_signal(barrier, inc=1, device_id=one, device_id_type=MESH_ID)

    def meet(self):
        pl.semaphore_wait(pltpu.get_barrier_semaphore(), self.nz + 3)


class Copy:
    def __init__(self, describe):
        self.describe, self.sent = describe, False

    def start(self):
        self.describe().start()

    def wait_recv(self):
        self.describe().wait_recv()

    def wait_send(self):
        if not self.sent:
            self.describe().wait_send()
            self.sent = True


class Links:
    def __init__(self, send, recv):
        self.send, self.recv, self.count, self.open = send, recv, 0, []

    def plan(self, src, dst, device):
        i = self.count
        self.count += 1

        def describe():
            return pltpu.make_async_remote_copy(
                src() if callable(src) else src,
                dst() if callable(dst) else dst,
                self.send.at[i],
                self.recv.at[i],
                device_id=device() if callable(device) else device,
                device_id_type=MESH_ID,
            )

        return Copy(describe)

    def start(self, src, dst, device):
        copy = self.plan(src, dst, device)
        copy.start()
        self.open.append(copy)
        return copy

    def drain(self):
        for copy in self.open:
            copy.wait_send()


class Locals:
    def __init__(self, sems):
        self.sems, self.count = sems, 0

    def start(self, src, dst):
        copy = pltpu.make_async_copy(src, dst, self.sems.at[self.count])
        self.count += 1
        copy.start()
        return copy


class Line:
    def __init__(self, place):
        z = place.z
        self.place = place
        self.way = 1 - 2 * (z // 2)
        self.inner = (z // 2) * (3 - z) + (1 - z // 2) * z

    def off(self, end, inner):
        return self.place.z + self.way * ((1 - self.inner) * end + self.inner * inner)

    def near(self):
        return self.off(1, -1)

    def second(self):
        return self.off(2, 1)

    def third(self):
        return self.off(3, 2)

    def id(self, z):
        return self.place.at(self.place.y, self.place.x, z, self.place.c)

    def at_end(self, event):
        pl.when(self.inner == 0)(event)

    def at_inner(self, event):
        pl.when(self.inner == 1)(event)


class Spread:
    def __init__(self, links, line, block, own=None):
        z = line.place.z
        mine = own if own is not None else lambda: block(z)

        def here():
            return block(z)

        def second():
            return block(line.second())

        def third():
            return block(line.third())

        self.line = line
        self.beside = links.plan(mine, here, lambda: line.id(line.near()))
        self.across = links.plan(mine, here, lambda: line.id(line.second()))
        self.far = links.plan(mine, here, lambda: line.id(line.second()))
        self.hand_second = links.plan(second, second, lambda: line.id(line.near()))
        self.hand_third = links.plan(third, third, lambda: line.id(line.near()))

    def begin(self):
        self.beside.start()
        self.line.at_inner(self.across.start)
        self.line.at_end(self.far.start)

    def arrive_near(self, then=None):
        self.beside.wait_recv()
        if then:
            then[0].start()

    def arrive_inner(self, then=None):
        @self.line.at_inner
        def _():
            self.across.wait_recv()
            self.hand_second.start()
            if then:
                then[1].start()
            self.far.wait_recv()
            self.hand_third.start()
            if then:
                then[2].start()

    def arrive_end(self, then=None):
        @self.line.at_end
        def _():
            self.hand_second.wait_recv()
            if then:
                then[1].start()
            self.hand_third.wait_recv()
            if then:
                then[2].start()

    def drain(self):
        self.beside.wait_send()

        @self.line.at_inner
        def _():
            for copy in (self.across, self.hand_second, self.hand_third):
                copy.wait_send()

        self.line.at_end(self.far.wait_send)


class Gather:
    def __init__(self, links, place, line, block, own=None):
        def plane(z):
            return block(place.y, z)

        self.spread = Spread(links, line, plane, own)
        mine = own if own is not None else lambda: plane(place.z)
        self.cross = links.plan(mine, lambda: plane(place.z), place.yid)
        self.cross_on = [
            links.plan(lambda at=at: plane(at()), lambda at=at: plane(at()), place.yid)
            for at in (line.near, line.second, line.third)
        ]

    def begin(self):
        self.spread.begin()
        self.cross.start()

    def forward(self):
        self.spread.arrive_near(self.cross_on)
        self.spread.arrive_inner(self.cross_on)

    def late(self):
        self.spread.arrive_end(self.cross_on)

    def finish(self):
        for copy in [self.cross] + self.cross_on:
            copy.wait_recv()

    def drain(self):
        self.spread.drain()
        for copy in [self.cross] + self.cross_on:
            copy.wait_send()


class GatherCross:
    def __init__(self, links, place, line, block, own=None):
        def plane(z):
            return block(place.y, z)

        def other(z):
            return block(1 - place.y, z)

        mine = own if own is not None else lambda: plane(place.z)
        self.cross = links.plan(mine, lambda: plane(place.z), place.yid)
        self.spread = Spread(links, line, plane, own)
        self.spread_other = Spread(links, line, other)

    def begin(self):
        self.cross.start()
        self.spread.begin()

    def forward(self):
        self.cross.wait_recv()
        self.spread_other.begin()
        self.spread.arrive_near()
        self.spread.arrive_inner()

    def late(self):
        self.spread.arrive_end()
        self.spread_other.arrive_near()
        self.spread_other.arrive_inner()

    def finish(self):
        self.spread_other.arrive_end()

    def drain(self):
        self.cross.wait_send()
        self.spread.drain()
        self.spread_other.drain()


def dot_nn(a, b):
    return jnp.dot(a, b, preferred_element_type=WIDE)


def dot_nt(a, b):
    return lax.dot_general(a, b, (((1,), (1,)), ((), ())), preferred_element_type=WIDE)


def dot_tn(a, b):
    return lax.dot_general(a, b, (((0,), (0,)), ((), ())), preferred_element_type=WIDE)


def fold_rows(values):
    rows, cols = values.shape
    return jnp.sum(values.reshape(rows // 8, 8, cols), axis=0)


class Fold:
    def __init__(self, links, line, block, land):
        self.line, self.block, self.land = line, block, land

        def to(at, where, slot):
            return links.plan(lambda: block(at()), lambda: land(slot), lambda: line.id(where()))

        self.beside = to(line.near, line.near, 0)
        self.across = to(line.second, line.second, 1)
        self.far = to(line.second, line.second, 2)
        self.hand = to(line.third, line.near, 3)
        self.handed = to(line.third, line.third, 1)

    def send(self, k):
        if k == 0:
            self.line.at_end(self.hand.start)
        if k == 1:
            self.line.at_inner(self.across.start)
            self.line.at_end(self.far.start)
        if k == 2:
            self.beside.start()

    def hand_on(self):
        @self.line.at_inner
        def _():
            self.hand.wait_recv()
            block = self.block(self.line.third())
            block[...] = (block[...].astype(WIDE) + self.land(3)[...].astype(WIDE)).astype(LOW)
            self.handed.start()

    def total(self, own, emit):
        self.beside.wait_recv()

        @self.line.at_end
        def _():
            self.handed.wait_recv()
            emit(own() + self.land(0)[...].astype(WIDE) + self.land(1)[...].astype(WIDE))

        @self.line.at_inner
        def _():
            self.across.wait_recv()
            self.far.wait_recv()
            total = own() + self.land(0)[...].astype(WIDE) + self.land(1)[...].astype(WIDE)
            emit(total + self.land(2)[...].astype(WIDE))

    def drain(self):
        self.beside.wait_send()

        @self.line.at_inner
        def _():
            self.across.wait_send()
            self.handed.wait_send()

        @self.line.at_end
        def _():
            self.far.wait_send()
            self.hand.wait_send()


class Scatter:
    def __init__(self, links, place, line, theirs, mine, ybuf, zbuf):
        self.place, self.line, self.mine, self.ybuf = place, line, mine, ybuf
        self.order = [line.third, line.second, line.near, lambda: place.z]
        self.ys = [
            links.plan(lambda at=at: theirs(at()), lambda at=at: ybuf(at()), place.yid)
            for at in self.order
        ]
        self.fold = Fold(links, line, ybuf, zbuf)

    def begin(self):
        for copy in self.ys:
            copy.start()

    def turn(self, k):
        self.ys[k].wait_recv()
        if k < 3:
            at = self.order[k]()
            land = self.ybuf(at)
            land[...] = (land[...].astype(WIDE) + self.mine(at)[...].astype(WIDE)).astype(LOW)
        self.fold.send(k)
        if k == 2:
            self.fold.hand_on()

    def total(self, emit):
        z = self.place.z
        self.fold.total(
            lambda: self.ybuf(z)[...].astype(WIDE) + self.mine(z)[...].astype(WIDE), emit
        )

    def drain(self):
        for copy in self.ys:
            copy.wait_send()
        self.fold.drain()


class ScatterCross:
    def __init__(self, links, place, line, parts, zbuf, hold, land):
        self.place, self.parts, self.hold, self.land = place, parts, hold, land
        self.fold = Fold(links, line, parts, zbuf)
        self.cross = links.plan(lambda: hold.at[1 - place.y], lambda: land, place.yid)

    def begin(self):
        for k in range(3):
            self.fold.send(k)

    def hand_on(self):
        self.fold.hand_on()

    def turn(self):
        def emit(total):
            self.hold[...] = total.astype(LOW)

        self.fold.total(lambda: self.parts(self.place.z)[...].astype(WIDE), emit)
        self.cross.start()

    def total(self):
        self.cross.wait_recv()
        return self.hold[self.place.y].astype(WIDE) + self.land[...].astype(WIDE)

    def drain(self):
        self.cross.wait_send()
        self.fold.drain()


def layer_kernel(
    ny, nz,
    lens, tok, cot, mix_w, out_w, up_w, down_w, norms, freq, scale_in, dct, spread,
    out_rows, grad_rows, gmix_out, gout_out, gup_out, gdown_out, gains_out,
    xs, gs, nf, na, act, gp, feed, gxf, gm,
    up, down, mix, outw, small, gains, meta, table, scale,
    gdown, gout, gout_by, ydown, zdown, ymix, zmix,
    zval, hval, yval, zout, hout, yout,
    up_send, up_recv, mix_send, mix_recv, gacc, gsum, gy, g2, gz, g3, gm_sum,
    send, recv, sems, sib_sems, own_sems, far_sems, sib_free, far_free, act_free,
):
    place = Places(ny, nz)
    y, x, z, c = place.y, place.x, place.z, place.c
    me = x * 2 + c
    micro, span, width = xs.shape[1:]
    shard = out_w.shape[0]
    feed_shard = down_w.shape[0]
    half = up.shape[-1]
    quarter = half // 2
    heads = width // HEAD // 4
    group = heads * HEAD
    none = jnp.zeros((), LOW)
    local = Locals(sems)

    def raw(n):
        return feed.at[3, 0, pl.ds(n * shard, shard)]

    def raw_load(weight, first):
        count = weight.shape[1] // width
        return [
            local.start(weight.at[:, pl.ds(n * width, width)], raw(first + n)) for n in range(count)
        ]

    mix_load = raw_load(mix_w, 0)
    up_load = raw_load(up_w, len(mix_load))
    out_mine = local.start(out_w, outw.at[y, z // 2, z % 2, c])
    tok_mine = local.start(tok, gp.at[0])
    cot_mine = local.start(cot, gs.at[0])
    down_mine = [
        local.start(down_w.at[:, pl.ds(k * half, half)], down.at[k, y, z]) for k in range(2)
    ]
    place.signal()

    row = lax.broadcasted_iota(jnp.int32, (8, 128), 0)
    lane = lax.broadcasted_iota(jnp.int32, (8, 128), 1)
    facts = jnp.zeros((8, 128), WIDE)
    for s in range(micro):
        for k in range(lens.shape[1]):
            facts = jnp.where((row == 1 + s) & (lane == k), lens[s, k].astype(WIDE), facts)
    at_row = lax.broadcasted_iota(jnp.int32, (shard, 128), 0)
    at_lane = lax.broadcasted_iota(jnp.int32, (shard, 128), 1)
    for k in range(4):
        pick = jnp.where(at_lane == at_row + k * shard, 1.0, 0.0).astype(LOW)
        facts = jnp.where(row == 0, facts + dot_nn(norms[k : k + 1, :], pick), facts)
    small[y, x, z, c] = facts

    def up_stage(q):
        return gdown.at[:, q, pl.ds(0, shard), pl.ds(0, half)]

    def mix_stage(t, q):
        return gdown.at[0, q, pl.ds((t + 1) * shard, shard), pl.ds(half, group)]

    def raw_cols(base, first, count):
        at = first % width
        return raw(base + first // width)[:, at : at + count]

    for copy in mix_load:
        copy.wait()
    pair = group // ny
    for q in range(4):
        for t in range(3):
            for by in range(ny):
                first = t * width + ((by * 2 + q // 2) * 2 + q % 2) * pair
                mix_stage(t, q)[:, by * pair : (by + 1) * pair] = raw_cols(0, first, pair)
    for copy in up_load:
        copy.wait()
    for q in range(4):
        for by in range(ny):
            for bz in range(nz):
                first = (((by * 2 + q // 2) * nz + bz) * 2 + q % 2) * feed_shard
                cols = slice(bz * feed_shard, (bz + 1) * feed_shard)
                up_stage(q)[by, :, cols] = raw_cols(len(mix_load), first, feed_shard)
    up[:, y, x, z, c] = up_stage(me)[...]
    for t in range(3):
        mix[t, y, x, z, c] = mix_stage(t, me)[...]
    place.meet()
    links = Links(send, recv)
    line = Line(place)

    def swap(src, dst):
        copies = []
        for r in (1, 2, 3):
            mx, mc = place.member(r)
            copies.append(links.start(src(mx * 2 + mc), dst, place.member_id(r)))
        return copies

    def landed(copies):
        for copy in copies:
            copy.wait_recv()

    small_swaps = swap(lambda q: small.at[y, x, z, c], small.at[y, x, z, c])
    mix_swaps = []
    for t in range(3):
        mix_swaps += swap(lambda q, t=t: mix_stage(t, q), mix.at[t, y, x, z, c])
    up_swaps = swap(up_stage, up.at[:, y, x, z, c])
    chunks = [GatherCross(links, place, line, lambda by, bz: outw.at[by, bz // 2, bz % 2, c])]
    for t in range(3):
        chunks.append(Gather(links, place, line, lambda by, bz, t=t: mix.at[t, by, :, bz]))
    halves = [(k, pl.ds(h * quarter, quarter)) for k in range(2) for h in range(2)]
    for k, cols in halves:
        chunks.append(
            Gather(
                links, place, line,
                lambda by, bz, k=k, cols=cols: up.at[k, by, :, bz, :, :, cols],
            )
        )
    for k, cols in halves:
        way = GatherCross if (k, cols) == halves[-1] else Gather
        chunks.append(
            way(links, place, line, lambda by, bz, k=k, cols=cols: down.at[k, by, bz, :, cols])
        )
    of_mix, of_up, of_down = range(1, 4), range(4, 8), range(8, 12)
    ahead = 3
    hurried = [3]

    def turn_chunk(i):
        chunks[i].forward()
        if i and i - 1 not in hurried:
            chunks[i - 1].late()
        if i + ahead < len(chunks):
            chunks[i + ahead].begin()

    out_mine.wait()
    chunks[0].begin()
    tok_mine.wait()
    tok_sib = links.start(gp.at[0], gp.at[1], place.member_id(1))
    tok_far = links.start(gp.at[0], gp.at[2], place.member_id(2))
    small_gather = Gather(links, place, line, lambda by, bz: small.at[by, :, bz])
    landed(small_swaps)
    small_gather.begin()
    landed(mix_swaps)
    chunks[1].begin()
    chunks[2].begin()
    cot_mine.wait()
    at_place = lax.broadcasted_iota(jnp.int32, (span, 1), 0)
    for s in range(micro):
        used = lens[s, 0]
        for k in range(1, lens.shape[1]):
            used = used + lens[s, k]
        gs[0, s] = jnp.where(at_place < used, gs[0, s], none)
    cot_sib = links.start(gs.at[0], gs.at[1], place.member_id(1))
    cot_far = links.start(gs.at[0], gs.at[2], place.member_id(2))

    raw = lax.dot_general(
        dct[...], freq[...], (((0,), (1,)), ((), ())),
        precision=lax.Precision.HIGHEST, preferred_element_type=WIDE,
    ) / math.sqrt(HEAD)
    raw = raw.astype(LOW)
    tile_row = lax.broadcasted_iota(jnp.int32, (HEAD, group), 0)
    tile_col = lax.broadcasted_iota(jnp.int32, (HEAD, group), 1)
    tiled = jnp.where(tile_col % HEAD == tile_row, 1.0, 0.0).astype(LOW)
    wide_table = dot_tn(tiled, dot_nn(raw, tiled).astype(LOW))
    block_row = lax.broadcasted_iota(jnp.int32, (group, group), 0) // HEAD
    block_col = lax.broadcasted_iota(jnp.int32, (group, group), 1) // HEAD
    table[...] = jnp.where(block_row == block_col, wide_table, 0.0).astype(LOW)
    scale[...] = lax.dot_general(
        jnp.broadcast_to(scale_in[...], (8, HEAD)), tiled.astype(WIDE), (((1,), (0,)), ((), ())),
        precision=lax.Precision.HIGHEST, preferred_element_type=WIDE,
    )

    small_gather.forward()
    small_gather.late()
    turn_chunk(0)
    small_gather.finish()
    count = ny * 2 * nz * 2
    packed = jnp.sum(jnp.where(row == 0, small[...].reshape(count, 8, 128), 0.0), axis=1)
    packed = packed.astype(LOW)
    pick_row = lax.broadcasted_iota(jnp.int32, (128, width), 0)
    pick_col = lax.broadcasted_iota(jnp.int32, (128, width), 1) % shard
    owner = lax.broadcasted_iota(jnp.int32, (count, width), 0)
    owned = lax.broadcasted_iota(jnp.int32, (count, width), 1) // shard
    for k in range(4):
        pick = jnp.where(pick_row == pick_col + k * shard, 1.0, 0.0).astype(LOW)
        part = jnp.where(owned == owner, dot_nn(packed, pick), 0.0)
        gains[k : k + 1, :] = jnp.sum(part, axis=0, keepdims=True)
    gacc[...] = jnp.zeros_like(gacc)

    places = lax.broadcasted_iota(jnp.int32, (1, span), 1).astype(WIDE)
    turn_row = lax.broadcasted_iota(jnp.int32, (ROT // 2, 1), 0)
    inverse = jnp.zeros((ROT // 2, 1), WIDE)
    for k in range(ROT // 2):
        inverse = jnp.where(turn_row == k, 10000.0 ** (-2.0 * k / ROT), inverse)
    fact_row = lax.broadcasted_iota(jnp.int32, (8, span), 0)
    for r in range(4):
        mx, mc = place.member(r)
        facts = small[y, mx, z, mc]
        for s in range(micro):
            end = jnp.zeros((1, 1), WIDE)
            segment = jnp.zeros((1, span), WIDE)
            begin = jnp.zeros((1, span), WIDE)
            for k in range(lens.shape[1]):
                end = end + facts[1 + s : 2 + s, k : k + 1]
                past = places >= end
                segment = segment + jnp.where(past, 1.0, 0.0)
                begin = jnp.where(past, end, begin)
            angle = inverse * (places - begin)
            meta[r, s, 0:8, :] = jnp.cos(angle)
            meta[r, s, 8:16, :] = jnp.sin(angle)
            valid = jnp.where(segment < lens.shape[1], 1.0, 0.0)
            rest = jnp.where(fact_row == 0, segment, jnp.where(fact_row == 1, 1.0, 0.0))
            meta[r, s, 16:24, :] = jnp.where(fact_row == 2, valid, rest)

    def norm(j):
        def body(i, carry):
            s = i // (span // 128)
            rs = pl.ds(pl.multiple_of(i % (span // 128) * 128, 128), 128)
            values = gp[j, s, rs, :].astype(WIDE)
            center = values - jnp.mean(values, axis=1, keepdims=True)
            deviation = jnp.mean(center * center, axis=1, keepdims=True)
            hat = center * lax.rsqrt(deviation + epsilon)
            na[j, s, rs, :] = (hat * gains[0:1, :] + gains[1:2, :]).astype(LOW)
            nf[j, s, rs, :] = (hat * gains[2:3, :] + gains[3:4, :]).astype(LOW)
            xs[j, s, rs, :] = hat.astype(LOW)
            return carry

        lax.fori_loop(0, micro * span // 128, body, 0)

    def loop(first, last, body, events):
        def step(i, carry):
            def pump(part):
                for (at, which), event in events.items():
                    if which == part:

                        @pl.when(i == at)
                        def _(event=event):
                            event()

            body(i, pump)
            return carry

        lax.fori_loop(first, last, step, 0)

    head_lane = lax.broadcasted_iota(jnp.int32, (1, group), 1)
    of_head = [head_lane // HEAD == h for h in range(heads)]
    low_lane = lax.broadcasted_iota(jnp.int32, (1, 128), 1) % HEAD < ROT // 2
    key_at = lax.broadcasted_iota(jnp.int32, (span, span), 1)
    query_at = lax.broadcasted_iota(jnp.int32, (span, span), 0)
    wide_mix = 3 * group

    def turn(values, cosine, sine):
        parts = []
        for first in range(0, group, 128):
            part = values[:, first : first + 128]
            other = jnp.where(
                low_lane, pltpu.roll(part, 128 - ROT // 2, 1), pltpu.roll(part, ROT // 2, 1)
            )
            parts.append(part * cosine + other * sine)
        return jnp.concatenate(parts, axis=1)

    def spread_meta(j, s, first, last):
        return lax.dot_general(
            meta[j, s], spread[:, first:last], (((0,), (0,)), ((), ())),
            precision=lax.Precision.HIGHEST, preferred_element_type=WIDE,
        )

    def attend_forward(j, s):
        rows = na[j, s]
        turns = spread_meta(j, s, 0, 384)
        cosine, sine, owner = turns[:, :128], turns[:, 128:256], turns[:, 256:384]
        owner = jnp.concatenate([owner, owner], axis=1)
        allowed = (owner == meta[j, s, 16:17, :]) & (key_at <= query_at)
        query, key, value = (dot_nn(rows, mix[t].reshape(width, group)) for t in range(3))
        query = turn(query, cosine, sine).astype(LOW)
        key = turn(key, cosine, sine).astype(LOW)
        value = value.astype(LOW)
        raised_query = scale[0:1, :] * jnp.exp(dot_nn(query, table[...]))
        raised_key = scale[0:1, :] * jnp.exp(dot_nn(key, table[...]))
        phi_query = raised_query.astype(LOW)
        phi_key = raised_key.astype(LOW)
        scores, totals = [], []
        numer = jnp.zeros((span, group), WIDE)
        total = jnp.zeros((span, group), WIDE)
        for h in range(heads):
            score = dot_nt(jnp.where(of_head[h], phi_query, none), phi_key)
            score = jnp.where(allowed, score, 0.0)
            totals.append(jnp.sum(score, axis=1, keepdims=True))
            scores.append(score.astype(LOW))
            numer += dot_nn(scores[h], jnp.where(of_head[h], value, none))
            total = jnp.where(of_head[h], totals[h], total)
        att = (numer / total).astype(LOW)
        gm[j, s, :, wide_mix:] = att
        feed[j, s] = dot_nn(att, outw[:, c].reshape(group, width)).astype(LOW)
        return (cosine, sine, allowed, raised_query, raised_key, phi_query, phi_key, value,
                scores, totals, numer, total)

    def attend_back(j, s, kept):
        (cosine, sine, allowed, raised_query, raised_key, phi_query, phi_key, value,
         scores, totals, numer, total) = kept
        grad_att = dot_nt(gs[j, s], outw[:, c].reshape(group, width))
        grad_numer = (grad_att / total).astype(LOW)
        product = grad_att * numer
        grad_query = jnp.zeros((span, group), WIDE)
        grad_key = jnp.zeros((span, group), WIDE)
        grad_value = jnp.zeros((span, group), WIDE)
        for h in range(heads):
            grad_total = -jnp.sum(jnp.where(of_head[h], product, 0.0), axis=1, keepdims=True)
            grad_total = grad_total / (totals[h] * totals[h])
            numer_h = jnp.where(of_head[h], grad_numer, none)
            grad_score = dot_nt(numer_h, value) + grad_total
            grad_score = jnp.where(allowed, grad_score, 0.0).astype(LOW)
            grad_query += dot_nn(grad_score, jnp.where(of_head[h], phi_key, none))
            grad_key += dot_tn(grad_score, jnp.where(of_head[h], phi_query, none))
            grad_value += dot_tn(scores[h], numer_h)
        back_query = turn(
            dot_nt((grad_query * raised_query).astype(LOW), table[...]), cosine, -sine
        )
        back_key = turn(dot_nt((grad_key * raised_key).astype(LOW), table[...]), cosine, -sine)
        parts = (back_query.astype(LOW), back_key.astype(LOW), grad_value.astype(LOW))
        grad_normed = jnp.zeros((span, width), WIDE)
        for t in range(3):
            gm[j, s, :, t * group : (t + 1) * group] = parts[t]
            grad_normed += dot_nt(parts[t], mix[t].reshape(width, group))
        gacc[0:8, :] += fold_rows(grad_normed * xs[j, s].astype(WIDE))
        gacc[8:16, :] += fold_rows(grad_normed)
        gxf[j, s] = (grad_normed * gains[0:1, :]).astype(LOW)

    def attend(j, pump):
        pump(0)
        kept = [attend_forward(j, s) for s in range(micro)]
        pump(1)
        for s in range(micro):
            attend_back(j, s, kept[s])
        pump(2)

    def hidden(k):
        def body(i, pump):
            j, s = i // micro, i % micro
            pump(0)
            h = dot_nn(nf[j, s], up[k].reshape(width, half))
            cdf = 0.5 * (1.0 + lax.erf(h * math.sqrt(0.5)))
            pdf = jnp.exp(-0.5 * h * h) * (1.0 / math.sqrt(2.0 * math.pi))
            act[j, s, :, pl.ds(k * half, half)] = (h * cdf).astype(LOW)
            gp[j, s, :, pl.ds(k * half, half)] = (cdf + h * pdf).astype(LOW)

        return body

    rest = 4 * micro * span
    blocks = width // 256

    def other_first(i):
        return (i + (1 - y) * (blocks // 2)) % blocks

    def outer(a, b, first, last, store):
        def body(i, carry):
            at = other_first(i)
            cols = pl.ds(pl.multiple_of(at * 256, 256), 256)
            store(at, dot_tn(a[:, :, :, cols].reshape(rest, 256), b().reshape(rest, -1)))
            return carry

        lax.fori_loop(first, last, body, 0)

    def keep_down(at, part):
        per = 256 // feed_shard
        for k in range(per):
            block = at * per + k
            rows = slice(k * feed_shard, (k + 1) * feed_shard)
            gdown[block // nz, block % nz] = part[rows].astype(LOW)

    def keep_up(at, part):
        xs[at, 0] = part.astype(LOW)

    def up_block(ref, first, s, at):
        size = 2 * shard
        return ref.at[pl.ds(first, 2), s, pl.ds(pl.multiple_of(at * size, size), size)]

    def keep_mix(at, part):
        for t in range(3):
            cols = part[:, t * group : (t + 1) * group].astype(LOW)
            mix[t, at // 2, at % 2] = cols.reshape(nz, 2, shard, group)

    def outer_down(first, last):
        outer(act, lambda: gs[...], first, last, keep_down)

    def outer_up(first, last):
        outer(nf, lambda: gp[...], first, last, keep_up)

    def outer_mix(first, last):
        outer(na, lambda: gm[:, :, :, 0:wide_mix], first, last, keep_mix)

    down_sum = Scatter(
        links, place, line, lambda at: gdown.at[1 - y, at], lambda at: gdown.at[y, at],
        lambda at: ydown.at[at], lambda k: zdown.at[k],
    )
    up_sum = Scatter(
        links, place, line, lambda at: up_block(xs, (1 - y) * 2, 0, at),
        lambda at: up_block(xs, y * 2, 0, at), lambda at: up_block(act, 0, 0, at),
        lambda k: up_block(act, 0, 1, k),
    )
    two = pl.ds(0, 2)
    mix_sum = Scatter(
        links, place, line, lambda at: mix.at[two, 1 - y, :, at],
        lambda at: mix.at[two, y, :, at], lambda at: ymix.at[at], lambda k: zmix.at[k],
    )
    val_sum = ScatterCross(
        links, place, line, lambda at: mix.at[2, :, :, at], lambda k: zval.at[k], hval, yval
    )
    out_sum = ScatterCross(
        links, place, line, lambda at: gout_by.at[:, at // 2, at % 2], lambda k: zout.at[k],
        hout, yout,
    )

    landed(up_swaps)
    turn_chunk(1)
    norm(0)
    landed([tok_sib])
    norm(1)
    turn_chunk(2)
    chunks[0].finish()
    out_here = outw.at[:, 1 - c, :, c]
    out_swap = links.start(out_here, out_here, place.member_id(1))
    turn_chunk(3)
    for copy in down_mine:
        copy.wait()
    landed([out_swap, cot_sib])
    chunks[3].late()
    for i in of_mix:
        chunks[i].finish()
    tok_fwd = links.plan(gp.at[2], gp.at[3], partial(place.member_id, 1))

    def take_tokens():
        tok_far.wait_recv()
        tok_fwd.start()

    loop(
        0, 2, attend,
        {
            (0, 1): lambda: (turn_chunk(4), take_tokens()),
            (0, 2): lambda: turn_chunk(5),
            (1, 1): lambda: turn_chunk(6),
            (1, 2): lambda: turn_chunk(7),
        },
    )
    norm(2)
    landed([tok_fwd])
    norm(3)
    for copy in (tok_sib, tok_far, tok_fwd):
        copy.wait_send()
    for i in of_up[:2]:
        chunks[i].finish()
    loop(0, 4 * micro, hidden(0), {})
    turn_chunk(8)
    landed([cot_far])
    cot_fwd = links.start(gs.at[2], gs.at[3], place.member_id(1))
    for copy in mix_swaps + up_swaps:
        copy.wait_send()
    landed([cot_fwd])

    loop(
        2, 4, attend,
        {
            (2, 1): lambda: turn_chunk(9),
            (2, 2): lambda: turn_chunk(10),
            (3, 1): lambda: turn_chunk(11),
        },
    )
    for i in of_mix:
        chunks[i].drain()
    outer_mix(0, blocks // 2)
    mix_sum.begin()
    outer_mix(blocks // 2, blocks)
    val_sum.begin()
    part = dot_tn(gm[:, :, :, wide_mix:].reshape(rest, group), gs[...].reshape(rest, width))
    gout[...] = part.astype(LOW).reshape(gout.shape)
    grad_swap = links.start(gout.at[:, :, 1 - c], gout_by.at[:, c], place.member_id(1))
    gout_by[:, c] = gout[:, :, c]
    for sem, r in ((sib_free, 1), (far_free, 2)):
        pl.semaphore_signal(sem, inc=1, device_id=place.member_id(r), device_id_type=MESH_ID)
    for i in of_up[2:]:
        chunks[i].finish()
    loop(0, 4 * micro, hidden(1), {})
    landed([grad_swap])
    out_sum.begin()
    val_sum.hand_on()
    outer_down(0, blocks // 2)
    down_sum.begin()
    mix_sum.turn(0)
    chunks[of_down[-1]].late()
    for i in of_down:
        chunks[i].finish()
    for sem in (sib_free, far_free):
        pl.semaphore_wait(sem, 1)

    def rows_copy(sem, j, r, land):
        def copy(s, kind):
            buf = (feed, gxf)[kind]
            return pltpu.make_async_remote_copy(
                buf.at[j, s], land(kind, s), sem.at[0, kind, s], sem.at[1, kind, s],
                device_id=place.member_id(r), device_id_type=MESH_ID,
            )

        return copy

    sib_copy = rows_copy(sib_sems, 3, 1, lambda kind, s: gm.at[2 + kind, s])
    far_copy = rows_copy(far_sems, 2, 2, lambda kind, s: na.at[kind, s])
    own_copy = rows_copy(own_sems, 1, 1, lambda kind, s: gm.at[kind, s])

    def hand_on(j, s, value, kind):
        buf = (feed, gxf)[kind]

        @pl.when(j != 2)
        def _():
            buf[j, s] = value.astype(LOW)

        @pl.when(j == 3)
        def _():
            sib_copy(s, kind).start()

        @pl.when(j == 2)
        def _():
            sib_copy(s, kind).wait_recv()
            buf[j, s] = (value + gm[2 + kind, s].astype(WIDE)).astype(LOW)
            far_copy(s, kind).start()

        @pl.when(j == 1)
        def _():
            own_copy(s, kind).start()

    def back(i, pump):
        late, r = i // 4, i % 4
        j = (1 - late) * (3 - r % 2) + late * (1 - r // 2)
        s = (1 - late) * (r // 2) + late * (r % 2)
        pump(0)
        rows = act[j, s]
        sums = [dot_nn(rows, down[k].reshape(2 * half, half)) for k in range(2)]
        hand_on(j, s, jnp.concatenate(sums, axis=1) + feed[j, s].astype(WIDE), 0)
        ga = dot_nt(gs[j, s, :, 0:half], down[0].reshape(2 * half, half))
        ga += dot_nt(gs[j, s, :, half : 2 * half], down[1].reshape(2 * half, half))
        gh = (ga * gp[j, s].astype(WIDE)).astype(LOW)
        gp[j, s] = gh
        gn = dot_nt(gh[:, :half], up[0].reshape(width, half))
        gn += dot_nt(gh[:, half:], up[1].reshape(width, half))
        gacc[16:24, :] += fold_rows(gn * xs[j, s].astype(WIDE))
        gacc[24:32, :] += fold_rows(gn)
        hand_on(j, s, gn * gains[2:3, :] + gxf[j, s].astype(WIDE), 1)

    loop(
        0, 4 * micro, back,
        {
            (0, 0): lambda: out_sum.hand_on(),
            (1, 0): lambda: mix_sum.turn(1),
            (2, 0): lambda: mix_sum.turn(2),
            (3, 0): lambda: mix_sum.turn(3),
            (5, 0): lambda: val_sum.turn(),
            (6, 0): lambda: out_sum.turn(),
        },
    )

    gsum[...] = jnp.zeros_like(gsum)
    for k in range(4):
        gsum[k : k + 1, :] = jnp.sum(gacc[8 * k : 8 * k + 8, :], axis=0, keepdims=True)
    gain_y = links.start(gsum, gy, place.yid())
    own_again = local.start(tok, na.at[2])
    outer_down(blocks // 2, blocks)
    for one in [place.yid()] + [place.zid(step) for step in range(1, nz)]:
        pl.semaphore_signal(act_free, inc=1, device_id=one, device_id_type=MESH_ID)
    outer_up(0, blocks // 2)
    pl.semaphore_wait(act_free, nz)
    up_sum.begin()
    for k in range(3):
        down_sum.turn(k)
    outer_up(blocks // 2, blocks)
    landed([gain_y])
    g2[...] = gsum[...] + gy[...]
    gain_zs = [links.start(g2, gz.at[step - 1], place.zid(step)) for step in range(1, nz)]

    def finish(s, carry):
        for kind in (0, 1):
            own_copy(s, kind).wait_recv()
            far_copy(s, kind).wait_recv()
        keep = spread_meta(0, s, 384, 512)[:, :1]
        values = na[2, s].astype(WIDE)
        added = feed[0, s].astype(WIDE) + gm[0, s].astype(WIDE) + na[0, s].astype(WIDE)
        feed[0, s] = (values + keep * added).astype(LOW)
        grad = gxf[0, s].astype(WIDE) + gm[1, s].astype(WIDE) + na[1, s].astype(WIDE)
        center = values - jnp.mean(values, axis=1, keepdims=True)
        rate = lax.rsqrt(jnp.mean(center * center, axis=1, keepdims=True) + epsilon)
        hat = center * rate
        inner = jnp.mean(grad * hat, axis=1, keepdims=True)
        grad = grad - jnp.mean(grad, axis=1, keepdims=True) - hat * inner
        gxf[0, s] = (rate * grad).astype(LOW)
        return carry

    def put_up(qx, qc, values):
        for by in range(ny):
            rows = pl.ds(pl.multiple_of((by * 2 + qx) * shard, shard), shard)
            for bz in range(nz):
                first = (bz * 2 + qc) * feed_shard
                cols = pl.ds(pl.multiple_of(first, feed_shard), feed_shard)
                at = (by * nz + bz) * feed_shard
                nf[0, 0, rows, cols] = values[:, at : at + feed_shard]

    def put_mix(qx, qc, values):
        for t in range(3):
            for by in range(ny):
                first = ((by * 2 + qx) * 2 + qc) * pair
                cols = pl.ds(pl.multiple_of(first, pair), pair)
                nf[0, 1, t * shard : (t + 1) * shard, cols] = values[t, :, by * pair : (by + 1) * pair]

    def put_out(first, dst):
        count = dst.shape[1] // width
        return [
            local.start(nf.at[0, first, pl.ds(n * shard, shard)], dst.at[:, pl.ds(n * width, width)])
            for n in range(count)
        ]

    def share(hold, at, land):
        copies = []
        for r in (1, 2, 3):
            mx, mc = place.member(r)
            copies.append(links.start(at(hold, mx, mc), land.at[r - 1], place.member_id(r)))
        return copies

    def of_mix_share(hold, mx, mc):
        return hold.at[:, mx, mc]

    def of_up_share(hold, mx, mc):
        return hold.at[mx, pl.ds(pl.multiple_of(mc * shard, shard), shard)]

    def collect(copies, hold, at, land, put):
        put(x, c, at(hold, x, c)[...])
        for r in (1, 2, 3):
            mx, mc = place.member(r)
            copies[r - 1].wait_recv()
            put(mx, mc, land[r - 1])

    def keep_sum(hold):
        def emit(total):
            hold[...] = total.astype(LOW)

        return emit

    mix_sum.total(keep_sum(mix_send.at[two]))
    mix_send[2] = val_sum.total().astype(LOW)
    mix_shares = share(mix_send, of_mix_share, mix_recv)
    down_sum.turn(3)
    nf[1, 1, 0:shard, :] = out_sum.total().astype(LOW)
    written = [local.start(nf.at[1, 1, pl.ds(0, shard)], gout_out)]
    collect(mix_shares, mix_send, of_mix_share, mix_recv, put_mix)
    written += put_out(1, gmix_out)
    up_sum.turn(0)
    landed(gain_zs)
    g3[...] = g2[...] + sum(gz[step - 1] for step in range(1, nz))
    gain_ms = [links.start(g3, gm_sum.at[r - 1], place.member_id(r)) for r in (1, 2, 3)]
    up_sum.turn(1)
    up_sum.turn(2)
    down_sum.total(keep_sum(nf.at[1, 0, pl.ds(0, feed_shard)]))
    written.append(local.start(nf.at[1, 0, pl.ds(0, feed_shard)], gdown_out))
    own_again.wait()
    lax.fori_loop(0, micro, finish, 0)
    rows_out = local.start(feed.at[0], out_rows)
    grads_out = local.start(gxf.at[0], grad_rows)
    up_sum.turn(3)
    landed(gain_ms)
    totals = g3[...] + gm_sum[0] + gm_sum[1] + gm_sum[2]
    mine = ((y * 2 + x) * nz + z) * 2 + c
    pick_row = lax.broadcasted_iota(jnp.int32, (width, shard), 0) - mine * shard
    pick_col = lax.broadcasted_iota(jnp.int32, (width, shard), 1)
    gains_out[...] = lax.dot_general(
        totals, jnp.where(pick_row == pick_col, 1.0, 0.0), (((1,), (0,)), ((), ())),
        precision=lax.Precision.HIGHEST, preferred_element_type=WIDE,
    )
    up_sum.total(keep_sum(up_send))
    up_shares = share(up_send, of_up_share, up_recv)
    collect(up_shares, up_send, of_up_share, up_recv, put_up)
    written += put_out(0, gup_out)
    for copy in written + [rows_out, grads_out]:
        copy.wait()
    links.drain()
    for one in chunks + [small_gather, down_sum, up_sum, mix_sum, val_sum, out_sum]:
        one.drain()
    for kind in (0, 1):
        for s in range(micro):
            sib_copy(s, kind).wait_send()
            far_copy(s, kind).wait_send()
            own_copy(s, kind).wait_send()


VMEM = pl.BlockSpec(memory_space=pltpu.VMEM)
SMEM = pl.BlockSpec(memory_space=pltpu.SMEM)
ANY = pl.BlockSpec(memory_space=pl.ANY)
SHAPE = jax.ShapeDtypeStruct
LIMIT = 59 * 2**20


def cosine_basis():
    order, sample = np.arange(HEAD)[:, None], np.arange(HEAD)[None, :]
    factor = np.where(order == 0, math.sqrt(1.0 / HEAD), math.sqrt(2.0 / HEAD))
    return (factor * np.cos(math.pi * (2 * sample + 1) * order / (2 * HEAD))).astype(np.float32)


def spread_rows():
    row = np.arange(24)[:, None]
    lane = np.arange(512)[None, :]
    part, dim = lane // 128, lane % HEAD
    half = ROT // 2
    cosine = (part == 0) & (dim < ROT) & (row == dim % half)
    cosine = cosine | ((part == 0) & (dim >= ROT) & (row == 17))
    sine = (part == 1) & (dim < ROT) & (row == half + dim % half)
    rest = ((part == 2) & (row == 16)) | ((part == 3) & (row == 18))
    sign = np.where((part == 1) & (dim < half), -1.0, 1.0)
    return np.where(cosine | sine | rest, sign, 0.0).astype(np.float32)


def per_device_group(
    ny,
    nz,
    tokens,
    lengths,
    mix_weight,
    out_weight,
    up_weight,
    down_weight,
    attn_gain,
    attn_bias,
    feed_gain,
    feed_bias,
    feature_freq,
    feature_scale,
    cotangent,
):
    micro, span, width = tokens.shape
    shard = mix_weight.shape[0]
    feed_shard = down_weight.shape[0]
    group = width // 4
    hidden = feed_shard * ny * nz
    half = hidden // 2
    norms = jnp.stack([attn_gain, attn_bias, feed_gain, feed_bias])

    dma = pltpu.SemaphoreType.DMA
    whole = pltpu.VMEM((4, micro, span, width), LOW)

    def low(*shape):
        return pltpu.VMEM(shape, LOW)

    def wide(*shape):
        return pltpu.VMEM(shape, WIDE)

    out_rows, grad_rows, gmix, gout, gup, gdown, gains = pl.pallas_call(
        partial(layer_kernel, ny, nz),
        out_shape=[
            SHAPE((micro, span, width), LOW),
            SHAPE((micro, span, width), LOW),
            SHAPE(mix_weight.shape, LOW),
            SHAPE(out_weight.shape, LOW),
            SHAPE(up_weight.shape, LOW),
            SHAPE(down_weight.shape, LOW),
            SHAPE((8, shard), WIDE),
        ],
        in_specs=[SMEM] + [ANY] * 6 + [VMEM] * 5,
        out_specs=[ANY] * 6 + [VMEM],
        scratch_shapes=[whole] * 9
        + [
            low(2, ny, 2, nz, 2, shard, half),
            low(2, ny, nz, feed_shard, half),
            low(3, ny, 2, nz, 2, shard, group),
            low(ny, nz // 2, 2, 2, shard, width),
            wide(ny, 2, nz, 2, 8, 128),
            wide(8, width),
            wide(4, micro, 24, span),
            low(group, group),
            wide(8, group),
            low(ny, nz, feed_shard, width),
            low(ny, 2, 2, shard, width),
            low(ny, nz // 2, 2, shard, width),
            low(nz, feed_shard, width),
            low(4, feed_shard, width),
            low(nz, 2, 2, 2, shard, group),
            low(4, 2, 2, 2, shard, group),
            low(4, ny, 2, 2, shard, group),
            low(ny, 2, 2, shard, group),
            low(2, 2, shard, group),
            low(4, ny, shard, width),
            low(ny, shard, width),
            low(shard, width),
            low(2, 2 * shard, hidden),
            low(3, shard, hidden),
            low(3, 2, 2, shard, group),
            low(3, 3, shard, group),
            wide(32, width),
            wide(8, width),
            wide(8, width),
            wide(8, width),
            wide(nz - 1, 8, width),
            wide(8, width),
            wide(3, 8, width),
            dma((200,)),
            dma((200,)),
            dma((28,)),
            dma((2, 2, 2)),
            dma((2, 2, 2)),
            dma((2, 2, 2)),
            pltpu.SemaphoreType.REGULAR,
            pltpu.SemaphoreType.REGULAR,
            pltpu.SemaphoreType.REGULAR,
        ],
        name="layer",
        cost_estimate=pl.CostEstimate(flops=45 * 10**9, bytes_accessed=20 * 10**6, transcendentals=0),
        compiler_params=pltpu.CompilerParams(
            collective_id=0, has_side_effects=True, vmem_limit_bytes=LIMIT
        ),
    )(
        lengths[:, 0], tokens, cotangent, mix_weight, out_weight, up_weight, down_weight, norms,
        feature_freq, feature_scale[None], cosine_basis(), spread_rows(),
    )
    return (
        out_rows,
        cotangent.astype(WIDE) + grad_rows.astype(WIDE),
        gmix.astype(WIDE),
        gout.astype(WIDE),
        gup.astype(WIDE),
        gdown.astype(WIDE),
        gains[0],
        gains[1],
        gains[2],
        gains[3],
    )


def solution(mesh):
    ny, nz = mesh.shape["dp"] // 2, mesh.shape["fsdp"] // 2
    grouped = ny == 2 and nz == 4 and D // mesh.size % 32 == 0
    body = partial(per_device_group, ny, nz) if grouped else per_device_plain
    rows = P(("dp", "fsdp"), None)
    vector = P(("dp", "fsdp"))
    slots = P(None, ("dp", "fsdp"), None)
    return jax.shard_map(
        body,
        mesh=mesh,
        in_specs=(slots, slots, *[rows] * 4, *[vector] * 4, P(), P(), slots),
        out_specs=(slots, slots, *[rows] * 4, *[vector] * 4),
        check_vma=False,
    )
```

```python
from functools import partial
import math

import jax
import jax.numpy as jnp
import numpy as np
from jax import lax
from jax.experimental import pallas as pl
from jax.experimental.pallas import tpu as pltpu
from jax.sharding import PartitionSpec as P

D = 1024
HEAD = 64
ROT = 16


epsilon = 1e-05
exact_precision = lax.Precision.HIGHEST


def dct_matrix(width):
    order = jnp.arange(width, dtype=jnp.float32)[:, None]
    sample = jnp.arange(width, dtype=jnp.float32)[None, :]
    factor = jnp.where(order == 0, jnp.sqrt(1.0 / width), jnp.sqrt(2.0 / width))
    return factor * jnp.cos(math.pi * (2.0 * sample + 1.0) * order / (2.0 * width))


def feature_table(feature_freq):
    table = jnp.dot(dct_matrix(HEAD).T, feature_freq.T, precision=exact_precision) / math.sqrt(HEAD)
    return table.astype(jnp.bfloat16)


def slot_layout(span_table, slot_len):
    seg_ends = jnp.cumsum(span_table, axis=-1)
    seg_starts = seg_ends - span_table
    places = jnp.arange(slot_len, dtype=jnp.int32)
    segment = jnp.sum((places[:, None] >= seg_ends[..., None, :]).astype(jnp.int32), axis=-1)
    numbers = jnp.arange(span_table.shape[-1], dtype=jnp.int32)
    matched = segment[..., None] == numbers
    begin_at = jnp.sum(jnp.where(matched, seg_starts[..., None, :], 0), axis=-1)
    begin_at = begin_at + jnp.where(segment == span_table.shape[-1], seg_ends[..., -1:], 0)
    position = (places - begin_at).astype(jnp.float32)
    valid = (segment < span_table.shape[-1]).astype(jnp.float32)
    return (segment, position, valid)


def rotate(raw_heads, position):
    half_rot = ROT // 2
    inverse = 10000.0 ** (-2.0 * jnp.arange(half_rot, dtype=jnp.float32) / ROT)
    angle = position[..., None] * inverse
    cosine_wave = jnp.cos(angle)[..., None, :]
    sine = jnp.sin(angle)[..., None, :]
    first = raw_heads[..., :half_rot]
    second = raw_heads[..., half_rot:ROT]
    return jnp.concatenate(
        [
            first * cosine_wave - second * sine,
            second * cosine_wave + first * sine,
            raw_heads[..., ROT:],
        ],
        axis=-1,
    )


def feature_map(raw_heads, position, table, feature_scale):
    rotated_rows = rotate(raw_heads, position).astype(jnp.bfloat16)
    pre = jnp.einsum("shd,df->shf", rotated_rows, table, preferred_element_type=jnp.float32)
    return feature_scale * jnp.exp(pre)


def feature_back(raw_heads, grad_phi, position, table, feature_scale):
    phi = feature_map(raw_heads, position, table, feature_scale)
    grad_pre = (grad_phi * phi).astype(jnp.bfloat16)
    grad_turned = jnp.einsum("shf,df->shd", grad_pre, table, preferred_element_type=jnp.float32)
    _, turn_pull = jax.vjp(lambda values: rotate(values, position), raw_heads)
    return turn_pull(grad_turned)[0]


def norm_apply(inputs, gain, shift):
    center = inputs - jnp.mean(inputs, axis=-1, keepdims=True)
    spread = jnp.mean(center * center, axis=-1, keepdims=True)
    return center * lax.rsqrt(spread + epsilon) * gain + shift


def head_major(values):
    return jnp.swapaxes(values, 0, 1)


def attend_head(allowed, pieces):
    mapped_query, mapped_key, value_rows = pieces
    score_matrix = jnp.einsum(
        "qf,kf->qk", mapped_query, mapped_key, preferred_element_type=jnp.float32
    )
    score_matrix = jnp.where(allowed, score_matrix, 0.0)
    totals = jnp.sum(score_matrix, axis=1)
    numerator = jnp.dot(
        score_matrix.astype(jnp.bfloat16), value_rows, preferred_element_type=jnp.float32
    )
    return numerator / totals[:, None]


def attend_back(allowed, pieces):
    mapped_query, mapped_key, value_rows, grad_heads = pieces
    score_matrix = jnp.einsum(
        "qf,kf->qk", mapped_query, mapped_key, preferred_element_type=jnp.float32
    )
    score_matrix = jnp.where(allowed, score_matrix, 0.0)
    totals = jnp.sum(score_matrix, axis=1)
    scores_low = score_matrix.astype(jnp.bfloat16)
    numerator = jnp.dot(scores_low, value_rows, preferred_element_type=jnp.float32)
    grad_numer = (grad_heads / totals[:, None]).astype(jnp.bfloat16)
    grad_totals = -jnp.sum(grad_heads * numerator, axis=1) / (totals * totals)
    grad_scores = jnp.einsum(
        "qd,kd->qk", grad_numer, value_rows, preferred_element_type=jnp.float32
    )
    grad_scores = jnp.where(allowed, grad_scores + grad_totals[:, None], 0.0).astype(jnp.bfloat16)
    grad_query = jnp.dot(grad_scores, mapped_key, preferred_element_type=jnp.float32)
    grad_key = jnp.einsum(
        "qk,qf->kf", grad_scores, mapped_query, preferred_element_type=jnp.float32
    )
    grad_value = jnp.einsum("qk,qd->kd", scores_low, grad_numer, preferred_element_type=jnp.float32)
    return (grad_query, grad_key, grad_value)


def fetch_attention(shards):
    return (
        lax.all_gather(shards[0], ("dp", "fsdp"), axis=0, tiled=True),
        lax.all_gather(shards[1], ("dp", "fsdp"), axis=0, tiled=True),
        lax.all_gather(shards[2], ("dp", "fsdp"), axis=0, tiled=True),
        lax.all_gather(shards[3], ("dp", "fsdp"), axis=0, tiled=True),
    )


def fetch_feed(shards):
    return (
        lax.all_gather(shards[0], ("dp", "fsdp"), axis=0, tiled=True),
        lax.all_gather(shards[1], ("dp", "fsdp"), axis=0, tiled=True),
        lax.all_gather(shards[2], ("dp", "fsdp"), axis=0, tiled=True),
        lax.all_gather(shards[3], ("dp", "fsdp"), axis=0, tiled=True),
    )


def reduce_attention(grads):
    return (
        lax.psum_scatter(grads[0], ("dp", "fsdp"), scatter_dimension=0, tiled=True),
        lax.psum_scatter(grads[1], ("dp", "fsdp"), scatter_dimension=0, tiled=True),
        lax.psum_scatter(grads[2], ("dp", "fsdp"), scatter_dimension=0, tiled=True),
        lax.psum_scatter(grads[3], ("dp", "fsdp"), scatter_dimension=0, tiled=True),
    )


def reduce_feed(grads):
    return (
        lax.psum_scatter(grads[0], ("dp", "fsdp"), scatter_dimension=0, tiled=True),
        lax.psum_scatter(grads[1], ("dp", "fsdp"), scatter_dimension=0, tiled=True),
        lax.psum_scatter(grads[2], ("dp", "fsdp"), scatter_dimension=0, tiled=True),
        lax.psum_scatter(grads[3], ("dp", "fsdp"), scatter_dimension=0, tiled=True),
    )


def add_tuples(running, update):
    if running is None:
        return tuple(update)
    return tuple(jax.tree.map(jnp.add, tuple(running), tuple(update)))


def per_device_plain(
    tokens,
    lengths,
    mix_weight,
    out_weight,
    up_weight,
    down_weight,
    attn_gain,
    attn_bias,
    feed_gain,
    feed_bias,
    feature_freq,
    feature_scale,
    cotangent,
):
    table = feature_table(feature_freq)
    slot_len = tokens.shape[1]
    head_count = D // HEAD
    attn_shards = (mix_weight, out_weight, attn_gain, attn_bias)
    feed_shards = (up_weight, down_weight, feed_gain, feed_bias)
    places = jnp.arange(slot_len, dtype=jnp.int32)
    output_rows = []
    grad_inputs = []
    attn_total = None
    feed_total = None
    for micro_index in range(tokens.shape[0]):
        attn_full = fetch_attention(attn_shards)
        feed_full = fetch_feed(feed_shards)
        mix_full, out_full, gain_one, bias_one = attn_full
        up_full, down_full, gain_two, bias_two = feed_full
        gain_attn = gain_one.astype(jnp.float32)
        shift_attn = bias_one.astype(jnp.float32)
        gain_feed = gain_two.astype(jnp.float32)
        shift_feed = bias_two.astype(jnp.float32)
        inputs = tokens[micro_index].astype(jnp.float32)
        segment, position, valid = slot_layout(lengths[micro_index, 0], slot_len)
        allowed = (segment[:, None] == segment[None, :]) & (places[None, :] <= places[:, None])
        normed_attn = norm_apply(inputs, gain_attn, shift_attn).astype(jnp.bfloat16)
        normed_feed = norm_apply(inputs, gain_feed, shift_feed).astype(jnp.bfloat16)
        mixed = jnp.dot(normed_attn, mix_full, preferred_element_type=jnp.float32)
        mixed = mixed.reshape(slot_len, 3, head_count, HEAD)
        query_raw = mixed[:, 0]
        key_raw = mixed[:, 1]
        value_rows = mixed[:, 2].astype(jnp.bfloat16)
        mapped_query = feature_map(query_raw, position, table, feature_scale).astype(jnp.bfloat16)
        mapped_key = feature_map(key_raw, position, table, feature_scale).astype(jnp.bfloat16)
        attended = lax.map(
            partial(attend_head, allowed),
            (head_major(mapped_query), head_major(mapped_key), head_major(value_rows)),
        )
        attended = head_major(attended).reshape(slot_len, D).astype(jnp.bfloat16)
        attn_rows = jnp.dot(attended, out_full, preferred_element_type=jnp.float32)
        hidden = jnp.dot(normed_feed, up_full, preferred_element_type=jnp.float32)
        active = jax.nn.gelu(hidden, approximate=False).astype(jnp.bfloat16)
        feed_rows = jnp.dot(active, down_full, preferred_element_type=jnp.float32)
        result = inputs + valid[:, None] * (attn_rows + feed_rows)
        output_rows.append(result.astype(jnp.bfloat16))
        attn_full = fetch_attention(attn_shards)
        feed_full = fetch_feed(feed_shards)
        mix_full, out_full, gain_one, bias_one = attn_full
        up_full, down_full, gain_two, bias_two = feed_full
        grad_rows = cotangent[micro_index]
        grad_branch = jnp.where(valid[:, None] > 0.0, grad_rows, jnp.zeros_like(grad_rows))
        grad_down = jnp.einsum("sf,sd->fd", active, grad_branch, preferred_element_type=jnp.float32)
        grad_out = jnp.einsum(
            "sd,se->de", attended, grad_branch, preferred_element_type=jnp.float32
        )
        grad_active = jnp.einsum(
            "sd,fd->sf", grad_branch, down_full, preferred_element_type=jnp.float32
        )
        _, gelu_pull = jax.vjp(partial(jax.nn.gelu, approximate=False), hidden)
        grad_hidden = gelu_pull(grad_active)[0].astype(jnp.bfloat16)
        grad_up = jnp.einsum(
            "sd,sf->df", normed_feed, grad_hidden, preferred_element_type=jnp.float32
        )
        grad_normed_feed = jnp.einsum(
            "sf,df->sd", grad_hidden, up_full, preferred_element_type=jnp.float32
        )
        grad_attended = jnp.einsum(
            "sd,ed->se", grad_branch, out_full, preferred_element_type=jnp.float32
        )
        grad_attended = grad_attended.reshape(slot_len, head_count, HEAD)
        grad_phi_q, grad_phi_k, grad_value = lax.map(
            partial(attend_back, allowed),
            (
                head_major(mapped_query),
                head_major(mapped_key),
                head_major(value_rows),
                head_major(grad_attended),
            ),
        )
        grad_query = feature_back(query_raw, head_major(grad_phi_q), position, table, feature_scale)
        grad_key = feature_back(key_raw, head_major(grad_phi_k), position, table, feature_scale)
        grad_mixed = jnp.stack([grad_query, grad_key, head_major(grad_value)], axis=1)
        grad_mixed = grad_mixed.reshape(slot_len, 3 * D).astype(jnp.bfloat16)
        grad_mix = jnp.einsum(
            "sd,se->de", normed_attn, grad_mixed, preferred_element_type=jnp.float32
        )
        grad_normed_attn = jnp.einsum(
            "se,de->sd", grad_mixed, mix_full, preferred_element_type=jnp.float32
        )
        _, attn_norm_pull = jax.vjp(norm_apply, inputs, gain_attn, shift_attn)
        grad_in_one, grad_gain_one, grad_bias_one = attn_norm_pull(grad_normed_attn)
        _, feed_norm_pull = jax.vjp(norm_apply, inputs, gain_feed, shift_feed)
        grad_in_two, grad_gain_two, grad_bias_two = feed_norm_pull(grad_normed_feed)
        grad_inputs.append(grad_rows.astype(jnp.float32) + grad_in_one + grad_in_two)
        attn_grads = (grad_mix, grad_out, grad_gain_one, grad_bias_one)
        feed_grads = (grad_up, grad_down, grad_gain_two, grad_bias_two)
        attn_grads = reduce_attention(attn_grads)
        feed_grads = reduce_feed(feed_grads)
        attn_total = add_tuples(attn_total, attn_grads)
        feed_total = add_tuples(feed_total, feed_grads)
    return (
        jnp.stack(output_rows),
        jnp.stack(grad_inputs),
        attn_total[0],
        attn_total[1],
        feed_total[0],
        feed_total[1],
        attn_total[2],
        attn_total[3],
        feed_total[2],
        feed_total[3],
    )


MESH_ID = pl.DeviceIdType.MESH
LOW = jnp.bfloat16
WIDE = jnp.float32


def here(nz):
    dp = lax.axis_index("dp")
    fs = lax.axis_index("fsdp")
    return dp // 2, dp % 2, fs // 2, fs % 2


class Places:
    def __init__(self, ny, nz):
        self.ny, self.nz = ny, nz
        self.y, self.x, self.z, self.c = here(nz)

    def at(self, y, x, z, c):
        return (y * 2 + x, z * 2 + c)

    def member(self, r):
        x = 1 - self.x if r & 2 else self.x
        c = 1 - self.c if r & 1 else self.c
        return x, c

    def member_id(self, r):
        x, c = self.member(r)
        return self.at(self.y, x, self.z, c)

    def yid(self):
        return self.at(1 - self.y, self.x, self.z, self.c)

    def zid(self, step):
        return self.at(self.y, self.x, (self.z + step) % self.nz, self.c)

    def zsrc(self, step):
        return (self.z + self.nz - step) % self.nz

    def signal(self):
        barrier = pltpu.get_barrier_semaphore()
        ids = [self.member_id(r) for r in (1, 2, 3)] + [self.yid()]
        ids += [self.zid(step) for step in range(1, self.nz)]
        for one in ids:
            pl.semaphore_signal(barrier, inc=1, device_id=one, device_id_type=MESH_ID)

    def meet(self):
        pl.semaphore_wait(pltpu.get_barrier_semaphore(), self.nz + 3)


class Copy:
    def __init__(self, describe):
        self.describe, self.sent = describe, False

    def start(self):
        self.describe().start()

    def wait_recv(self):
        self.describe().wait_recv()

    def wait_send(self):
        if not self.sent:
            self.describe().wait_send()
            self.sent = True


class Links:
    def __init__(self, send, recv):
        self.send, self.recv, self.count, self.open = send, recv, 0, []

    def plan(self, src, dst, device):
        i = self.count
        self.count += 1

        def describe():
            return pltpu.make_async_remote_copy(
                src() if callable(src) else src,
                dst() if callable(dst) else dst,
                self.send.at[i],
                self.recv.at[i],
                device_id=device() if callable(device) else device,
                device_id_type=MESH_ID,
            )

        return Copy(describe)

    def start(self, src, dst, device):
        copy = self.plan(src, dst, device)
        copy.start()
        self.open.append(copy)
        return copy

    def drain(self):
        for copy in self.open:
            copy.wait_send()


class Locals:
    def __init__(self, sems):
        self.sems, self.count = sems, 0

    def start(self, src, dst):
        copy = pltpu.make_async_copy(src, dst, self.sems.at[self.count])
        self.count += 1
        copy.start()
        return copy


class Line:
    def __init__(self, place):
        z = place.z
        self.place = place
        self.way = 1 - 2 * (z // 2)
        self.inner = (z // 2) * (3 - z) + (1 - z // 2) * z

    def off(self, end, inner):
        return self.place.z + self.way * ((1 - self.inner) * end + self.inner * inner)

    def near(self):
        return self.off(1, -1)

    def second(self):
        return self.off(2, 1)

    def third(self):
        return self.off(3, 2)

    def id(self, z):
        return self.place.at(self.place.y, self.place.x, z, self.place.c)

    def at_end(self, event):
        pl.when(self.inner == 0)(event)

    def at_inner(self, event):
        pl.when(self.inner == 1)(event)


class Spread:
    def __init__(self, links, line, block, own=None):
        z = line.place.z
        mine = own if own is not None else lambda: block(z)

        def here():
            return block(z)

        def second():
            return block(line.second())

        def third():
            return block(line.third())

        self.line = line
        self.sources = [line.near, line.second, line.third]
        self.beside = links.plan(mine, here, lambda: line.id(line.near()))
        self.across = links.plan(mine, here, lambda: line.id(line.second()))
        self.far = links.plan(mine, here, lambda: line.id(line.second()))
        self.hand_second = links.plan(second, second, lambda: line.id(line.near()))
        self.hand_third = links.plan(third, third, lambda: line.id(line.near()))

    def begin(self):
        self.beside.start()
        self.line.at_inner(self.across.start)
        self.line.at_end(self.far.start)

    def arrive_near(self, then=None):
        self.beside.wait_recv()
        if then:
            then[0].start()

    def arrive_inner(self, then=None):
        @self.line.at_inner
        def _():
            self.across.wait_recv()
            self.hand_second.start()
            if then:
                then[1].start()
            self.far.wait_recv()
            self.hand_third.start()
            if then:
                then[2].start()

    def arrive_end(self, then=None):
        @self.line.at_end
        def _():
            self.hand_second.wait_recv()
            if then:
                then[1].start()
            self.hand_third.wait_recv()
            if then:
                then[2].start()

    def drain(self):
        self.beside.wait_send()

        @self.line.at_inner
        def _():
            for copy in (self.across, self.hand_second, self.hand_third):
                copy.wait_send()

        self.line.at_end(self.far.wait_send)


class Direct:
    def __init__(self, links, line, block, own=None):
        place = line.place
        self.sources = [partial(place.zsrc, step) for step in range(1, place.nz)]
        mine = own if own is not None else lambda: block(place.z)
        self.copies = [
            links.plan(mine, lambda: block(place.z), partial(place.zid, step))
            for step in range(1, place.nz)
        ]

    def begin(self):
        for copy in self.copies:
            copy.start()

    def arrive_near(self, then=()):
        for k, copy in enumerate(self.copies):
            copy.wait_recv()
            if then:
                then[k].start()

    def arrive_inner(self, then=None):
        pass

    def arrive_end(self, then=None):
        pass

    def drain(self):
        for copy in self.copies:
            copy.wait_send()


class Gather:
    def __init__(self, links, place, line, block, own=None, way=Spread):
        def plane(z):
            return block(place.y, z)

        self.spread = way(links, line, plane, own)
        mine = own if own is not None else lambda: plane(place.z)
        self.cross = links.plan(mine, lambda: plane(place.z), place.yid)
        self.cross_on = [
            links.plan(lambda at=at: plane(at()), lambda at=at: plane(at()), place.yid)
            for at in self.spread.sources
        ]

    def begin(self):
        self.spread.begin()
        self.cross.start()

    def forward(self):
        self.spread.arrive_near(self.cross_on)
        self.spread.arrive_inner(self.cross_on)

    def late(self):
        self.spread.arrive_end(self.cross_on)

    def finish(self):
        for copy in [self.cross] + self.cross_on:
            copy.wait_recv()

    def drain(self):
        self.spread.drain()
        for copy in [self.cross] + self.cross_on:
            copy.wait_send()


class GatherCross:
    def __init__(self, links, place, line, block, own=None, way=Spread):
        def plane(z):
            return block(place.y, z)

        def other(z):
            return block(1 - place.y, z)

        mine = own if own is not None else lambda: plane(place.z)
        self.cross = links.plan(mine, lambda: plane(place.z), place.yid)
        self.spread = way(links, line, plane, own)
        self.spread_other = way(links, line, other)

    def begin(self):
        self.cross.start()
        self.spread.begin()

    def forward(self):
        self.cross.wait_recv()
        self.spread_other.begin()
        self.spread.arrive_near()
        self.spread.arrive_inner()

    def late(self):
        self.spread.arrive_end()
        self.spread_other.arrive_near()
        self.spread_other.arrive_inner()

    def finish(self):
        self.spread_other.arrive_end()

    def drain(self):
        self.cross.wait_send()
        self.spread.drain()
        self.spread_other.drain()


def dot_nn(a, b):
    return jnp.dot(a, b, preferred_element_type=WIDE)


def dot_nt(a, b):
    return lax.dot_general(a, b, (((1,), (1,)), ((), ())), preferred_element_type=WIDE)


def dot_tn(a, b):
    return lax.dot_general(a, b, (((0,), (0,)), ((), ())), preferred_element_type=WIDE)


def fold_rows(values):
    rows, cols = values.shape
    return jnp.sum(values.reshape(rows // 8, 8, cols), axis=0)


class Fold:
    def __init__(self, links, line, block, land):
        self.line, self.block, self.land = line, block, land

        def to(at, where, slot):
            return links.plan(lambda: block(at()), lambda: land(slot), lambda: line.id(where()))

        self.beside = to(line.near, line.near, 0)
        self.across = to(line.second, line.second, 1)
        self.far = to(line.second, line.second, 2)
        self.hand = to(line.third, line.near, 3)
        self.handed = to(line.third, line.third, 1)

    def send(self, k):
        if k == 0:
            self.line.at_inner(self.across.start)
            self.line.at_end(self.far.start)
        if k == 1:
            self.line.at_end(self.hand.start)
        if k == 2:
            self.beside.start()

    def hand_on(self):
        @self.line.at_inner
        def _():
            self.hand.wait_recv()
            block = self.block(self.line.third())
            block[...] = (block[...].astype(WIDE) + self.land(3)[...].astype(WIDE)).astype(LOW)
            self.handed.start()

    def total(self, own, emit):
        self.beside.wait_recv()

        @self.line.at_end
        def _():
            self.handed.wait_recv()
            emit(own() + self.land(0)[...].astype(WIDE) + self.land(1)[...].astype(WIDE))

        @self.line.at_inner
        def _():
            self.across.wait_recv()
            self.far.wait_recv()
            total = own() + self.land(0)[...].astype(WIDE) + self.land(1)[...].astype(WIDE)
            emit(total + self.land(2)[...].astype(WIDE))

    def drain(self):
        self.beside.wait_send()

        @self.line.at_inner
        def _():
            self.across.wait_send()
            self.handed.wait_send()

        @self.line.at_end
        def _():
            self.far.wait_send()
            self.hand.wait_send()


class Scatter:
    def __init__(self, links, place, line, theirs, mine, ybuf, zbuf):
        self.place, self.line, self.mine, self.ybuf = place, line, mine, ybuf
        self.order = [line.second, line.third, line.near, lambda: place.z]
        self.ys = [
            links.plan(lambda at=at: theirs(at()), lambda at=at: ybuf(at()), place.yid)
            for at in self.order
        ]
        self.fold = Fold(links, line, ybuf, zbuf)

    def begin(self):
        for copy in self.ys:
            copy.start()

    def turn(self, k):
        self.ys[k].wait_recv()
        if k < 3:
            at = self.order[k]()
            land = self.ybuf(at)
            land[...] = (land[...].astype(WIDE) + self.mine(at)[...].astype(WIDE)).astype(LOW)
        self.fold.send(k)
        if k == 2:
            self.fold.hand_on()

    def total(self, emit):
        z = self.place.z
        self.fold.total(
            lambda: self.ybuf(z)[...].astype(WIDE) + self.mine(z)[...].astype(WIDE), emit
        )

    def drain(self):
        for copy in self.ys:
            copy.wait_send()
        self.fold.drain()


class ScatterCross:
    def __init__(self, links, place, line, parts, zbuf, hold, land):
        self.place, self.parts, self.hold, self.land = place, parts, hold, land
        self.fold = Fold(links, line, parts, zbuf)
        self.cross = links.plan(lambda: hold.at[1 - place.y], lambda: land, place.yid)

    def begin(self):
        for k in range(3):
            self.fold.send(k)

    def hand_on(self):
        self.fold.hand_on()

    def turn(self):
        def emit(total):
            self.hold[...] = total.astype(LOW)

        self.fold.total(lambda: self.parts(self.place.z)[...].astype(WIDE), emit)
        self.cross.start()

    def total(self):
        self.cross.wait_recv()
        return self.hold[self.place.y].astype(WIDE) + self.land[...].astype(WIDE)

    def drain(self):
        self.cross.wait_send()
        self.fold.drain()


def layer_kernel(
    ny, nz,
    lens, tok, cot, mix_w, out_w, up_w, down_w, norms, freq, scale_in, dct, spread,
    out_rows, grad_rows, gmix_out, gout_out, gup_out, gdown_out, gains_out,
    xs, gs, nf, na, act, gp, feed, gxf, gm,
    up, down, mix, outw, small, gains, meta, table, scale,
    gdown, ydown, zdown, ymix, zmix,
    zval, hval, yval, zout, hout, yout,
    up_send, up_recv, mix_send, mix_recv, gacc, gsum, gy, g2, gz, g3, gm_sum,
    send, recv, sems, sib_sems, own_sems, far_sems, out_free, sib_free, far_free, act_free,
):
    place = Places(ny, nz)
    y, x, z, c = place.y, place.x, place.z, place.c
    me = x * 2 + c
    micro, span, width = xs.shape[1:]
    shard = out_w.shape[0]
    feed_shard = down_w.shape[0]
    half = up.shape[-1]
    quarter = half // 2
    heads = width // HEAD // 4
    group = heads * HEAD
    none = jnp.zeros((), LOW)
    local = Locals(sems)

    def raw(n):
        return feed.at[3, 0, pl.ds(n * shard, shard)]

    def raw_load(weight, first):
        count = weight.shape[1] // width
        return [
            local.start(weight.at[:, pl.ds(n * width, width)], raw(first + n)) for n in range(count)
        ]

    mix_load = raw_load(mix_w, 0)
    up_load = raw_load(up_w, len(mix_load))
    out_mine = local.start(out_w, outw.at[y, z // 2, z % 2, c])
    tok_mine = local.start(tok, gp.at[0])
    cot_mine = local.start(cot, gs.at[0])
    down_mine = [
        local.start(down_w.at[:, pl.ds(k * half, half)], down.at[k, y, z]) for k in range(2)
    ]
    place.signal()

    row = lax.broadcasted_iota(jnp.int32, (8, 128), 0)
    lane = lax.broadcasted_iota(jnp.int32, (8, 128), 1)
    facts = jnp.zeros((8, 128), WIDE)
    for s in range(micro):
        for k in range(lens.shape[1]):
            facts = jnp.where((row == 1 + s) & (lane == k), lens[s, k].astype(WIDE), facts)
    at_row = lax.broadcasted_iota(jnp.int32, (shard, 128), 0)
    at_lane = lax.broadcasted_iota(jnp.int32, (shard, 128), 1)
    for k in range(4):
        pick = jnp.where(at_lane == at_row + k * shard, 1.0, 0.0).astype(LOW)
        facts = jnp.where(row == 0, facts + dot_nn(norms[k : k + 1, :], pick), facts)
    small[y, x, z, c] = facts

    def up_stage(q):
        return gdown.at[:, q, pl.ds(0, shard), pl.ds(0, half)]

    def mix_stage(t, q):
        return gdown.at[0, q, pl.ds((t + 1) * shard, shard), pl.ds(half, group)]

    def raw_cols(base, first, count):
        at = first % width
        return raw(base + first // width)[:, at : at + count]

    for copy in mix_load:
        copy.wait()
    pair = group // ny
    for q in range(4):
        for t in range(3):
            for by in range(ny):
                first = t * width + ((by * 2 + q // 2) * 2 + q % 2) * pair
                mix_stage(t, q)[:, by * pair : (by + 1) * pair] = raw_cols(0, first, pair)
    for copy in up_load:
        copy.wait()
    for q in range(4):
        for by in range(ny):
            for bz in range(nz):
                first = (((by * 2 + q // 2) * nz + bz) * 2 + q % 2) * feed_shard
                cols = slice(bz * feed_shard, (bz + 1) * feed_shard)
                up_stage(q)[by, :, cols] = raw_cols(len(mix_load), first, feed_shard)
    up[:, y, x, z, c] = up_stage(me)[...]
    for t in range(3):
        mix[t, y, x, z, c] = mix_stage(t, me)[...]
    place.meet()
    links = Links(send, recv)
    line = Line(place)

    def swap(src, dst):
        copies = []
        for r in (1, 2, 3):
            mx, mc = place.member(r)
            copies.append(links.start(src(mx * 2 + mc), dst, place.member_id(r)))
        return copies

    def landed(copies):
        for copy in copies:
            copy.wait_recv()

    small_swaps = swap(lambda q: small.at[y, x, z, c], small.at[y, x, z, c])
    mix_swaps = []
    for t in range(3):
        mix_swaps += swap(lambda q, t=t: mix_stage(t, q), mix.at[t, y, x, z, c])
    up_swaps = swap(up_stage, up.at[:, y, x, z, c])
    chunks = [GatherCross(links, place, line, lambda by, bz: outw.at[by, bz // 2, bz % 2, c])]
    for t in range(3):
        chunks.append(Gather(links, place, line, lambda by, bz, t=t: mix.at[t, by, :, bz]))
    halves = [(k, pl.ds(h * quarter, quarter)) for k in range(2) for h in range(2)]
    for k, cols in halves:
        chunks.append(
            Gather(
                links, place, line,
                lambda by, bz, k=k, cols=cols: up.at[k, by, :, bz, :, :, cols],
            )
        )
    for k, cols in halves:
        way = GatherCross if (k, cols) == halves[-1] else Gather
        chunks.append(
            way(links, place, line, lambda by, bz, k=k, cols=cols: down.at[k, by, bz, :, cols])
        )
    of_mix, of_up, of_down = range(1, 4), range(4, 8), range(8, 12)
    ahead = 3
    hurried = [3]

    def turn_chunk(i):
        chunks[i].forward()
        if i and i - 1 not in hurried:
            chunks[i - 1].late()
        if i + ahead < len(chunks):
            chunks[i + ahead].begin()

    out_mine.wait()
    chunks[0].begin()
    tok_mine.wait()
    tok_sib = links.start(gp.at[0], gp.at[1], place.member_id(1))
    tok_far = links.start(gp.at[0], gp.at[2], place.member_id(2))
    small_gather = Gather(links, place, line, lambda by, bz: small.at[by, :, bz])
    landed(small_swaps)
    small_gather.begin()
    landed(mix_swaps)
    chunks[1].begin()
    chunks[2].begin()
    cot_mine.wait()
    at_place = lax.broadcasted_iota(jnp.int32, (span, 1), 0)
    for s in range(micro):
        used = lens[s, 0]
        for k in range(1, lens.shape[1]):
            used = used + lens[s, k]
        gs[0, s] = jnp.where(at_place < used, gs[0, s], none)
    cot_sib = links.start(gs.at[0], gs.at[1], place.member_id(1))
    cot_far = links.start(gs.at[0], gs.at[2], place.member_id(2))

    raw = lax.dot_general(
        dct[...], freq[...], (((0,), (1,)), ((), ())),
        precision=lax.Precision.HIGHEST, preferred_element_type=WIDE,
    ) / math.sqrt(HEAD)
    raw = raw.astype(LOW)
    tile_row = lax.broadcasted_iota(jnp.int32, (HEAD, group), 0)
    tile_col = lax.broadcasted_iota(jnp.int32, (HEAD, group), 1)
    tiled = jnp.where(tile_col % HEAD == tile_row, 1.0, 0.0).astype(LOW)
    wide_table = dot_tn(tiled, dot_nn(raw, tiled).astype(LOW))
    block_row = lax.broadcasted_iota(jnp.int32, (group, group), 0) // HEAD
    block_col = lax.broadcasted_iota(jnp.int32, (group, group), 1) // HEAD
    table[...] = jnp.where(block_row == block_col, wide_table, 0.0).astype(LOW)
    scale[...] = lax.dot_general(
        jnp.broadcast_to(scale_in[...], (8, HEAD)), tiled.astype(WIDE), (((1,), (0,)), ((), ())),
        precision=lax.Precision.HIGHEST, preferred_element_type=WIDE,
    )

    small_gather.forward()
    small_gather.late()
    turn_chunk(0)
    small_gather.finish()
    count = ny * 2 * nz * 2
    packed = jnp.sum(jnp.where(row == 0, small[...].reshape(count, 8, 128), 0.0), axis=1)
    packed = packed.astype(LOW)
    pick_row = lax.broadcasted_iota(jnp.int32, (128, width), 0)
    pick_col = lax.broadcasted_iota(jnp.int32, (128, width), 1) % shard
    owner = lax.broadcasted_iota(jnp.int32, (count, width), 0)
    owned = lax.broadcasted_iota(jnp.int32, (count, width), 1) // shard
    for k in range(4):
        pick = jnp.where(pick_row == pick_col + k * shard, 1.0, 0.0).astype(LOW)
        part = jnp.where(owned == owner, dot_nn(packed, pick), 0.0)
        gains[k : k + 1, :] = jnp.sum(part, axis=0, keepdims=True)
    gacc[...] = jnp.zeros_like(gacc)

    places = lax.broadcasted_iota(jnp.int32, (1, span), 1).astype(WIDE)
    turn_row = lax.broadcasted_iota(jnp.int32, (ROT // 2, 1), 0)
    inverse = jnp.zeros((ROT // 2, 1), WIDE)
    for k in range(ROT // 2):
        inverse = jnp.where(turn_row == k, 10000.0 ** (-2.0 * k / ROT), inverse)
    fact_row = lax.broadcasted_iota(jnp.int32, (8, span), 0)
    for r in range(4):
        mx, mc = place.member(r)
        facts = small[y, mx, z, mc]
        for s in range(micro):
            end = jnp.zeros((1, 1), WIDE)
            segment = jnp.zeros((1, span), WIDE)
            begin = jnp.zeros((1, span), WIDE)
            for k in range(lens.shape[1]):
                end = end + facts[1 + s : 2 + s, k : k + 1]
                past = places >= end
                segment = segment + jnp.where(past, 1.0, 0.0)
                begin = jnp.where(past, end, begin)
            angle = inverse * (places - begin)
            valid = jnp.where(segment < lens.shape[1], 1.0, 0.0)
            rest = jnp.where(fact_row == 0, segment, jnp.where(fact_row == 1, 1.0, 0.0))
            rest = jnp.where(fact_row == 2, valid, rest)
            left = jnp.concatenate([jnp.cos(angle), jnp.sin(angle)], axis=0)
            for first in (0, 24, 40):
                part = left.astype(LOW)
                left = left - part.astype(WIDE)
                meta[r, s, first : first + 16, :] = part
            meta[r, s, 16:24, :] = rest.astype(LOW)
            meta[r, s, 56:64, :] = jnp.zeros((8, span), LOW)

    def norm(j):
        def body(i, carry):
            s = i // (span // 128)
            rs = pl.ds(pl.multiple_of(i % (span // 128) * 128, 128), 128)
            values = gp[j, s, rs, :].astype(WIDE)
            center = values - jnp.mean(values, axis=1, keepdims=True)
            deviation = jnp.mean(center * center, axis=1, keepdims=True)
            hat = center * lax.rsqrt(deviation + epsilon)
            na[j, s, rs, :] = (hat * gains[0:1, :] + gains[1:2, :]).astype(LOW)
            nf[j, s, rs, :] = (hat * gains[2:3, :] + gains[3:4, :]).astype(LOW)
            xs[j, s, rs, :] = hat.astype(LOW)
            return carry

        lax.fori_loop(0, micro * span // 128, body, 0)

    def loop(first, last, body, events):
        def step(i, carry):
            def pump(part):
                for (at, which), event in events.items():
                    if which == part:

                        @pl.when(i == at)
                        def _(event=event):
                            event()

            body(i, pump)
            return carry

        lax.fori_loop(first, last, step, 0)

    head_lane = lax.broadcasted_iota(jnp.int32, (1, group), 1)
    of_head = [head_lane // HEAD == h for h in range(heads)]
    low_lane = lax.broadcasted_iota(jnp.int32, (1, 128), 1) % HEAD < ROT // 2
    key_at = lax.broadcasted_iota(jnp.int32, (span, span), 1)
    query_at = lax.broadcasted_iota(jnp.int32, (span, span), 0)
    wide_mix = 3 * group

    def turn(values, cosine, sine):
        parts = []
        for first in range(0, group, 128):
            part = values[:, first : first + 128]
            other = jnp.where(
                low_lane, pltpu.roll(part, 128 - ROT // 2, 1), pltpu.roll(part, ROT // 2, 1)
            )
            parts.append(part * cosine + other * sine)
        return jnp.concatenate(parts, axis=1)

    def spread_meta(j, s, first, last):
        return dot_tn(meta[j, s], spread[:, first:last])

    def attend_forward(j, s):
        rows = na[j, s]
        turns = spread_meta(j, s, 0, 384)
        cosine, sine, owner = turns[:, :128], turns[:, 128:256], turns[:, 256:384]
        owner = jnp.concatenate([owner, owner], axis=1)
        allowed = (owner == meta[j, s, 16:24, :][0:1, :].astype(WIDE)) & (key_at <= query_at)
        query, key, value = (dot_nn(rows, mix[t].reshape(width, group)) for t in range(3))
        query = turn(query, cosine, sine).astype(LOW)
        key = turn(key, cosine, sine).astype(LOW)
        value = value.astype(LOW)
        raised_query = scale[0:1, :] * jnp.exp(dot_nn(query, table[...]))
        raised_key = scale[0:1, :] * jnp.exp(dot_nn(key, table[...]))
        phi_query = raised_query.astype(LOW)
        phi_key = raised_key.astype(LOW)
        scores, totals = [], []
        numer = jnp.zeros((span, group), WIDE)
        total = jnp.zeros((span, group), WIDE)
        for h in range(heads):
            score = dot_nt(jnp.where(of_head[h], phi_query, none), phi_key)
            score = jnp.where(allowed, score, 0.0)
            totals.append(jnp.sum(score, axis=1, keepdims=True))
            scores.append(score.astype(LOW))
            numer += dot_nn(scores[h], jnp.where(of_head[h], value, none))
            total = jnp.where(of_head[h], totals[h], total)
        att = (numer / total).astype(LOW)
        gm[j, s, :, wide_mix:] = att
        return (att, cosine, sine, allowed, raised_query, raised_key, phi_query, phi_key, value,
                scores, totals, numer, total)

    def attend_back(j, s, kept):
        (att, cosine, sine, allowed, raised_query, raised_key, phi_query, phi_key, value,
         scores, totals, numer, total) = kept
        feed[j, s] = dot_nn(att, outw[:, c].reshape(group, width)).astype(LOW)
        grad_att = dot_nt(gs[j, s], outw[:, c].reshape(group, width))
        grad_numer = (grad_att / total).astype(LOW)
        product = grad_att * numer
        grad_query = jnp.zeros((span, group), WIDE)
        grad_key = jnp.zeros((span, group), WIDE)
        grad_value = jnp.zeros((span, group), WIDE)
        for h in range(heads):
            grad_total = -jnp.sum(jnp.where(of_head[h], product, 0.0), axis=1, keepdims=True)
            grad_total = grad_total / (totals[h] * totals[h])
            numer_h = jnp.where(of_head[h], grad_numer, none)
            grad_score = dot_nt(numer_h, value) + grad_total
            grad_score = jnp.where(allowed, grad_score, 0.0).astype(LOW)
            grad_query += dot_nn(grad_score, jnp.where(of_head[h], phi_key, none))
            grad_key += dot_tn(grad_score, jnp.where(of_head[h], phi_query, none))
            grad_value += dot_tn(scores[h], numer_h)
        back_query = turn(
            dot_nt((grad_query * raised_query).astype(LOW), table[...]), cosine, -sine
        )
        back_key = turn(dot_nt((grad_key * raised_key).astype(LOW), table[...]), cosine, -sine)
        parts = (back_query.astype(LOW), back_key.astype(LOW), grad_value.astype(LOW))
        grad_normed = jnp.zeros((span, width), WIDE)
        for t in range(3):
            gm[j, s, :, t * group : (t + 1) * group] = parts[t]
            grad_normed += dot_nt(parts[t], mix[t].reshape(width, group))
        gacc[0:8, :] += fold_rows(grad_normed * xs[j, s].astype(WIDE))
        gacc[8:16, :] += fold_rows(grad_normed)
        gxf[j, s] = (grad_normed * gains[0:1, :]).astype(LOW)

    def attend(j, pump):
        kept = []
        for s in range(micro):
            kept.append(attend_forward(j, s))
            pump(s)
        for s in range(micro):
            attend_back(j, s, kept[s])
            pump(micro + s)

    def hidden(k):
        def body(i, pump):
            j, s = i // micro, i % micro
            pump(0)
            h = dot_nn(nf[j, s], up[k].reshape(width, half))
            cdf = 0.5 * (1.0 + lax.erf(h * math.sqrt(0.5)))
            pdf = jnp.exp(-0.5 * h * h) * (1.0 / math.sqrt(2.0 * math.pi))
            act[j, s, :, pl.ds(k * half, half)] = (h * cdf).astype(LOW)
            gp[j, s, :, pl.ds(k * half, half)] = (cdf + h * pdf).astype(LOW)

        return body

    rest = 4 * micro * span
    blocks = width // 256

    def other_first(i):
        return (i + (1 - y) * (blocks // 2)) % blocks

    def outer(a, b, first, last, store):
        def body(i, carry):
            at = other_first(i)
            cols = pl.ds(pl.multiple_of(at * 256, 256), 256)
            store(at, dot_tn(a[:, :, :, cols].reshape(rest, 256), b().reshape(rest, -1)))
            return carry

        lax.fori_loop(first, last, body, 0)

    def keep_down(at, part):
        per = 256 // feed_shard
        for k in range(per):
            block = at * per + k
            rows = slice(k * feed_shard, (k + 1) * feed_shard)
            gdown[block // nz, block % nz] = part[rows].astype(LOW)

    def keep_up(at, part):
        na[2 + at // 2, at % 2] = part.astype(LOW)

    def up_block(ref, j, at, cols):
        size = 2 * shard
        return ref.at[j, :, pl.ds(pl.multiple_of(at * size, size), size), cols]

    def keep_mix(at, part):
        for t in range(3):
            cols = part[:, t * group : (t + 1) * group].astype(LOW)
            mix[t, at // 2, at % 2] = cols.reshape(nz, 2, shard, group)

    def outer_down(first, last):
        outer(act, lambda: gs[...], first, last, keep_down)

    def outer_up(first, last):
        outer(nf, lambda: gp[...], first, last, keep_up)

    def outer_mix(first, last):
        outer(na, lambda: gm[:, :, :, 0:wide_mix], first, last, keep_mix)

    down_sum = Scatter(
        links, place, line, lambda at: gdown.at[1 - y, at], lambda at: gdown.at[y, at],
        lambda at: ydown.at[at], lambda k: zdown.at[k],
    )
    up_sums = []
    for k in range(2):
        cols = pl.ds(k * half, half)
        up_sums.append(
            Scatter(
                links, place, line,
                lambda at, cols=cols: up_block(na, 3 - y, at, cols),
                lambda at, cols=cols: up_block(na, 2 + y, at, cols),
                lambda at, cols=cols: up_block(act, 2, at, cols),
                lambda at, cols=cols: up_block(act, 3, at, cols),
            )
        )
    two = pl.ds(0, 2)
    mix_sum = Scatter(
        links, place, line, lambda at: mix.at[two, 1 - y, :, at],
        lambda at: mix.at[two, y, :, at], lambda at: ymix.at[at], lambda k: zmix.at[k],
    )
    val_sum = ScatterCross(
        links, place, line, lambda at: mix.at[2, :, :, at], lambda k: zval.at[k], hval, yval
    )
    out_sum = ScatterCross(
        links, place, line, lambda at: outw.at[:, at // 2, at % 2, c], lambda k: zout.at[k],
        hout, yout,
    )

    landed(up_swaps)
    turn_chunk(1)
    norm(0)
    landed([tok_sib])
    norm(1)
    turn_chunk(2)
    chunks[0].finish()
    out_here = outw.at[:, 1 - c, :, c]
    out_swap = links.start(out_here, out_here, place.member_id(1))
    turn_chunk(3)
    for copy in down_mine:
        copy.wait()
    landed([out_swap, cot_sib])
    chunks[3].late()
    for i in of_mix:
        chunks[i].finish()
    tok_fwd = links.plan(gp.at[2], gp.at[3], partial(place.member_id, 1))

    def take_tokens():
        tok_far.wait_recv()
        tok_fwd.start()

    loop(
        0, 2, attend,
        {
            (0, 0): lambda: turn_chunk(4),
            (0, 1): take_tokens,
            (0, 2): lambda: turn_chunk(5),
            (1, 0): lambda: turn_chunk(6),
            (1, 2): lambda: turn_chunk(7),
        },
    )
    norm(2)
    landed([tok_fwd])
    norm(3)
    for copy in (tok_sib, tok_far, tok_fwd):
        copy.wait_send()
    for i in of_up[:2]:
        chunks[i].finish()
    loop(0, 4 * micro, hidden(0), {})
    turn_chunk(8)
    cot_fwd = links.plan(gs.at[2], gs.at[3], partial(place.member_id, 1))

    def take_cot():
        cot_far.wait_recv()
        cot_fwd.start()

    for copy in mix_swaps + up_swaps:
        copy.wait_send()

    chunks[0].drain()
    out_swap.wait_send()
    pl.semaphore_signal(out_free, inc=1, device_id=place.member_id(1), device_id_type=MESH_ID)

    loop(
        2, 4, attend,
        {
            (2, 0): lambda: turn_chunk(9),
            (2, 1): take_cot,
            (2, 2): lambda: turn_chunk(10),
            (3, 0): lambda: turn_chunk(11),
            (3, 1): cot_fwd.wait_recv,
            (3, 2): chunks[11].late,
        },
    )
    for i in of_mix:
        chunks[i].drain()
    outer_mix(0, blocks // 2)
    mix_sum.begin()
    outer_mix(blocks // 2, blocks)
    val_sum.begin()
    part = dot_tn(gm[:, :, :, wide_mix:].reshape(rest, group), gs[...].reshape(rest, width))
    outw[:, c] = part.astype(LOW).reshape(ny, 2, 2, shard, width)
    pl.semaphore_wait(out_free, 1)
    of_sibling = outw.at[:, c, :, 1 - c]
    grad_swap = links.start(of_sibling, of_sibling, place.member_id(1))
    for sem, r in ((sib_free, 1), (far_free, 2)):
        pl.semaphore_signal(sem, inc=1, device_id=place.member_id(r), device_id_type=MESH_ID)
    for i in of_up[2:]:
        chunks[i].finish()
    loop(0, 4 * micro, hidden(1), {})
    landed([grad_swap])
    out_sum.begin()
    val_sum.hand_on()
    outer_down(0, blocks // 2)
    down_sum.begin()
    mix_sum.turn(0)
    for i in of_down:
        chunks[i].finish()
    for sem in (sib_free, far_free):
        pl.semaphore_wait(sem, 1)

    def rows_copy(sem, j, r, land):
        def copy(s, kind):
            buf = (feed, gxf)[kind]
            return pltpu.make_async_remote_copy(
                buf.at[j, s], land(kind, s), sem.at[0, kind, s], sem.at[1, kind, s],
                device_id=place.member_id(r), device_id_type=MESH_ID,
            )

        return copy

    sib_copy = rows_copy(sib_sems, 3, 1, lambda kind, s: gm.at[2 + kind, s])
    far_copy = rows_copy(far_sems, 2, 2, lambda kind, s: na.at[kind, s])
    own_copy = rows_copy(own_sems, 1, 1, lambda kind, s: gm.at[kind, s])

    def hand_on(j, s, value, kind):
        buf = (feed, gxf)[kind]

        @pl.when(j != 2)
        def _():
            buf[j, s] = value.astype(LOW)

        @pl.when(j == 3)
        def _():
            sib_copy(s, kind).start()

        @pl.when(j == 2)
        def _():
            sib_copy(s, kind).wait_recv()
            buf[j, s] = (value + gm[2 + kind, s].astype(WIDE)).astype(LOW)
            far_copy(s, kind).start()

        @pl.when(j == 1)
        def _():
            own_copy(s, kind).start()

    def grad_hidden(j, s):
        ga = dot_nt(gs[j, s, :, 0:half], down[0].reshape(2 * half, half))
        ga += dot_nt(gs[j, s, :, half : 2 * half], down[1].reshape(2 * half, half))
        gp[j, s] = (ga * gp[j, s].astype(WIDE)).astype(LOW)

    def rows_out_of(j, s):
        rows = act[j, s]
        sums = [dot_nn(rows, down[k].reshape(2 * half, half)) for k in range(2)]
        hand_on(j, s, jnp.concatenate(sums, axis=1) + feed[j, s].astype(WIDE), 0)

    def rows_back(j, s):
        gh = gp[j, s]
        gn = dot_nt(gh[:, :half], up[0].reshape(width, half))
        gn += dot_nt(gh[:, half:], up[1].reshape(width, half))
        gacc[16:24, :] += fold_rows(gn * xs[j, s].astype(WIDE))
        gacc[24:32, :] += fold_rows(gn)
        hand_on(j, s, gn * gains[2:3, :] + gxf[j, s].astype(WIDE), 1)

    def back_far(i, pump):
        j, s = 3 - i % 2, i // 2
        pump(0)
        rows_out_of(j, s)
        grad_hidden(j, s)
        rows_back(j, s)

    def back_own(i, pump):
        pump(0)
        grad_hidden(i // micro, i % micro)

    def rows_own(i, pump):
        j, s = 1 - i // micro, i % micro
        pump(0)
        rows_out_of(j, s)
        rows_back(j, s)

    loop(
        0, 2 * micro, back_far,
        {
            (0, 0): lambda: out_sum.hand_on(),
            (1, 0): lambda: mix_sum.turn(1),
            (2, 0): lambda: mix_sum.turn(2),
            (3, 0): lambda: mix_sum.turn(3),
        },
    )
    outer_down(blocks // 2, blocks)
    for one in [place.yid()] + [place.zid(step) for step in range(1, nz)]:
        pl.semaphore_signal(act_free, inc=1, device_id=one, device_id_type=MESH_ID)
    loop(
        0, 2 * micro, back_own,
        {
            (0, 0): lambda: (val_sum.turn(), out_sum.turn()),
            (1, 0): lambda: down_sum.turn(0),
            (2, 0): lambda: down_sum.turn(1),
        },
    )
    outer_up(0, blocks // 2)
    pl.semaphore_wait(act_free, nz)
    first_up, second_up = up_sums
    first_up.begin()
    loop(
        0, 2 * micro, rows_own,
        {
            (0, 0): lambda: down_sum.turn(2),
            (1, 0): lambda: down_sum.turn(3),
        },
    )
    gsum[...] = jnp.zeros_like(gsum)
    for k in range(4):
        gsum[k : k + 1, :] = jnp.sum(gacc[8 * k : 8 * k + 8, :], axis=0, keepdims=True)
    gain_y = links.start(gsum, gy, place.yid())
    second_up.begin()
    outer_up(blocks // 2, blocks)
    own_again = local.start(tok, xs.at[0])

    def finish(s, carry):
        for kind in (0, 1):
            own_copy(s, kind).wait_recv()
            far_copy(s, kind).wait_recv()
        keep = spread_meta(0, s, 384, 512)[:, :1]
        values = xs[0, s].astype(WIDE)
        added = feed[0, s].astype(WIDE) + gm[0, s].astype(WIDE) + na[0, s].astype(WIDE)
        feed[0, s] = (values + keep * added).astype(LOW)
        grad = gxf[0, s].astype(WIDE) + gm[1, s].astype(WIDE) + na[1, s].astype(WIDE)
        center = values - jnp.mean(values, axis=1, keepdims=True)
        rate = lax.rsqrt(jnp.mean(center * center, axis=1, keepdims=True) + epsilon)
        hat = center * rate
        inner = jnp.mean(grad * hat, axis=1, keepdims=True)
        grad = grad - jnp.mean(grad, axis=1, keepdims=True) - hat * inner
        gxf[0, s] = (rate * grad).astype(LOW)
        return carry

    def put_up(k, qx, qc, values):
        rows = pl.ds(pl.multiple_of((k * 2 + qx) * shard, shard), shard)
        for bz in range(nz):
            first = (bz * 2 + qc) * feed_shard
            cols = pl.ds(pl.multiple_of(first, feed_shard), feed_shard)
            nf[0, 0, rows, cols] = values[:, bz * feed_shard : (bz + 1) * feed_shard]

    def put_mix(qx, qc, values):
        for t in range(3):
            for by in range(ny):
                first = ((by * 2 + qx) * 2 + qc) * pair
                cols = pl.ds(pl.multiple_of(first, pair), pair)
                nf[0, 1, t * shard : (t + 1) * shard, cols] = values[t, :, by * pair : (by + 1) * pair]

    def put_out(first, dst):
        count = dst.shape[1] // width
        return [
            local.start(nf.at[0, first, pl.ds(n * shard, shard)], dst.at[:, pl.ds(n * width, width)])
            for n in range(count)
        ]

    def share(hold, at, land):
        copies = []
        for r in (1, 2, 3):
            mx, mc = place.member(r)
            copies.append(links.start(at(hold, mx, mc), land.at[r - 1], place.member_id(r)))
        return copies

    def of_mix_share(hold, mx, mc):
        return hold.at[:, mx, mc]

    def of_up_share(hold, mx, mc):
        return hold.at[mx, pl.ds(pl.multiple_of(mc * shard, shard), shard)]

    def collect(copies, hold, at, land, put):
        put(x, c, at(hold, x, c)[...])
        for r in (1, 2, 3):
            mx, mc = place.member(r)
            copies[r - 1].wait_recv()
            put(mx, mc, land.at[r - 1][...])

    def keep_sum(hold):
        def emit(total):
            hold[...] = total.astype(LOW)

        return emit

    for one in chunks + [small_gather]:
        one.drain()
    mix_sum.total(keep_sum(mix_send.at[two]))
    mix_send[2] = val_sum.total().astype(LOW)
    mix_shares = share(mix_send, of_mix_share, mix_recv)
    nf[1, 1, 0:shard, :] = out_sum.total().astype(LOW)
    written = [local.start(nf.at[1, 1, pl.ds(0, shard)], gout_out)]
    first_up.turn(0)
    first_up.turn(1)
    down_sum.total(keep_sum(nf.at[1, 0, pl.ds(0, feed_shard)]))
    written.append(local.start(nf.at[1, 0, pl.ds(0, feed_shard)], gdown_out))
    first_up.turn(2)
    for one in (down_sum, mix_sum, val_sum, out_sum):
        one.drain()
    first_up.turn(3)
    landed([gain_y])
    g2[...] = gsum[...] + gy[...]
    gain_zs = [links.start(g2, gz.at[step - 1], place.zid(step)) for step in range(1, nz)]
    second_up.turn(0)
    second_up.turn(1)
    second_up.turn(2)
    first_up.total(keep_sum(up_send.at[0]))
    up_shares = [share(up_send.at[0], of_up_share, up_recv.at[0])]
    second_up.turn(3)
    landed(gain_zs)
    g3[...] = g2[...] + sum(gz[step - 1] for step in range(1, nz))
    gain_ms = [links.start(g3, gm_sum.at[r - 1], place.member_id(r)) for r in (1, 2, 3)]
    own_again.wait()
    lax.fori_loop(0, micro, finish, 0)
    rows_out = local.start(feed.at[0], out_rows)
    grads_out = local.start(gxf.at[0], grad_rows)
    collect(mix_shares, mix_send, of_mix_share, mix_recv, put_mix)
    written += put_out(1, gmix_out)
    collect(up_shares[0], up_send.at[0], of_up_share, up_recv.at[0], partial(put_up, 0))
    second_up.total(keep_sum(up_send.at[1]))
    up_shares.append(share(up_send.at[1], of_up_share, up_recv.at[1]))
    landed(gain_ms)
    totals = g3[...] + gm_sum[0] + gm_sum[1] + gm_sum[2]
    mine = ((y * 2 + x) * nz + z) * 2 + c
    pick_row = lax.broadcasted_iota(jnp.int32, (width, shard), 0) - mine * shard
    pick_col = lax.broadcasted_iota(jnp.int32, (width, shard), 1)
    gains_out[...] = lax.dot_general(
        totals, jnp.where(pick_row == pick_col, 1.0, 0.0), (((1,), (0,)), ((), ())),
        precision=lax.Precision.HIGHEST, preferred_element_type=WIDE,
    )
    collect(up_shares[1], up_send.at[1], of_up_share, up_recv.at[1], partial(put_up, 1))
    written += put_out(0, gup_out)
    for copy in written + [rows_out, grads_out]:
        copy.wait()
    cot_fwd.wait_send()
    links.drain()
    for one in up_sums + [down_sum, mix_sum, val_sum, out_sum]:
        one.drain()
    for kind in (0, 1):
        for s in range(micro):
            sib_copy(s, kind).wait_send()
            far_copy(s, kind).wait_send()
            own_copy(s, kind).wait_send()


VMEM = pl.BlockSpec(memory_space=pltpu.VMEM)
SMEM = pl.BlockSpec(memory_space=pltpu.SMEM)
ANY = pl.BlockSpec(memory_space=pl.ANY)
SHAPE = jax.ShapeDtypeStruct
LIMIT = 59 * 2**20


def cosine_basis():
    order, sample = np.arange(HEAD)[:, None], np.arange(HEAD)[None, :]
    factor = np.where(order == 0, math.sqrt(1.0 / HEAD), math.sqrt(2.0 / HEAD))
    return (factor * np.cos(math.pi * (2 * sample + 1) * order / (2 * HEAD))).astype(np.float32)


def spread_rows():
    row = np.arange(64)[:, None]
    turn = np.where(row < 16, row, np.where((row >= 24) & (row < 56), (row - 24) % 16, -1))
    lane = np.arange(512)[None, :]
    part, dim = lane // 128, lane % HEAD
    half = ROT // 2
    cosine = (part == 0) & (dim < ROT) & (turn == dim % half)
    cosine = cosine | ((part == 0) & (dim >= ROT) & (row == 17))
    sine = (part == 1) & (dim < ROT) & (turn == half + dim % half)
    rest = ((part == 2) & (row == 16)) | ((part == 3) & (row == 18))
    sign = np.where((part == 1) & (dim < half), -1.0, 1.0)
    return np.where(cosine | sine | rest, sign, 0.0).astype(jnp.bfloat16)


def per_device_group(
    ny,
    nz,
    tokens,
    lengths,
    mix_weight,
    out_weight,
    up_weight,
    down_weight,
    attn_gain,
    attn_bias,
    feed_gain,
    feed_bias,
    feature_freq,
    feature_scale,
    cotangent,
):
    micro, span, width = tokens.shape
    shard = mix_weight.shape[0]
    feed_shard = down_weight.shape[0]
    group = width // 4
    hidden = feed_shard * ny * nz
    half = hidden // 2
    norms = jnp.stack([attn_gain, attn_bias, feed_gain, feed_bias])

    dma = pltpu.SemaphoreType.DMA
    whole = pltpu.VMEM((4, micro, span, width), LOW)

    def low(*shape):
        return pltpu.VMEM(shape, LOW)

    def wide(*shape):
        return pltpu.VMEM(shape, WIDE)

    out_rows, grad_rows, gmix, gout, gup, gdown, gains = pl.pallas_call(
        partial(layer_kernel, ny, nz),
        out_shape=[
            SHAPE((micro, span, width), LOW),
            SHAPE((micro, span, width), LOW),
            SHAPE(mix_weight.shape, LOW),
            SHAPE(out_weight.shape, LOW),
            SHAPE(up_weight.shape, LOW),
            SHAPE(down_weight.shape, LOW),
            SHAPE((8, shard), WIDE),
        ],
        in_specs=[SMEM] + [ANY] * 6 + [VMEM] * 5,
        out_specs=[ANY] * 6 + [VMEM],
        scratch_shapes=[whole] * 9
        + [
            low(2, ny, 2, nz, 2, shard, half),
            low(2, ny, nz, feed_shard, half),
            low(3, ny, 2, nz, 2, shard, group),
            low(ny, nz // 2, 2, 2, shard, width),
            wide(ny, 2, nz, 2, 8, 128),
            wide(8, width),
            low(4, micro, 64, span),
            low(group, group),
            wide(8, group),
            low(ny, nz, feed_shard, width),
            low(nz, feed_shard, width),
            low(4, feed_shard, width),
            low(nz, 2, 2, 2, shard, group),
            low(4, 2, 2, 2, shard, group),
            low(4, ny, 2, 2, shard, group),
            low(ny, 2, 2, shard, group),
            low(2, 2, shard, group),
            low(4, ny, shard, width),
            low(ny, shard, width),
            low(shard, width),
            low(2, 2, 2 * shard, half),
            low(2, 3, shard, half),
            low(3, 2, 2, shard, group),
            low(3, 3, shard, group),
            wide(32, width),
            wide(8, width),
            wide(8, width),
            wide(8, width),
            wide(nz - 1, 8, width),
            wide(8, width),
            wide(3, 8, width),
            dma((240,)),
            dma((240,)),
            dma((28,)),
            dma((2, 2, 2)),
            dma((2, 2, 2)),
            dma((2, 2, 2)),
            pltpu.SemaphoreType.REGULAR,
            pltpu.SemaphoreType.REGULAR,
            pltpu.SemaphoreType.REGULAR,
            pltpu.SemaphoreType.REGULAR,
        ],
        name="layer",
        cost_estimate=pl.CostEstimate(flops=45 * 10**9, bytes_accessed=20 * 10**6, transcendentals=0),
        compiler_params=pltpu.CompilerParams(
            collective_id=0, has_side_effects=True, vmem_limit_bytes=LIMIT
        ),
    )(
        lengths[:, 0], tokens, cotangent, mix_weight, out_weight, up_weight, down_weight, norms,
        feature_freq, feature_scale[None], cosine_basis(), spread_rows(),
    )
    return (
        out_rows,
        cotangent.astype(WIDE) + grad_rows.astype(WIDE),
        gmix.astype(WIDE),
        gout.astype(WIDE),
        gup.astype(WIDE),
        gdown.astype(WIDE),
        gains[0],
        gains[1],
        gains[2],
        gains[3],
    )


def solution(mesh):
    ny, nz = mesh.shape["dp"] // 2, mesh.shape["fsdp"] // 2
    grouped = ny == 2 and nz == 4 and D // mesh.size % 32 == 0
    body = partial(per_device_group, ny, nz) if grouped else per_device_plain
    rows = P(("dp", "fsdp"), None)
    vector = P(("dp", "fsdp"))
    slots = P(None, ("dp", "fsdp"), None)
    return jax.shard_map(
        body,
        mesh=mesh,
        in_specs=(slots, slots, *[rows] * 4, *[vector] * 4, P(), P(), slots),
        out_specs=(slots, slots, *[rows] * 4, *[vector] * 4),
        check_vma=False,
    )
```

```python
from functools import partial
import math

import jax
import jax.numpy as jnp
import numpy as np
from jax import lax
from jax.experimental import pallas as pl
from jax.experimental.pallas import tpu as pltpu
from jax.sharding import PartitionSpec as P

D = 1024
HEAD = 64
ROT = 16


epsilon = 1e-05
exact_precision = lax.Precision.HIGHEST


def dct_matrix(width):
    order = jnp.arange(width, dtype=jnp.float32)[:, None]
    sample = jnp.arange(width, dtype=jnp.float32)[None, :]
    factor = jnp.where(order == 0, jnp.sqrt(1.0 / width), jnp.sqrt(2.0 / width))
    return factor * jnp.cos(math.pi * (2.0 * sample + 1.0) * order / (2.0 * width))


def feature_table(feature_freq):
    table = jnp.dot(dct_matrix(HEAD).T, feature_freq.T, precision=exact_precision) / math.sqrt(HEAD)
    return table.astype(jnp.bfloat16)


def slot_layout(span_table, slot_len):
    seg_ends = jnp.cumsum(span_table, axis=-1)
    seg_starts = seg_ends - span_table
    places = jnp.arange(slot_len, dtype=jnp.int32)
    segment = jnp.sum((places[:, None] >= seg_ends[..., None, :]).astype(jnp.int32), axis=-1)
    numbers = jnp.arange(span_table.shape[-1], dtype=jnp.int32)
    matched = segment[..., None] == numbers
    begin_at = jnp.sum(jnp.where(matched, seg_starts[..., None, :], 0), axis=-1)
    begin_at = begin_at + jnp.where(segment == span_table.shape[-1], seg_ends[..., -1:], 0)
    position = (places - begin_at).astype(jnp.float32)
    valid = (segment < span_table.shape[-1]).astype(jnp.float32)
    return (segment, position, valid)


def rotate(raw_heads, position):
    half_rot = ROT // 2
    inverse = 10000.0 ** (-2.0 * jnp.arange(half_rot, dtype=jnp.float32) / ROT)
    angle = position[..., None] * inverse
    cosine_wave = jnp.cos(angle)[..., None, :]
    sine = jnp.sin(angle)[..., None, :]
    first = raw_heads[..., :half_rot]
    second = raw_heads[..., half_rot:ROT]
    return jnp.concatenate(
        [
            first * cosine_wave - second * sine,
            second * cosine_wave + first * sine,
            raw_heads[..., ROT:],
        ],
        axis=-1,
    )


def feature_map(raw_heads, position, table, feature_scale):
    rotated_rows = rotate(raw_heads, position).astype(jnp.bfloat16)
    pre = jnp.einsum("shd,df->shf", rotated_rows, table, preferred_element_type=jnp.float32)
    return feature_scale * jnp.exp(pre)


def feature_back(raw_heads, grad_phi, position, table, feature_scale):
    phi = feature_map(raw_heads, position, table, feature_scale)
    grad_pre = (grad_phi * phi).astype(jnp.bfloat16)
    grad_turned = jnp.einsum("shf,df->shd", grad_pre, table, preferred_element_type=jnp.float32)
    _, turn_pull = jax.vjp(lambda values: rotate(values, position), raw_heads)
    return turn_pull(grad_turned)[0]


def norm_apply(inputs, gain, shift):
    center = inputs - jnp.mean(inputs, axis=-1, keepdims=True)
    spread = jnp.mean(center * center, axis=-1, keepdims=True)
    return center * lax.rsqrt(spread + epsilon) * gain + shift


def head_major(values):
    return jnp.swapaxes(values, 0, 1)


def attend_head(allowed, pieces):
    mapped_query, mapped_key, value_rows = pieces
    score_matrix = jnp.einsum(
        "qf,kf->qk", mapped_query, mapped_key, preferred_element_type=jnp.float32
    )
    score_matrix = jnp.where(allowed, score_matrix, 0.0)
    totals = jnp.sum(score_matrix, axis=1)
    numerator = jnp.dot(
        score_matrix.astype(jnp.bfloat16), value_rows, preferred_element_type=jnp.float32
    )
    return numerator / totals[:, None]


def attend_back(allowed, pieces):
    mapped_query, mapped_key, value_rows, grad_heads = pieces
    score_matrix = jnp.einsum(
        "qf,kf->qk", mapped_query, mapped_key, preferred_element_type=jnp.float32
    )
    score_matrix = jnp.where(allowed, score_matrix, 0.0)
    totals = jnp.sum(score_matrix, axis=1)
    scores_low = score_matrix.astype(jnp.bfloat16)
    numerator = jnp.dot(scores_low, value_rows, preferred_element_type=jnp.float32)
    grad_numer = (grad_heads / totals[:, None]).astype(jnp.bfloat16)
    grad_totals = -jnp.sum(grad_heads * numerator, axis=1) / (totals * totals)
    grad_scores = jnp.einsum(
        "qd,kd->qk", grad_numer, value_rows, preferred_element_type=jnp.float32
    )
    grad_scores = jnp.where(allowed, grad_scores + grad_totals[:, None], 0.0).astype(jnp.bfloat16)
    grad_query = jnp.dot(grad_scores, mapped_key, preferred_element_type=jnp.float32)
    grad_key = jnp.einsum(
        "qk,qf->kf", grad_scores, mapped_query, preferred_element_type=jnp.float32
    )
    grad_value = jnp.einsum("qk,qd->kd", scores_low, grad_numer, preferred_element_type=jnp.float32)
    return (grad_query, grad_key, grad_value)


def fetch_attention(shards):
    return (
        lax.all_gather(shards[0], ("dp", "fsdp"), axis=0, tiled=True),
        lax.all_gather(shards[1], ("dp", "fsdp"), axis=0, tiled=True),
        lax.all_gather(shards[2], ("dp", "fsdp"), axis=0, tiled=True),
        lax.all_gather(shards[3], ("dp", "fsdp"), axis=0, tiled=True),
    )


def fetch_feed(shards):
    return (
        lax.all_gather(shards[0], ("dp", "fsdp"), axis=0, tiled=True),
        lax.all_gather(shards[1], ("dp", "fsdp"), axis=0, tiled=True),
        lax.all_gather(shards[2], ("dp", "fsdp"), axis=0, tiled=True),
        lax.all_gather(shards[3], ("dp", "fsdp"), axis=0, tiled=True),
    )


def reduce_attention(grads):
    return (
        lax.psum_scatter(grads[0], ("dp", "fsdp"), scatter_dimension=0, tiled=True),
        lax.psum_scatter(grads[1], ("dp", "fsdp"), scatter_dimension=0, tiled=True),
        lax.psum_scatter(grads[2], ("dp", "fsdp"), scatter_dimension=0, tiled=True),
        lax.psum_scatter(grads[3], ("dp", "fsdp"), scatter_dimension=0, tiled=True),
    )


def reduce_feed(grads):
    return (
        lax.psum_scatter(grads[0], ("dp", "fsdp"), scatter_dimension=0, tiled=True),
        lax.psum_scatter(grads[1], ("dp", "fsdp"), scatter_dimension=0, tiled=True),
        lax.psum_scatter(grads[2], ("dp", "fsdp"), scatter_dimension=0, tiled=True),
        lax.psum_scatter(grads[3], ("dp", "fsdp"), scatter_dimension=0, tiled=True),
    )


def add_tuples(running, update):
    if running is None:
        return tuple(update)
    return tuple(jax.tree.map(jnp.add, tuple(running), tuple(update)))


def per_device_plain(
    tokens,
    lengths,
    mix_weight,
    out_weight,
    up_weight,
    down_weight,
    attn_gain,
    attn_bias,
    feed_gain,
    feed_bias,
    feature_freq,
    feature_scale,
    cotangent,
):
    table = feature_table(feature_freq)
    slot_len = tokens.shape[1]
    head_count = D // HEAD
    attn_shards = (mix_weight, out_weight, attn_gain, attn_bias)
    feed_shards = (up_weight, down_weight, feed_gain, feed_bias)
    places = jnp.arange(slot_len, dtype=jnp.int32)
    output_rows = []
    grad_inputs = []
    attn_total = None
    feed_total = None
    for micro_index in range(tokens.shape[0]):
        attn_full = fetch_attention(attn_shards)
        feed_full = fetch_feed(feed_shards)
        mix_full, out_full, gain_one, bias_one = attn_full
        up_full, down_full, gain_two, bias_two = feed_full
        gain_attn = gain_one.astype(jnp.float32)
        shift_attn = bias_one.astype(jnp.float32)
        gain_feed = gain_two.astype(jnp.float32)
        shift_feed = bias_two.astype(jnp.float32)
        inputs = tokens[micro_index].astype(jnp.float32)
        segment, position, valid = slot_layout(lengths[micro_index, 0], slot_len)
        allowed = (segment[:, None] == segment[None, :]) & (places[None, :] <= places[:, None])
        normed_attn = norm_apply(inputs, gain_attn, shift_attn).astype(jnp.bfloat16)
        normed_feed = norm_apply(inputs, gain_feed, shift_feed).astype(jnp.bfloat16)
        mixed = jnp.dot(normed_attn, mix_full, preferred_element_type=jnp.float32)
        mixed = mixed.reshape(slot_len, 3, head_count, HEAD)
        query_raw = mixed[:, 0]
        key_raw = mixed[:, 1]
        value_rows = mixed[:, 2].astype(jnp.bfloat16)
        mapped_query = feature_map(query_raw, position, table, feature_scale).astype(jnp.bfloat16)
        mapped_key = feature_map(key_raw, position, table, feature_scale).astype(jnp.bfloat16)
        attended = lax.map(
            partial(attend_head, allowed),
            (head_major(mapped_query), head_major(mapped_key), head_major(value_rows)),
        )
        attended = head_major(attended).reshape(slot_len, D).astype(jnp.bfloat16)
        attn_rows = jnp.dot(attended, out_full, preferred_element_type=jnp.float32)
        hidden = jnp.dot(normed_feed, up_full, preferred_element_type=jnp.float32)
        active = jax.nn.gelu(hidden, approximate=False).astype(jnp.bfloat16)
        feed_rows = jnp.dot(active, down_full, preferred_element_type=jnp.float32)
        result = inputs + valid[:, None] * (attn_rows + feed_rows)
        output_rows.append(result.astype(jnp.bfloat16))
        attn_full = fetch_attention(attn_shards)
        feed_full = fetch_feed(feed_shards)
        mix_full, out_full, gain_one, bias_one = attn_full
        up_full, down_full, gain_two, bias_two = feed_full
        grad_rows = cotangent[micro_index]
        grad_branch = jnp.where(valid[:, None] > 0.0, grad_rows, jnp.zeros_like(grad_rows))
        grad_down = jnp.einsum("sf,sd->fd", active, grad_branch, preferred_element_type=jnp.float32)
        grad_out = jnp.einsum(
            "sd,se->de", attended, grad_branch, preferred_element_type=jnp.float32
        )
        grad_active = jnp.einsum(
            "sd,fd->sf", grad_branch, down_full, preferred_element_type=jnp.float32
        )
        _, gelu_pull = jax.vjp(partial(jax.nn.gelu, approximate=False), hidden)
        grad_hidden = gelu_pull(grad_active)[0].astype(jnp.bfloat16)
        grad_up = jnp.einsum(
            "sd,sf->df", normed_feed, grad_hidden, preferred_element_type=jnp.float32
        )
        grad_normed_feed = jnp.einsum(
            "sf,df->sd", grad_hidden, up_full, preferred_element_type=jnp.float32
        )
        grad_attended = jnp.einsum(
            "sd,ed->se", grad_branch, out_full, preferred_element_type=jnp.float32
        )
        grad_attended = grad_attended.reshape(slot_len, head_count, HEAD)
        grad_phi_q, grad_phi_k, grad_value = lax.map(
            partial(attend_back, allowed),
            (
                head_major(mapped_query),
                head_major(mapped_key),
                head_major(value_rows),
                head_major(grad_attended),
            ),
        )
        grad_query = feature_back(query_raw, head_major(grad_phi_q), position, table, feature_scale)
        grad_key = feature_back(key_raw, head_major(grad_phi_k), position, table, feature_scale)
        grad_mixed = jnp.stack([grad_query, grad_key, head_major(grad_value)], axis=1)
        grad_mixed = grad_mixed.reshape(slot_len, 3 * D).astype(jnp.bfloat16)
        grad_mix = jnp.einsum(
            "sd,se->de", normed_attn, grad_mixed, preferred_element_type=jnp.float32
        )
        grad_normed_attn = jnp.einsum(
            "se,de->sd", grad_mixed, mix_full, preferred_element_type=jnp.float32
        )
        _, attn_norm_pull = jax.vjp(norm_apply, inputs, gain_attn, shift_attn)
        grad_in_one, grad_gain_one, grad_bias_one = attn_norm_pull(grad_normed_attn)
        _, feed_norm_pull = jax.vjp(norm_apply, inputs, gain_feed, shift_feed)
        grad_in_two, grad_gain_two, grad_bias_two = feed_norm_pull(grad_normed_feed)
        grad_inputs.append(grad_rows.astype(jnp.float32) + grad_in_one + grad_in_two)
        attn_grads = (grad_mix, grad_out, grad_gain_one, grad_bias_one)
        feed_grads = (grad_up, grad_down, grad_gain_two, grad_bias_two)
        attn_grads = reduce_attention(attn_grads)
        feed_grads = reduce_feed(feed_grads)
        attn_total = add_tuples(attn_total, attn_grads)
        feed_total = add_tuples(feed_total, feed_grads)
    return (
        jnp.stack(output_rows),
        jnp.stack(grad_inputs),
        attn_total[0],
        attn_total[1],
        feed_total[0],
        feed_total[1],
        attn_total[2],
        attn_total[3],
        feed_total[2],
        feed_total[3],
    )


MESH_ID = pl.DeviceIdType.MESH
LOW = jnp.bfloat16
WIDE = jnp.float32


def here(nz):
    dp = lax.axis_index("dp")
    fs = lax.axis_index("fsdp")
    return dp // 2, dp % 2, fs // 2, fs % 2


class Places:
    def __init__(self, ny, nz):
        self.ny, self.nz = ny, nz
        self.y, self.x, self.z, self.c = here(nz)

    def at(self, y, x, z, c):
        return (y * 2 + x, z * 2 + c)

    def member(self, r):
        x = 1 - self.x if r & 2 else self.x
        c = 1 - self.c if r & 1 else self.c
        return x, c

    def member_id(self, r):
        x, c = self.member(r)
        return self.at(self.y, x, self.z, c)

    def yid(self):
        return self.at(1 - self.y, self.x, self.z, self.c)

    def zid(self, step):
        return self.at(self.y, self.x, (self.z + step) % self.nz, self.c)

    def zsrc(self, step):
        return (self.z + self.nz - step) % self.nz

    def signal(self):
        barrier = pltpu.get_barrier_semaphore()
        ids = [self.member_id(r) for r in (1, 2, 3)] + [self.yid()]
        ids += [self.zid(step) for step in range(1, self.nz)]
        for one in ids:
            pl.semaphore_signal(barrier, inc=1, device_id=one, device_id_type=MESH_ID)

    def meet(self):
        pl.semaphore_wait(pltpu.get_barrier_semaphore(), self.nz + 3)


class Copy:
    def __init__(self, describe):
        self.describe, self.sent = describe, False

    def start(self):
        self.describe().start()

    def wait_recv(self):
        self.describe().wait_recv()

    def wait_send(self):
        if not self.sent:
            self.describe().wait_send()
            self.sent = True


class Links:
    def __init__(self, send, recv):
        self.send, self.recv, self.count, self.open = send, recv, 0, []

    def plan(self, src, dst, device):
        i = self.count
        self.count += 1

        def describe():
            return pltpu.make_async_remote_copy(
                src() if callable(src) else src,
                dst() if callable(dst) else dst,
                self.send.at[i],
                self.recv.at[i],
                device_id=device() if callable(device) else device,
                device_id_type=MESH_ID,
            )

        return Copy(describe)

    def start(self, src, dst, device):
        copy = self.plan(src, dst, device)
        copy.start()
        self.open.append(copy)
        return copy

    def drain(self):
        for copy in self.open:
            copy.wait_send()


class Locals:
    def __init__(self, sems):
        self.sems, self.count = sems, 0

    def start(self, src, dst):
        copy = pltpu.make_async_copy(src, dst, self.sems.at[self.count])
        self.count += 1
        copy.start()
        return copy


class Line:
    def __init__(self, place):
        z = place.z
        self.place = place
        self.way = 1 - 2 * (z // 2)
        self.inner = (z // 2) * (3 - z) + (1 - z // 2) * z

    def off(self, end, inner):
        return self.place.z + self.way * ((1 - self.inner) * end + self.inner * inner)

    def near(self):
        return self.off(1, -1)

    def second(self):
        return self.off(2, 1)

    def third(self):
        return self.off(3, 2)

    def id(self, z):
        return self.place.at(self.place.y, self.place.x, z, self.place.c)

    def at_end(self, event):
        pl.when(self.inner == 0)(event)

    def at_inner(self, event):
        pl.when(self.inner == 1)(event)


class Spread:
    def __init__(self, links, line, block, own=None):
        z = line.place.z
        mine = own if own is not None else lambda: block(z)

        def here():
            return block(z)

        def second():
            return block(line.second())

        def third():
            return block(line.third())

        self.line = line
        self.sources = [line.near, line.second, line.third]
        self.beside = links.plan(mine, here, lambda: line.id(line.near()))
        self.across = links.plan(mine, here, lambda: line.id(line.second()))
        self.far = links.plan(mine, here, lambda: line.id(line.second()))
        self.hand_second = links.plan(second, second, lambda: line.id(line.near()))
        self.hand_third = links.plan(third, third, lambda: line.id(line.near()))

    def begin(self):
        self.beside.start()
        self.line.at_inner(self.across.start)
        self.line.at_end(self.far.start)

    def arrive_near(self, then=None):
        self.beside.wait_recv()
        if then:
            then[0].start()

    def arrive_inner(self, then=None):
        @self.line.at_inner
        def _():
            self.across.wait_recv()
            self.hand_second.start()
            if then:
                then[1].start()
            self.far.wait_recv()
            self.hand_third.start()
            if then:
                then[2].start()

    def arrive_end(self, then=None):
        @self.line.at_end
        def _():
            self.hand_second.wait_recv()
            if then:
                then[1].start()
            self.hand_third.wait_recv()
            if then:
                then[2].start()

    def drain(self):
        self.beside.wait_send()

        @self.line.at_inner
        def _():
            for copy in (self.across, self.hand_second, self.hand_third):
                copy.wait_send()

        self.line.at_end(self.far.wait_send)


class Direct:
    def __init__(self, links, line, block, own=None):
        place = line.place
        self.sources = [partial(place.zsrc, step) for step in range(1, place.nz)]
        mine = own if own is not None else lambda: block(place.z)
        self.copies = [
            links.plan(mine, lambda: block(place.z), partial(place.zid, step))
            for step in range(1, place.nz)
        ]

    def begin(self):
        for copy in self.copies:
            copy.start()

    def arrive_near(self, then=()):
        for k, copy in enumerate(self.copies):
            copy.wait_recv()
            if then:
                then[k].start()

    def arrive_inner(self, then=None):
        pass

    def arrive_end(self, then=None):
        pass

    def drain(self):
        for copy in self.copies:
            copy.wait_send()


class Gather:
    def __init__(self, links, place, line, block, own=None, way=Spread):
        def plane(z):
            return block(place.y, z)

        self.spread = way(links, line, plane, own)
        mine = own if own is not None else lambda: plane(place.z)
        self.cross = links.plan(mine, lambda: plane(place.z), place.yid)
        self.cross_on = [
            links.plan(lambda at=at: plane(at()), lambda at=at: plane(at()), place.yid)
            for at in self.spread.sources
        ]

    def begin(self):
        self.spread.begin()
        self.cross.start()

    def forward(self):
        self.spread.arrive_near(self.cross_on)
        self.spread.arrive_inner(self.cross_on)

    def late(self):
        self.spread.arrive_end(self.cross_on)

    def finish(self):
        for copy in [self.cross] + self.cross_on:
            copy.wait_recv()

    def drain(self):
        self.spread.drain()
        for copy in [self.cross] + self.cross_on:
            copy.wait_send()


class GatherCross:
    def __init__(self, links, place, line, block, own=None, way=Spread):
        def plane(z):
            return block(place.y, z)

        def other(z):
            return block(1 - place.y, z)

        mine = own if own is not None else lambda: plane(place.z)
        self.cross = links.plan(mine, lambda: plane(place.z), place.yid)
        self.spread = way(links, line, plane, own)
        self.spread_other = way(links, line, other)

    def begin(self):
        self.cross.start()
        self.spread.begin()

    def forward(self):
        self.cross.wait_recv()
        self.spread_other.begin()
        self.spread.arrive_near()
        self.spread.arrive_inner()

    def late(self):
        self.spread.arrive_end()
        self.spread_other.arrive_near()
        self.spread_other.arrive_inner()

    def finish(self):
        self.spread_other.arrive_end()

    def drain(self):
        self.cross.wait_send()
        self.spread.drain()
        self.spread_other.drain()


def dot_nn(a, b):
    return jnp.dot(a, b, preferred_element_type=WIDE)


def dot_nt(a, b):
    return lax.dot_general(a, b, (((1,), (1,)), ((), ())), preferred_element_type=WIDE)


def dot_tn(a, b):
    return lax.dot_general(a, b, (((0,), (0,)), ((), ())), preferred_element_type=WIDE)


def fold_rows(values):
    rows, cols = values.shape
    return jnp.sum(values.reshape(rows // 8, 8, cols), axis=0)


class Fold:
    def __init__(self, links, line, block, land):
        self.line, self.block, self.land = line, block, land

        def to(at, where, slot):
            return links.plan(lambda: block(at()), lambda: land(slot), lambda: line.id(where()))

        self.beside = to(line.near, line.near, 0)
        self.across = to(line.second, line.second, 1)
        self.far = to(line.second, line.second, 2)
        self.hand = to(line.third, line.near, 3)
        self.handed = to(line.third, line.third, 1)

    def send(self, k):
        if k == 0:
            self.line.at_inner(self.across.start)
            self.line.at_end(self.far.start)
        if k == 1:
            self.line.at_end(self.hand.start)
        if k == 2:
            self.beside.start()

    def hand_on(self):
        @self.line.at_inner
        def _():
            self.hand.wait_recv()
            block = self.block(self.line.third())
            block[...] = (block[...].astype(WIDE) + self.land(3)[...].astype(WIDE)).astype(LOW)
            self.handed.start()

    def total(self, own, emit):
        self.beside.wait_recv()

        @self.line.at_end
        def _():
            self.handed.wait_recv()
            emit(own() + self.land(0)[...].astype(WIDE) + self.land(1)[...].astype(WIDE))

        @self.line.at_inner
        def _():
            self.across.wait_recv()
            self.far.wait_recv()
            total = own() + self.land(0)[...].astype(WIDE) + self.land(1)[...].astype(WIDE)
            emit(total + self.land(2)[...].astype(WIDE))

    def drain(self):
        self.beside.wait_send()

        @self.line.at_inner
        def _():
            self.across.wait_send()
            self.handed.wait_send()

        @self.line.at_end
        def _():
            self.far.wait_send()
            self.hand.wait_send()


class Scatter:
    def __init__(self, links, place, line, theirs, mine, ybuf, zbuf):
        self.place, self.line, self.mine, self.ybuf = place, line, mine, ybuf
        self.order = [line.second, line.third, line.near, lambda: place.z]
        self.ys = [
            links.plan(lambda at=at: theirs(at()), lambda at=at: ybuf(at()), place.yid)
            for at in self.order
        ]
        self.fold = Fold(links, line, ybuf, zbuf)

    def begin(self):
        for copy in self.ys:
            copy.start()

    def turn(self, k):
        self.ys[k].wait_recv()
        if k < 3:
            at = self.order[k]()
            land = self.ybuf(at)
            land[...] = (land[...].astype(WIDE) + self.mine(at)[...].astype(WIDE)).astype(LOW)
        self.fold.send(k)

    def hand_on(self):
        self.fold.hand_on()

    def total(self, emit):
        z = self.place.z
        self.fold.total(
            lambda: self.ybuf(z)[...].astype(WIDE) + self.mine(z)[...].astype(WIDE), emit
        )

    def drain(self):
        for copy in self.ys:
            copy.wait_send()
        self.fold.drain()


class ScatterCross:
    def __init__(self, links, place, line, parts, zbuf, hold, land):
        self.place, self.parts, self.hold, self.land = place, parts, hold, land
        self.fold = Fold(links, line, parts, zbuf)
        self.cross = links.plan(lambda: hold.at[1 - place.y], lambda: land, place.yid)

    def begin(self):
        for k in range(3):
            self.fold.send(k)

    def hand_on(self):
        self.fold.hand_on()

    def turn(self):
        def emit(total):
            self.hold[...] = total.astype(LOW)

        self.fold.total(lambda: self.parts(self.place.z)[...].astype(WIDE), emit)
        self.cross.start()

    def total(self):
        self.cross.wait_recv()
        return self.hold[self.place.y].astype(WIDE) + self.land[...].astype(WIDE)

    def drain(self):
        self.cross.wait_send()
        self.fold.drain()


def layer_kernel(
    ny, nz,
    lens, tok, cot, mix_w, out_w, up_w, down_w, norms_in, freq_in, scale_ref, dct_in, spread_in,
    out_rows, grad_rows, gmix_out, gout_out, gup_out, gdown_out, gains_out,
    xs, gs, nf, na, act, gp, feed, gxf, gm,
    up, down, mix, outw, small, gains, meta, table, scale, norms, freq, scale_in, dct, spread,
    gdown, ydown, zdown, ymix, zmix,
    zval, hval, yval, zout, hout, yout,
    up_send, up_recv, mix_send, mix_recv, gacc, gsum, gy, g2, gz, g3, gm_sum,
    send, recv, sems, sib_sems, own_sems, far_sems, out_free, sib_free, far_free, act_free,
):
    place = Places(ny, nz)
    y, x, z, c = place.y, place.x, place.z, place.c
    me = x * 2 + c
    micro, span, width = xs.shape[1:]
    shard = out_w.shape[0]
    feed_shard = down_w.shape[0]
    half = up.shape[-1]
    quarter = half // 2
    heads = width // HEAD // 4
    group = heads * HEAD
    none = jnp.zeros((), LOW)
    local = Locals(sems)

    def raw(n):
        return feed.at[3, 0, pl.ds(n * shard, shard)]

    def raw_load(weight, first):
        count = weight.shape[1] // width
        return [
            local.start(weight.at[:, pl.ds(n * width, width)], raw(first + n)) for n in range(count)
        ]

    norms_load = local.start(norms_in, norms)
    mix_load = raw_load(mix_w, 0)
    up_load = raw_load(up_w, len(mix_load))
    out_mine = local.start(out_w, outw.at[y, z // 2, z % 2, c])
    tok_mine = local.start(tok, gp.at[0])
    cot_mine = local.start(cot, gs.at[0])
    down_mine = [
        local.start(down_w.at[:, pl.ds(k * half, half)], down.at[k, y, z]) for k in range(2)
    ]
    place.signal()
    table_loads = [
        local.start(src, dst)
        for src, dst in ((freq_in, freq), (scale_ref, scale_in), (dct_in, dct), (spread_in, spread))
    ]

    row = lax.broadcasted_iota(jnp.int32, (8, 128), 0)
    lane = lax.broadcasted_iota(jnp.int32, (8, 128), 1)
    facts = jnp.zeros((8, 128), WIDE)
    for s in range(micro):
        for k in range(lens.shape[1]):
            facts = jnp.where((row == 1 + s) & (lane == k), lens[s, k].astype(WIDE), facts)
    norms_load.wait()
    at_row = lax.broadcasted_iota(jnp.int32, (shard, 128), 0)
    at_lane = lax.broadcasted_iota(jnp.int32, (shard, 128), 1)
    for k in range(4):
        pick = jnp.where(at_lane == at_row + k * shard, 1.0, 0.0).astype(LOW)
        facts = jnp.where(row == 0, facts + dot_nn(norms[k : k + 1, :], pick), facts)
    small[y, x, z, c] = facts

    def up_stage(q):
        return gdown.at[:, q, pl.ds(0, shard), pl.ds(0, half)]

    def mix_stage(t, q):
        return gdown.at[0, q, pl.ds((t + 1) * shard, shard), pl.ds(half, group)]

    def raw_cols(base, first, count):
        at = first % width
        return raw(base + first // width)[:, at : at + count]

    for copy in mix_load:
        copy.wait()
    pair = group // ny
    for q in range(4):
        for t in range(3):
            for by in range(ny):
                first = t * width + ((by * 2 + q // 2) * 2 + q % 2) * pair
                mix_stage(t, q)[:, by * pair : (by + 1) * pair] = raw_cols(0, first, pair)
    for t in range(3):
        mix[t, y, x, z, c] = mix_stage(t, me)[...]
    place.meet()
    links = Links(send, recv)
    line = Line(place)

    def swap(src, dst):
        copies = []
        for r in (1, 2, 3):
            mx, mc = place.member(r)
            copies.append(links.start(src(mx * 2 + mc), dst, place.member_id(r)))
        return copies

    def landed(copies):
        for copy in copies:
            copy.wait_recv()

    small_swaps = swap(lambda q: small.at[y, x, z, c], small.at[y, x, z, c])
    mix_swaps = []
    for t in range(3):
        mix_swaps += swap(lambda q, t=t: mix_stage(t, q), mix.at[t, y, x, z, c])
    for copy in up_load:
        copy.wait()
    for q in range(4):
        for by in range(ny):
            for bz in range(nz):
                first = (((by * 2 + q // 2) * nz + bz) * 2 + q % 2) * feed_shard
                cols = slice(bz * feed_shard, (bz + 1) * feed_shard)
                up_stage(q)[by, :, cols] = raw_cols(len(mix_load), first, feed_shard)
    up[:, y, x, z, c] = up_stage(me)[...]
    up_swaps = swap(up_stage, up.at[:, y, x, z, c])
    chunks = [GatherCross(links, place, line, lambda by, bz: outw.at[by, bz // 2, bz % 2, c])]
    for t in range(3):
        chunks.append(Gather(links, place, line, lambda by, bz, t=t: mix.at[t, by, :, bz]))
    halves = [(k, pl.ds(h * quarter, quarter)) for k in range(2) for h in range(2)]
    for k, cols in halves:
        chunks.append(
            Gather(
                links, place, line,
                lambda by, bz, k=k, cols=cols: up.at[k, by, :, bz, :, :, cols],
            )
        )
    for k, cols in halves:
        way = GatherCross if (k, cols) == halves[-1] else Gather
        chunks.append(
            way(links, place, line, lambda by, bz, k=k, cols=cols: down.at[k, by, bz, :, cols])
        )
    of_mix, of_up, of_down = range(1, 4), range(4, 8), range(8, 12)
    ahead = 3
    hurried = [3]

    def turn_chunk(i):
        chunks[i].forward()
        if i and i - 1 not in hurried:
            chunks[i - 1].late()
        if i + ahead < len(chunks):
            chunks[i + ahead].begin()

    small_gather = Gather(links, place, line, lambda by, bz: small.at[by, :, bz])
    tok_sib = links.plan(gp.at[0], gp.at[1], partial(place.member_id, 1))
    tok_far = links.plan(gp.at[0], gp.at[2], partial(place.member_id, 2))
    cot_sib = links.plan(gs.at[0], gs.at[1], partial(place.member_id, 1))
    cot_far = links.plan(gs.at[0], gs.at[2], partial(place.member_id, 2))

    def send_tokens():
        tok_mine.wait()
        tok_sib.start()
        tok_far.start()

    def send_cot():
        cot_mine.wait()
        at_place = lax.broadcasted_iota(jnp.int32, (span, 1), 0)
        for s in range(micro):
            used = lens[s, 0]
            for k in range(1, lens.shape[1]):
                used = used + lens[s, k]
            gs[0, s] = jnp.where(at_place < used, gs[0, s], none)
        cot_sib.start()
        cot_far.start()

    def make_table():
        for copy in table_loads:
            copy.wait()
        raw = lax.dot_general(
            dct[...], freq[...], (((0,), (1,)), ((), ())),
            precision=lax.Precision.HIGHEST, preferred_element_type=WIDE,
        ) / math.sqrt(HEAD)
        raw = raw.astype(LOW)
        tile_row = lax.broadcasted_iota(jnp.int32, (HEAD, group), 0)
        tile_col = lax.broadcasted_iota(jnp.int32, (HEAD, group), 1)
        tiled = jnp.where(tile_col % HEAD == tile_row, 1.0, 0.0).astype(LOW)
        wide_table = dot_tn(tiled, dot_nn(raw, tiled).astype(LOW))
        block_row = lax.broadcasted_iota(jnp.int32, (group, group), 0) // HEAD
        block_col = lax.broadcasted_iota(jnp.int32, (group, group), 1) // HEAD
        table[...] = jnp.where(block_row == block_col, wide_table, 0.0).astype(LOW)
        scale[...] = lax.dot_general(
            jnp.broadcast_to(scale_in[...], (8, HEAD)), tiled.astype(WIDE), (((1,), (0,)), ((), ())),
            precision=lax.Precision.HIGHEST, preferred_element_type=WIDE,
        )

    def make_gains():
        count = ny * 2 * nz * 2
        packed = jnp.sum(jnp.where(row == 0, small[...].reshape(count, 8, 128), 0.0), axis=1)
        packed = packed.astype(LOW)
        pick_row = lax.broadcasted_iota(jnp.int32, (128, width), 0)
        pick_col = lax.broadcasted_iota(jnp.int32, (128, width), 1) % shard
        owner = lax.broadcasted_iota(jnp.int32, (count, width), 0)
        owned = lax.broadcasted_iota(jnp.int32, (count, width), 1) // shard
        for k in range(4):
            pick = jnp.where(pick_row == pick_col + k * shard, 1.0, 0.0).astype(LOW)
            part = jnp.where(owned == owner, dot_nn(packed, pick), 0.0)
            gains[k : k + 1, :] = jnp.sum(part, axis=0, keepdims=True)
        gacc[...] = jnp.zeros_like(gacc)

    def make_turns():
        places = lax.broadcasted_iota(jnp.int32, (1, span), 1).astype(WIDE)
        turn_row = lax.broadcasted_iota(jnp.int32, (ROT // 2, 1), 0)
        inverse = jnp.zeros((ROT // 2, 1), WIDE)
        for k in range(ROT // 2):
            inverse = jnp.where(turn_row == k, 10000.0 ** (-2.0 * k / ROT), inverse)
        fact_row = lax.broadcasted_iota(jnp.int32, (8, span), 0)
        for r in range(4):
            mx, mc = place.member(r)
            facts = small[y, mx, z, mc]
            for s in range(micro):
                end = jnp.zeros((1, 1), WIDE)
                segment = jnp.zeros((1, span), WIDE)
                begin = jnp.zeros((1, span), WIDE)
                for k in range(lens.shape[1]):
                    end = end + facts[1 + s : 2 + s, k : k + 1]
                    past = places >= end
                    segment = segment + jnp.where(past, 1.0, 0.0)
                    begin = jnp.where(past, end, begin)
                angle = inverse * (places - begin)
                valid = jnp.where(segment < lens.shape[1], 1.0, 0.0)
                rest = jnp.where(fact_row == 0, segment, jnp.where(fact_row == 1, 1.0, 0.0))
                rest = jnp.where(fact_row == 2, valid, rest)
                left = jnp.concatenate([jnp.cos(angle), jnp.sin(angle)], axis=0)
                for first in (0, 24, 40):
                    part = left.astype(LOW)
                    left = left - part.astype(WIDE)
                    meta[r, s, first : first + 16, :] = part
                meta[r, s, 16:24, :] = rest.astype(LOW)
                meta[r, s, 56:64, :] = jnp.zeros((8, span), LOW)

    def norm(j):
        def body(i, carry):
            s = i // (span // 128)
            rs = pl.ds(pl.multiple_of(i % (span // 128) * 128, 128), 128)
            values = gp[j, s, rs, :].astype(WIDE)
            center = values - jnp.mean(values, axis=1, keepdims=True)
            deviation = jnp.mean(center * center, axis=1, keepdims=True)
            hat = center * lax.rsqrt(deviation + epsilon)
            na[j, s, rs, :] = (hat * gains[0:1, :] + gains[1:2, :]).astype(LOW)
            nf[j, s, rs, :] = (hat * gains[2:3, :] + gains[3:4, :]).astype(LOW)
            xs[j, s, rs, :] = hat.astype(LOW)
            return carry

        lax.fori_loop(0, micro * span // 128, body, 0)

    def loop(first, last, body, events):
        def step(i, carry):
            def pump(part):
                for (at, which), event in events.items():
                    if which == part:

                        @pl.when(i == at)
                        def _(event=event):
                            event()

            body(i, pump)
            return carry

        lax.fori_loop(first, last, step, 0)

    head_lane = lax.broadcasted_iota(jnp.int32, (1, group), 1)
    of_head = [head_lane // HEAD == h for h in range(heads)]
    low_lane = lax.broadcasted_iota(jnp.int32, (1, 128), 1) % HEAD < ROT // 2
    key_at = lax.broadcasted_iota(jnp.int32, (span, span), 1)
    query_at = lax.broadcasted_iota(jnp.int32, (span, span), 0)
    wide_mix = 3 * group

    def turn(values, cosine, sine):
        parts = []
        for first in range(0, group, 128):
            part = values[:, first : first + 128]
            other = jnp.where(
                low_lane, pltpu.roll(part, 128 - ROT // 2, 1), pltpu.roll(part, ROT // 2, 1)
            )
            parts.append(part * cosine + other * sine)
        return jnp.concatenate(parts, axis=1)

    def spread_meta(j, s, first, last):
        return dot_tn(meta[j, s], spread[:, first:last])

    def attend_forward(j, s):
        rows = na[j, s]
        turns = spread_meta(j, s, 0, 384)
        cosine, sine, owner = turns[:, :128], turns[:, 128:256], turns[:, 256:384]
        owner = jnp.concatenate([owner, owner], axis=1)
        allowed = (owner == meta[j, s, 16:24, :][0:1, :].astype(WIDE)) & (key_at <= query_at)
        query, key, value = (dot_nn(rows, mix[t].reshape(width, group)) for t in range(3))
        query = turn(query, cosine, sine).astype(LOW)
        key = turn(key, cosine, sine).astype(LOW)
        value = value.astype(LOW)
        raised_query = scale[0:1, :] * jnp.exp(dot_nn(query, table[...]))
        raised_key = scale[0:1, :] * jnp.exp(dot_nn(key, table[...]))
        phi_query = raised_query.astype(LOW)
        phi_key = raised_key.astype(LOW)
        scores, totals = [], []
        numer = jnp.zeros((span, group), WIDE)
        total = jnp.zeros((span, group), WIDE)
        for h in range(heads):
            score = dot_nt(jnp.where(of_head[h], phi_query, none), phi_key)
            score = jnp.where(allowed, score, 0.0)
            totals.append(jnp.sum(score, axis=1, keepdims=True))
            scores.append(score.astype(LOW))
            numer += dot_nn(scores[h], jnp.where(of_head[h], value, none))
            total = jnp.where(of_head[h], totals[h], total)
        att = (numer / total).astype(LOW)
        gm[j, s, :, wide_mix:] = att
        return (att, cosine, sine, allowed, raised_query, raised_key, phi_query, phi_key, value,
                scores, totals, numer, total)

    def attend_back(j, s, kept):
        (att, cosine, sine, allowed, raised_query, raised_key, phi_query, phi_key, value,
         scores, totals, numer, total) = kept
        feed[j, s] = dot_nn(att, outw[:, c].reshape(group, width)).astype(LOW)
        grad_att = dot_nt(gs[j, s], outw[:, c].reshape(group, width))
        grad_numer = (grad_att / total).astype(LOW)
        product = grad_att * numer
        grad_query = jnp.zeros((span, group), WIDE)
        grad_key = jnp.zeros((span, group), WIDE)
        grad_value = jnp.zeros((span, group), WIDE)
        for h in range(heads):
            grad_total = -jnp.sum(jnp.where(of_head[h], product, 0.0), axis=1, keepdims=True)
            grad_total = grad_total / (totals[h] * totals[h])
            numer_h = jnp.where(of_head[h], grad_numer, none)
            grad_score = dot_nt(numer_h, value) + grad_total
            grad_score = jnp.where(allowed, grad_score, 0.0).astype(LOW)
            grad_query += dot_nn(grad_score, jnp.where(of_head[h], phi_key, none))
            grad_key += dot_tn(grad_score, jnp.where(of_head[h], phi_query, none))
            grad_value += dot_tn(scores[h], numer_h)
        back_query = turn(
            dot_nt((grad_query * raised_query).astype(LOW), table[...]), cosine, -sine
        )
        back_key = turn(dot_nt((grad_key * raised_key).astype(LOW), table[...]), cosine, -sine)
        parts = (back_query.astype(LOW), back_key.astype(LOW), grad_value.astype(LOW))
        grad_normed = jnp.zeros((span, width), WIDE)
        for t in range(3):
            gm[j, s, :, t * group : (t + 1) * group] = parts[t]
            grad_normed += dot_nt(parts[t], mix[t].reshape(width, group))
        gacc[0:8, :] += fold_rows(grad_normed * xs[j, s].astype(WIDE))
        gacc[8:16, :] += fold_rows(grad_normed)
        gxf[j, s] = (grad_normed * gains[0:1, :]).astype(LOW)

    def attend(j, pump):
        kept = []
        for s in range(micro):
            kept.append(attend_forward(j, s))
            pump(s)
        for s in range(micro):
            attend_back(j, s, kept[s])
            pump(micro + s)

    def hidden(k):
        def body(i, pump):
            j, s = i // micro, i % micro
            pump(0)
            h = dot_nn(nf[j, s], up[k].reshape(width, half))
            cdf = 0.5 * (1.0 + lax.erf(h * math.sqrt(0.5)))
            pdf = jnp.exp(-0.5 * h * h) * (1.0 / math.sqrt(2.0 * math.pi))
            act[j, s, :, pl.ds(k * half, half)] = (h * cdf).astype(LOW)
            gp[j, s, :, pl.ds(k * half, half)] = (cdf + h * pdf).astype(LOW)

        return body

    rest = 4 * micro * span
    blocks = width // 256

    def other_first(i):
        return (i + (1 - y) * (blocks // 2)) % blocks

    def outer(a, b, first, last, store):
        def body(i, carry):
            at = other_first(i)
            cols = pl.ds(pl.multiple_of(at * 256, 256), 256)
            store(at, dot_tn(a[:, :, :, cols].reshape(rest, 256), b().reshape(rest, -1)))
            return carry

        lax.fori_loop(first, last, body, 0)

    def keep_down(at, part):
        per = 256 // feed_shard
        for k in range(per):
            block = at * per + k
            rows = slice(k * feed_shard, (k + 1) * feed_shard)
            gdown[block // nz, block % nz] = part[rows].astype(LOW)

    def keep_up(at, part):
        na[2 + at // 2, at % 2] = part.astype(LOW)

    def up_block(ref, j, at, cols):
        size = 2 * shard
        return ref.at[j, :, pl.ds(pl.multiple_of(at * size, size), size), cols]

    def keep_mix(at, part):
        for t in range(3):
            cols = part[:, t * group : (t + 1) * group].astype(LOW)
            mix[t, at // 2, at % 2] = cols.reshape(nz, 2, shard, group)

    def outer_down(first, last):
        outer(act, lambda: gs[...], first, last, keep_down)

    def outer_up(first, last):
        outer(nf, lambda: gp[...], first, last, keep_up)

    def outer_mix(first, last):
        outer(na, lambda: gm[:, :, :, 0:wide_mix], first, last, keep_mix)

    down_sum = Scatter(
        links, place, line, lambda at: gdown.at[1 - y, at], lambda at: gdown.at[y, at],
        lambda at: ydown.at[at], lambda k: zdown.at[k],
    )
    up_sums = []
    for k in range(2):
        cols = pl.ds(k * half, half)
        up_sums.append(
            Scatter(
                links, place, line,
                lambda at, cols=cols: up_block(na, 3 - y, at, cols),
                lambda at, cols=cols: up_block(na, 2 + y, at, cols),
                lambda at, cols=cols: up_block(act, 2, at, cols),
                lambda at, cols=cols: up_block(act, 3, at, cols),
            )
        )
    two = pl.ds(0, 2)
    mix_sum = Scatter(
        links, place, line, lambda at: mix.at[two, 1 - y, :, at],
        lambda at: mix.at[two, y, :, at], lambda at: ymix.at[at], lambda k: zmix.at[k],
    )
    val_sum = ScatterCross(
        links, place, line, lambda at: mix.at[2, :, :, at], lambda k: zval.at[k], hval, yval
    )
    out_sum = ScatterCross(
        links, place, line, lambda at: outw.at[:, at // 2, at % 2, c], lambda k: zout.at[k],
        hout, yout,
    )

    out_here = outw.at[:, 1 - c, :, c]
    out_swap = links.plan(out_here, out_here, partial(place.member_id, 1))
    landed(small_swaps)
    small_gather.begin()
    out_mine.wait()
    chunks[0].begin()
    send_tokens()
    landed(mix_swaps[0:3])
    chunks[1].begin()
    landed(mix_swaps[3:6])
    chunks[2].begin()
    send_cot()
    small_gather.forward()
    small_gather.late()
    landed(mix_swaps[6:9])
    chunks[0].forward()
    chunks[3].begin()
    chunks[1].forward()
    landed(up_swaps)
    make_table()
    small_gather.finish()
    make_gains()
    make_turns()
    chunks[0].late()
    chunks[2].forward()
    landed([tok_sib])
    norm(1)
    chunks[1].late()
    chunks[3].forward()
    chunks[4].begin()
    chunks[0].finish()
    chunks[5].begin()
    out_swap.start()
    chunks[2].late()
    out_swap.wait_recv()
    landed([cot_sib])
    chunks[1].finish()
    norm(0)
    for copy in down_mine:
        copy.wait()
    chunks[3].late()
    chunks[2].finish()
    chunks[3].finish()
    chunks[6].begin()
    tok_fwd = links.plan(gp.at[2], gp.at[3], partial(place.member_id, 1))

    def take_tokens():
        tok_far.wait_recv()
        tok_fwd.start()

    loop(
        0, 2, attend,
        {
            (0, 0): lambda: turn_chunk(4),
            (0, 1): take_tokens,
            (0, 2): lambda: turn_chunk(5),
            (1, 0): lambda: turn_chunk(6),
            (1, 2): lambda: turn_chunk(7),
        },
    )
    norm(2)
    landed([tok_fwd])
    norm(3)
    for copy in (tok_sib, tok_far, tok_fwd):
        copy.wait_send()
    for i in of_up[:2]:
        chunks[i].finish()
    loop(0, 4 * micro, hidden(0), {})
    turn_chunk(8)
    cot_fwd = links.plan(gs.at[2], gs.at[3], partial(place.member_id, 1))

    def take_cot():
        cot_far.wait_recv()
        cot_fwd.start()

    for copy in mix_swaps + up_swaps:
        copy.wait_send()

    chunks[0].drain()
    out_swap.wait_send()
    pl.semaphore_signal(out_free, inc=1, device_id=place.member_id(1), device_id_type=MESH_ID)

    loop(
        2, 4, attend,
        {
            (2, 0): lambda: turn_chunk(9),
            (2, 1): take_cot,
            (2, 2): lambda: turn_chunk(10),
            (3, 0): lambda: turn_chunk(11),
            (3, 1): cot_fwd.wait_recv,
            (3, 2): chunks[11].late,
        },
    )
    for i in of_mix:
        chunks[i].drain()
    outer_mix(0, blocks // 2)
    mix_sum.begin()
    outer_mix(blocks // 2, blocks)
    val_sum.begin()
    part = dot_tn(gm[:, :, :, wide_mix:].reshape(rest, group), gs[...].reshape(rest, width))
    outw[:, c] = part.astype(LOW).reshape(ny, 2, 2, shard, width)
    pl.semaphore_wait(out_free, 1)
    of_sibling = outw.at[:, c, :, 1 - c]
    grad_swap = links.start(of_sibling, of_sibling, place.member_id(1))
    for sem, r in ((sib_free, 1), (far_free, 2)):
        pl.semaphore_signal(sem, inc=1, device_id=place.member_id(r), device_id_type=MESH_ID)
    for i in of_up[2:]:
        chunks[i].finish()
    loop(0, 4 * micro, hidden(1), {})
    landed([grad_swap])
    out_sum.begin()
    val_sum.hand_on()
    outer_down(0, blocks // 2)
    down_sum.begin()
    mix_sum.turn(0)
    for i in of_down:
        chunks[i].finish()
    for sem in (sib_free, far_free):
        pl.semaphore_wait(sem, 1)

    def rows_copy(sem, j, r, land):
        def copy(s, kind):
            buf = (feed, gxf)[kind]
            return pltpu.make_async_remote_copy(
                buf.at[j, s], land(kind, s), sem.at[0, kind, s], sem.at[1, kind, s],
                device_id=place.member_id(r), device_id_type=MESH_ID,
            )

        return copy

    sib_copy = rows_copy(sib_sems, 3, 1, lambda kind, s: gm.at[2 + kind, s])
    far_copy = rows_copy(far_sems, 2, 2, lambda kind, s: na.at[kind, s])
    own_copy = rows_copy(own_sems, 1, 1, lambda kind, s: gm.at[kind, s])

    def hand_on(j, s, value, kind):
        buf = (feed, gxf)[kind]

        @pl.when(j != 2)
        def _():
            buf[j, s] = value.astype(LOW)

        @pl.when(j == 3)
        def _():
            sib_copy(s, kind).start()

        @pl.when(j == 2)
        def _():
            sib_copy(s, kind).wait_recv()
            buf[j, s] = (value + gm[2 + kind, s].astype(WIDE)).astype(LOW)
            far_copy(s, kind).start()

        @pl.when(j == 1)
        def _():
            own_copy(s, kind).start()

    def grad_hidden(j, s):
        ga = dot_nt(gs[j, s, :, 0:half], down[0].reshape(2 * half, half))
        ga += dot_nt(gs[j, s, :, half : 2 * half], down[1].reshape(2 * half, half))
        gp[j, s] = (ga * gp[j, s].astype(WIDE)).astype(LOW)

    def rows_out_of(j, s):
        rows = act[j, s]
        sums = [dot_nn(rows, down[k].reshape(2 * half, half)) for k in range(2)]
        hand_on(j, s, jnp.concatenate(sums, axis=1) + feed[j, s].astype(WIDE), 0)

    def rows_back(j, s):
        gh = gp[j, s]
        gn = dot_nt(gh[:, :half], up[0].reshape(width, half))
        gn += dot_nt(gh[:, half:], up[1].reshape(width, half))
        gacc[16:24, :] += fold_rows(gn * xs[j, s].astype(WIDE))
        gacc[24:32, :] += fold_rows(gn)
        hand_on(j, s, gn * gains[2:3, :] + gxf[j, s].astype(WIDE), 1)

    def back_far(i, pump):
        j, s = 3 - i % 2, i // 2
        pump(0)
        rows_out_of(j, s)
        grad_hidden(j, s)
        rows_back(j, s)

    def back_own(i, pump):
        pump(0)
        grad_hidden(i // micro, i % micro)

    def rows_own(i, pump):
        j, s = 1 - i // micro, i % micro
        pump(0)
        rows_out_of(j, s)
        rows_back(j, s)

    loop(
        0, 2 * micro, back_far,
        {
            (0, 0): lambda: out_sum.hand_on(),
            (1, 0): lambda: mix_sum.turn(1),
            (2, 0): lambda: (mix_sum.turn(2), outer_down(blocks // 2, blocks)),
            (3, 0): lambda: mix_sum.turn(3),
        },
    )
    for one in [place.yid()] + [place.zid(step) for step in range(1, nz)]:
        pl.semaphore_signal(act_free, inc=1, device_id=one, device_id_type=MESH_ID)
    loop(
        0, 2 * micro, back_own,
        {
            (0, 0): lambda: down_sum.turn(0),
            (1, 0): lambda: (val_sum.turn(), out_sum.turn()),
            (2, 0): lambda: (down_sum.turn(1), mix_sum.hand_on()),
        },
    )
    outer_up(0, blocks // 2)
    pl.semaphore_wait(act_free, nz)
    first_up, second_up = up_sums
    first_up.begin()
    outer_up(blocks // 2, blocks)
    loop(
        0, 2 * micro, rows_own,
        {
            (0, 0): lambda: down_sum.turn(2),
            (1, 0): lambda: down_sum.turn(3),
            (2, 0): lambda: first_up.turn(0),
            (3, 0): lambda: (first_up.turn(1), down_sum.hand_on()),
        },
    )
    links.drain()
    gsum[...] = jnp.zeros_like(gsum)
    for k in range(4):
        gsum[k : k + 1, :] = jnp.sum(gacc[8 * k : 8 * k + 8, :], axis=0, keepdims=True)
    gain_y = links.start(gsum, gy, place.yid())
    second_up.begin()
    own_again = local.start(tok, xs.at[0])

    def finish(s, carry):
        for kind in (0, 1):
            own_copy(s, kind).wait_recv()
            far_copy(s, kind).wait_recv()
        keep = spread_meta(0, s, 384, 512)[:, :1]
        values = xs[0, s].astype(WIDE)
        added = feed[0, s].astype(WIDE) + gm[0, s].astype(WIDE) + na[0, s].astype(WIDE)
        feed[0, s] = (values + keep * added).astype(LOW)
        grad = gxf[0, s].astype(WIDE) + gm[1, s].astype(WIDE) + na[1, s].astype(WIDE)
        center = values - jnp.mean(values, axis=1, keepdims=True)
        rate = lax.rsqrt(jnp.mean(center * center, axis=1, keepdims=True) + epsilon)
        hat = center * rate
        inner = jnp.mean(grad * hat, axis=1, keepdims=True)
        grad = grad - jnp.mean(grad, axis=1, keepdims=True) - hat * inner
        gxf[0, s] = (rate * grad).astype(LOW)
        return carry

    def put_up(k, qx, qc, values):
        rows = pl.ds(pl.multiple_of((k * 2 + qx) * shard, shard), shard)
        for bz in range(nz):
            first = (bz * 2 + qc) * feed_shard
            cols = pl.ds(pl.multiple_of(first, feed_shard), feed_shard)
            nf[0, 0, rows, cols] = values[:, bz * feed_shard : (bz + 1) * feed_shard]

    def put_mix(qx, qc, values):
        for t in range(3):
            for by in range(ny):
                first = ((by * 2 + qx) * 2 + qc) * pair
                cols = pl.ds(pl.multiple_of(first, pair), pair)
                nf[0, 1, t * shard : (t + 1) * shard, cols] = values[t, :, by * pair : (by + 1) * pair]

    def put_out(first, dst):
        count = dst.shape[1] // width
        return [
            local.start(nf.at[0, first, pl.ds(n * shard, shard)], dst.at[:, pl.ds(n * width, width)])
            for n in range(count)
        ]

    def share(hold, at, land):
        copies = []
        for r in (1, 2, 3):
            mx, mc = place.member(r)
            copies.append(links.start(at(hold, mx, mc), land.at[r - 1], place.member_id(r)))
        return copies

    def of_mix_share(hold, mx, mc):
        return hold.at[:, mx, mc]

    def of_up_share(hold, mx, mc):
        return hold.at[mx, pl.ds(pl.multiple_of(mc * shard, shard), shard)]

    def collect(copies, hold, at, land, put):
        put(x, c, at(hold, x, c)[...])
        for r in (1, 2, 3):
            mx, mc = place.member(r)
            copies[r - 1].wait_recv()
            put(mx, mc, land.at[r - 1][...])

    def keep_sum(hold):
        def emit(total):
            hold[...] = total.astype(LOW)

        return emit

    first_up.turn(2)
    mix_sum.total(keep_sum(mix_send.at[two]))
    mix_send[2] = val_sum.total().astype(LOW)
    mix_shares = share(mix_send, of_mix_share, mix_recv)
    nf[1, 1, 0:shard, :] = out_sum.total().astype(LOW)
    written = [local.start(nf.at[1, 1, pl.ds(0, shard)], gout_out)]
    first_up.turn(3)
    landed([gain_y])
    g2[...] = gsum[...] + gy[...]
    gain_zs = [links.start(g2, gz.at[step - 1], place.zid(step)) for step in range(1, nz)]
    for one in chunks + [small_gather]:
        one.drain()
    second_up.turn(0)
    second_up.turn(1)
    first_up.hand_on()
    for one in (mix_sum, val_sum, out_sum):
        one.drain()
    second_up.turn(2)
    second_up.turn(3)
    second_up.hand_on()
    down_sum.total(keep_sum(nf.at[1, 0, pl.ds(0, feed_shard)]))
    written.append(local.start(nf.at[1, 0, pl.ds(0, feed_shard)], gdown_out))
    first_up.total(keep_sum(up_send.at[0]))
    up_shares = [share(up_send.at[0], of_up_share, up_recv.at[0])]
    landed(gain_zs)
    g3[...] = g2[...] + sum(gz[step - 1] for step in range(1, nz))
    gain_ms = [links.start(g3, gm_sum.at[r - 1], place.member_id(r)) for r in (1, 2, 3)]
    own_again.wait()
    lax.fori_loop(0, micro, finish, 0)
    rows_out = local.start(feed.at[0], out_rows)
    grads_out = local.start(gxf.at[0], grad_rows)
    second_up.total(keep_sum(up_send.at[1]))
    up_shares.append(share(up_send.at[1], of_up_share, up_recv.at[1]))
    collect(mix_shares, mix_send, of_mix_share, mix_recv, put_mix)
    written += put_out(1, gmix_out)
    collect(up_shares[0], up_send.at[0], of_up_share, up_recv.at[0], partial(put_up, 0))
    down_sum.drain()
    first_up.drain()
    landed(gain_ms)
    totals = g3[...] + gm_sum[0] + gm_sum[1] + gm_sum[2]
    mine = ((y * 2 + x) * nz + z) * 2 + c
    pick_row = lax.broadcasted_iota(jnp.int32, (width, shard), 0) - mine * shard
    pick_col = lax.broadcasted_iota(jnp.int32, (width, shard), 1)
    gains_out[...] = lax.dot_general(
        totals, jnp.where(pick_row == pick_col, 1.0, 0.0), (((1,), (0,)), ((), ())),
        precision=lax.Precision.HIGHEST, preferred_element_type=WIDE,
    )
    collect(up_shares[1], up_send.at[1], of_up_share, up_recv.at[1], partial(put_up, 1))
    written += put_out(0, gup_out)
    for copy in written + [rows_out, grads_out]:
        copy.wait()
    for copy in (cot_sib, cot_far, cot_fwd):
        copy.wait_send()
    links.drain()
    second_up.drain()
    for kind in (0, 1):
        for s in range(micro):
            sib_copy(s, kind).wait_send()
            far_copy(s, kind).wait_send()
            own_copy(s, kind).wait_send()


VMEM = pl.BlockSpec(memory_space=pltpu.VMEM)
SMEM = pl.BlockSpec(memory_space=pltpu.SMEM)
ANY = pl.BlockSpec(memory_space=pl.ANY)
SHAPE = jax.ShapeDtypeStruct
LIMIT = 59 * 2**20


def cosine_basis():
    order, sample = np.arange(HEAD)[:, None], np.arange(HEAD)[None, :]
    factor = np.where(order == 0, math.sqrt(1.0 / HEAD), math.sqrt(2.0 / HEAD))
    return (factor * np.cos(math.pi * (2 * sample + 1) * order / (2 * HEAD))).astype(np.float32)


def spread_rows():
    row = np.arange(64)[:, None]
    turn = np.where(row < 16, row, np.where((row >= 24) & (row < 56), (row - 24) % 16, -1))
    lane = np.arange(512)[None, :]
    part, dim = lane // 128, lane % HEAD
    half = ROT // 2
    cosine = (part == 0) & (dim < ROT) & (turn == dim % half)
    cosine = cosine | ((part == 0) & (dim >= ROT) & (row == 17))
    sine = (part == 1) & (dim < ROT) & (turn == half + dim % half)
    rest = ((part == 2) & (row == 16)) | ((part == 3) & (row == 18))
    sign = np.where((part == 1) & (dim < half), -1.0, 1.0)
    return np.where(cosine | sine | rest, sign, 0.0).astype(jnp.bfloat16)


def widen_kernel(
    rows, grads, cot, gains, mix, out, up, down,
    rows_out, grads_out, gain_one, bias_one, gain_two, bias_two, mix_out, out_out, up_out, down_out,
    rows_low, grads_low, cot_low, grads_wide, mix_low, mix_wide, out_low, out_wide,
    up_low, up_wide, down_low, down_wide, loaded, stored,
):
    parts = [(s, h) for s in range(rows.shape[0]) for h in range(2)]
    half = rows.shape[1] // 2
    weights = [
        (mix, mix_low, mix_wide, mix_out),
        (up, up_low, up_wide, up_out),
        (down, down_low, down_wide, down_out),
        (out, out_low, out_wide, out_out),
    ]
    copies = Locals(loaded)
    stores = Locals(stored)
    loads, written = [], []
    for s, h in parts:
        at = pl.ds(h * half, half)
        loads.append(
            (
                copies.start(grads.at[s, at], grads_low.at[s, at]),
                copies.start(cot.at[s, at], cot_low.at[s, at]),
            )
        )
    weight_loads = [copies.start(src, low) for src, low, _, _ in weights]
    row_loads = [copies.start(rows.at[s], rows_low.at[s]) for s in range(rows.shape[0])]
    for k, ref in enumerate((gain_one, bias_one, gain_two, bias_two)):
        ref[...] = gains[k : k + 1, :]
    for (s, h), pair in zip(parts, loads):
        for copy in pair:
            copy.wait()
        at = pl.ds(h * half, half)
        grads_wide[s, at] = cot_low[s, at].astype(WIDE) + grads_low[s, at].astype(WIDE)
        written.append(stores.start(grads_wide.at[s, at], grads_out.at[s, at]))
    for load, (_, low, wide, dst) in zip(weight_loads, weights):
        load.wait()
        wide[...] = low[...].astype(WIDE)
        written.append(stores.start(wide, dst))
    for s, load in enumerate(row_loads):
        load.wait()
        written.append(stores.start(rows_low.at[s], rows_out.at[s]))
    for copy in written:
        copy.wait()


def per_device_group(
    ny,
    nz,
    tokens,
    lengths,
    mix_weight,
    out_weight,
    up_weight,
    down_weight,
    attn_gain,
    attn_bias,
    feed_gain,
    feed_bias,
    feature_freq,
    feature_scale,
    cotangent,
):
    micro, span, width = tokens.shape
    shard = mix_weight.shape[0]
    feed_shard = down_weight.shape[0]
    group = width // 4
    hidden = feed_shard * ny * nz
    half = hidden // 2
    norms = jnp.stack([attn_gain, attn_bias, feed_gain, feed_bias])

    dma = pltpu.SemaphoreType.DMA
    whole = pltpu.VMEM((4, micro, span, width), LOW)

    def low(*shape):
        return pltpu.VMEM(shape, LOW)

    def wide(*shape):
        return pltpu.VMEM(shape, WIDE)

    out_rows, grad_rows, gmix, gout, gup, gdown, gains = pl.pallas_call(
        partial(layer_kernel, ny, nz),
        out_shape=[
            SHAPE((micro, span, width), LOW),
            SHAPE((micro, span, width), LOW),
            SHAPE(mix_weight.shape, LOW),
            SHAPE(out_weight.shape, LOW),
            SHAPE(up_weight.shape, LOW),
            SHAPE(down_weight.shape, LOW),
            SHAPE((8, shard), WIDE),
        ],
        in_specs=[SMEM] + [ANY] * 11,
        out_specs=[ANY] * 6 + [VMEM],
        scratch_shapes=[whole] * 9
        + [
            low(2, ny, 2, nz, 2, shard, half),
            low(2, ny, nz, feed_shard, half),
            low(3, ny, 2, nz, 2, shard, group),
            low(ny, nz // 2, 2, 2, shard, width),
            wide(ny, 2, nz, 2, 8, 128),
            wide(8, width),
            low(4, micro, 64, span),
            low(group, group),
            wide(8, group),
            low(4, shard),
            wide(HEAD, HEAD),
            wide(1, HEAD),
            wide(HEAD, HEAD),
            low(64, 512),
            low(ny, nz, feed_shard, width),
            low(nz, feed_shard, width),
            low(4, feed_shard, width),
            low(nz, 2, 2, 2, shard, group),
            low(4, 2, 2, 2, shard, group),
            low(4, ny, 2, 2, shard, group),
            low(ny, 2, 2, shard, group),
            low(2, 2, shard, group),
            low(4, ny, shard, width),
            low(ny, shard, width),
            low(shard, width),
            low(2, 2, 2 * shard, half),
            low(2, 3, shard, half),
            low(3, 2, 2, shard, group),
            low(3, 3, shard, group),
            wide(32, width),
            wide(8, width),
            wide(8, width),
            wide(8, width),
            wide(nz - 1, 8, width),
            wide(8, width),
            wide(3, 8, width),
            dma((240,)),
            dma((240,)),
            dma((36,)),
            dma((2, 2, 2)),
            dma((2, 2, 2)),
            dma((2, 2, 2)),
            pltpu.SemaphoreType.REGULAR,
            pltpu.SemaphoreType.REGULAR,
            pltpu.SemaphoreType.REGULAR,
            pltpu.SemaphoreType.REGULAR,
        ],
        name="layer",
        cost_estimate=pl.CostEstimate(flops=45 * 10**9, bytes_accessed=20 * 10**6, transcendentals=0),
        compiler_params=pltpu.CompilerParams(
            collective_id=0, has_side_effects=True, vmem_limit_bytes=LIMIT
        ),
    )(
        lengths[:, 0], tokens, cotangent, mix_weight, out_weight, up_weight, down_weight, norms,
        feature_freq, feature_scale[None], cosine_basis(), spread_rows(),
    )
    shapes = [w.shape for w in (mix_weight, out_weight, up_weight, down_weight)]
    one = SHAPE((1, shard), WIDE)
    results = pl.pallas_call(
        widen_kernel,
        out_shape=[SHAPE(out_rows.shape, LOW), SHAPE(out_rows.shape, WIDE), one, one, one, one]
        + [SHAPE(shape, WIDE) for shape in shapes],
        in_specs=[ANY] * 3 + [VMEM] + [ANY] * 4,
        out_specs=[ANY] * 2 + [VMEM] * 4 + [ANY] * 4,
        scratch_shapes=[low(*out_rows.shape)] * 3
        + [wide(*out_rows.shape)]
        + [kind(*shape) for shape in shapes[:2] for kind in (low, wide)]
        + [kind(*shape) for shape in shapes[2:] for kind in (low, wide)]
        + [dma((16,)), dma((16,))],
        name="widen",
    )(out_rows, grad_rows, cotangent, gains, gmix, gout, gup, gdown)
    rows, grads, *norm_grads = results[:6]
    return (rows, grads, *results[6:], *(part.reshape(shard) for part in norm_grads))


def solution(mesh):
    ny, nz = mesh.shape["dp"] // 2, mesh.shape["fsdp"] // 2
    grouped = ny == 2 and nz == 4 and D // mesh.size % 32 == 0
    body = partial(per_device_group, ny, nz) if grouped else per_device_plain
    rows = P(("dp", "fsdp"), None)
    vector = P(("dp", "fsdp"))
    slots = P(None, ("dp", "fsdp"), None)
    return jax.shard_map(
        body,
        mesh=mesh,
        in_specs=(slots, slots, *[rows] * 4, *[vector] * 4, P(), P(), slots),
        out_specs=(slots, slots, *[rows] * 4, *[vector] * 4),
        check_vma=False,
    )
```

```python
from functools import partial
import math

import jax
import jax.numpy as jnp
import numpy as np
from jax import lax
from jax.experimental import pallas as pl
from jax.experimental.pallas import tpu as pltpu
from jax.sharding import PartitionSpec as P

D = 1024
HEAD = 64
ROT = 16


epsilon = 1e-05
exact_precision = lax.Precision.HIGHEST


def dct_matrix(width):
    order = jnp.arange(width, dtype=jnp.float32)[:, None]
    sample = jnp.arange(width, dtype=jnp.float32)[None, :]
    factor = jnp.where(order == 0, jnp.sqrt(1.0 / width), jnp.sqrt(2.0 / width))
    return factor * jnp.cos(math.pi * (2.0 * sample + 1.0) * order / (2.0 * width))


def feature_table(feature_freq):
    table = jnp.dot(dct_matrix(HEAD).T, feature_freq.T, precision=exact_precision) / math.sqrt(HEAD)
    return table.astype(jnp.bfloat16)


def slot_layout(span_table, slot_len):
    seg_ends = jnp.cumsum(span_table, axis=-1)
    seg_starts = seg_ends - span_table
    places = jnp.arange(slot_len, dtype=jnp.int32)
    segment = jnp.sum((places[:, None] >= seg_ends[..., None, :]).astype(jnp.int32), axis=-1)
    numbers = jnp.arange(span_table.shape[-1], dtype=jnp.int32)
    matched = segment[..., None] == numbers
    begin_at = jnp.sum(jnp.where(matched, seg_starts[..., None, :], 0), axis=-1)
    begin_at = begin_at + jnp.where(segment == span_table.shape[-1], seg_ends[..., -1:], 0)
    position = (places - begin_at).astype(jnp.float32)
    valid = (segment < span_table.shape[-1]).astype(jnp.float32)
    return (segment, position, valid)


def rotate(raw_heads, position):
    half_rot = ROT // 2
    inverse = 10000.0 ** (-2.0 * jnp.arange(half_rot, dtype=jnp.float32) / ROT)
    angle = position[..., None] * inverse
    cosine_wave = jnp.cos(angle)[..., None, :]
    sine = jnp.sin(angle)[..., None, :]
    first = raw_heads[..., :half_rot]
    second = raw_heads[..., half_rot:ROT]
    return jnp.concatenate(
        [
            first * cosine_wave - second * sine,
            second * cosine_wave + first * sine,
            raw_heads[..., ROT:],
        ],
        axis=-1,
    )


def feature_map(raw_heads, position, table, feature_scale):
    rotated_rows = rotate(raw_heads, position).astype(jnp.bfloat16)
    pre = jnp.einsum("shd,df->shf", rotated_rows, table, preferred_element_type=jnp.float32)
    return feature_scale * jnp.exp(pre)


def feature_back(raw_heads, grad_phi, position, table, feature_scale):
    phi = feature_map(raw_heads, position, table, feature_scale)
    grad_pre = (grad_phi * phi).astype(jnp.bfloat16)
    grad_turned = jnp.einsum("shf,df->shd", grad_pre, table, preferred_element_type=jnp.float32)
    _, turn_pull = jax.vjp(lambda values: rotate(values, position), raw_heads)
    return turn_pull(grad_turned)[0]


def norm_apply(inputs, gain, shift):
    center = inputs - jnp.mean(inputs, axis=-1, keepdims=True)
    spread = jnp.mean(center * center, axis=-1, keepdims=True)
    return center * lax.rsqrt(spread + epsilon) * gain + shift


def head_major(values):
    return jnp.swapaxes(values, 0, 1)


def attend_head(allowed, pieces):
    mapped_query, mapped_key, value_rows = pieces
    score_matrix = jnp.einsum(
        "qf,kf->qk", mapped_query, mapped_key, preferred_element_type=jnp.float32
    )
    score_matrix = jnp.where(allowed, score_matrix, 0.0)
    totals = jnp.sum(score_matrix, axis=1)
    numerator = jnp.dot(
        score_matrix.astype(jnp.bfloat16), value_rows, preferred_element_type=jnp.float32
    )
    return numerator / totals[:, None]


def attend_back(allowed, pieces):
    mapped_query, mapped_key, value_rows, grad_heads = pieces
    score_matrix = jnp.einsum(
        "qf,kf->qk", mapped_query, mapped_key, preferred_element_type=jnp.float32
    )
    score_matrix = jnp.where(allowed, score_matrix, 0.0)
    totals = jnp.sum(score_matrix, axis=1)
    scores_low = score_matrix.astype(jnp.bfloat16)
    numerator = jnp.dot(scores_low, value_rows, preferred_element_type=jnp.float32)
    grad_numer = (grad_heads / totals[:, None]).astype(jnp.bfloat16)
    grad_totals = -jnp.sum(grad_heads * numerator, axis=1) / (totals * totals)
    grad_scores = jnp.einsum(
        "qd,kd->qk", grad_numer, value_rows, preferred_element_type=jnp.float32
    )
    grad_scores = jnp.where(allowed, grad_scores + grad_totals[:, None], 0.0).astype(jnp.bfloat16)
    grad_query = jnp.dot(grad_scores, mapped_key, preferred_element_type=jnp.float32)
    grad_key = jnp.einsum(
        "qk,qf->kf", grad_scores, mapped_query, preferred_element_type=jnp.float32
    )
    grad_value = jnp.einsum("qk,qd->kd", scores_low, grad_numer, preferred_element_type=jnp.float32)
    return (grad_query, grad_key, grad_value)


def fetch_attention(shards):
    return (
        lax.all_gather(shards[0], ("dp", "fsdp"), axis=0, tiled=True),
        lax.all_gather(shards[1], ("dp", "fsdp"), axis=0, tiled=True),
        lax.all_gather(shards[2], ("dp", "fsdp"), axis=0, tiled=True),
        lax.all_gather(shards[3], ("dp", "fsdp"), axis=0, tiled=True),
    )


def fetch_feed(shards):
    return (
        lax.all_gather(shards[0], ("dp", "fsdp"), axis=0, tiled=True),
        lax.all_gather(shards[1], ("dp", "fsdp"), axis=0, tiled=True),
        lax.all_gather(shards[2], ("dp", "fsdp"), axis=0, tiled=True),
        lax.all_gather(shards[3], ("dp", "fsdp"), axis=0, tiled=True),
    )


def reduce_attention(grads):
    return (
        lax.psum_scatter(grads[0], ("dp", "fsdp"), scatter_dimension=0, tiled=True),
        lax.psum_scatter(grads[1], ("dp", "fsdp"), scatter_dimension=0, tiled=True),
        lax.psum_scatter(grads[2], ("dp", "fsdp"), scatter_dimension=0, tiled=True),
        lax.psum_scatter(grads[3], ("dp", "fsdp"), scatter_dimension=0, tiled=True),
    )


def reduce_feed(grads):
    return (
        lax.psum_scatter(grads[0], ("dp", "fsdp"), scatter_dimension=0, tiled=True),
        lax.psum_scatter(grads[1], ("dp", "fsdp"), scatter_dimension=0, tiled=True),
        lax.psum_scatter(grads[2], ("dp", "fsdp"), scatter_dimension=0, tiled=True),
        lax.psum_scatter(grads[3], ("dp", "fsdp"), scatter_dimension=0, tiled=True),
    )


def add_tuples(running, update):
    if running is None:
        return tuple(update)
    return tuple(jax.tree.map(jnp.add, tuple(running), tuple(update)))


def per_device_plain(
    tokens,
    lengths,
    mix_weight,
    out_weight,
    up_weight,
    down_weight,
    attn_gain,
    attn_bias,
    feed_gain,
    feed_bias,
    feature_freq,
    feature_scale,
    cotangent,
):
    table = feature_table(feature_freq)
    slot_len = tokens.shape[1]
    head_count = D // HEAD
    attn_shards = (mix_weight, out_weight, attn_gain, attn_bias)
    feed_shards = (up_weight, down_weight, feed_gain, feed_bias)
    places = jnp.arange(slot_len, dtype=jnp.int32)
    output_rows = []
    grad_inputs = []
    attn_total = None
    feed_total = None
    for micro_index in range(tokens.shape[0]):
        attn_full = fetch_attention(attn_shards)
        feed_full = fetch_feed(feed_shards)
        mix_full, out_full, gain_one, bias_one = attn_full
        up_full, down_full, gain_two, bias_two = feed_full
        gain_attn = gain_one.astype(jnp.float32)
        shift_attn = bias_one.astype(jnp.float32)
        gain_feed = gain_two.astype(jnp.float32)
        shift_feed = bias_two.astype(jnp.float32)
        inputs = tokens[micro_index].astype(jnp.float32)
        segment, position, valid = slot_layout(lengths[micro_index, 0], slot_len)
        allowed = (segment[:, None] == segment[None, :]) & (places[None, :] <= places[:, None])
        normed_attn = norm_apply(inputs, gain_attn, shift_attn).astype(jnp.bfloat16)
        normed_feed = norm_apply(inputs, gain_feed, shift_feed).astype(jnp.bfloat16)
        mixed = jnp.dot(normed_attn, mix_full, preferred_element_type=jnp.float32)
        mixed = mixed.reshape(slot_len, 3, head_count, HEAD)
        query_raw = mixed[:, 0]
        key_raw = mixed[:, 1]
        value_rows = mixed[:, 2].astype(jnp.bfloat16)
        mapped_query = feature_map(query_raw, position, table, feature_scale).astype(jnp.bfloat16)
        mapped_key = feature_map(key_raw, position, table, feature_scale).astype(jnp.bfloat16)
        attended = lax.map(
            partial(attend_head, allowed),
            (head_major(mapped_query), head_major(mapped_key), head_major(value_rows)),
        )
        attended = head_major(attended).reshape(slot_len, D).astype(jnp.bfloat16)
        attn_rows = jnp.dot(attended, out_full, preferred_element_type=jnp.float32)
        hidden = jnp.dot(normed_feed, up_full, preferred_element_type=jnp.float32)
        active = jax.nn.gelu(hidden, approximate=False).astype(jnp.bfloat16)
        feed_rows = jnp.dot(active, down_full, preferred_element_type=jnp.float32)
        result = inputs + valid[:, None] * (attn_rows + feed_rows)
        output_rows.append(result.astype(jnp.bfloat16))
        attn_full = fetch_attention(attn_shards)
        feed_full = fetch_feed(feed_shards)
        mix_full, out_full, gain_one, bias_one = attn_full
        up_full, down_full, gain_two, bias_two = feed_full
        grad_rows = cotangent[micro_index]
        grad_branch = jnp.where(valid[:, None] > 0.0, grad_rows, jnp.zeros_like(grad_rows))
        grad_down = jnp.einsum("sf,sd->fd", active, grad_branch, preferred_element_type=jnp.float32)
        grad_out = jnp.einsum(
            "sd,se->de", attended, grad_branch, preferred_element_type=jnp.float32
        )
        grad_active = jnp.einsum(
            "sd,fd->sf", grad_branch, down_full, preferred_element_type=jnp.float32
        )
        _, gelu_pull = jax.vjp(partial(jax.nn.gelu, approximate=False), hidden)
        grad_hidden = gelu_pull(grad_active)[0].astype(jnp.bfloat16)
        grad_up = jnp.einsum(
            "sd,sf->df", normed_feed, grad_hidden, preferred_element_type=jnp.float32
        )
        grad_normed_feed = jnp.einsum(
            "sf,df->sd", grad_hidden, up_full, preferred_element_type=jnp.float32
        )
        grad_attended = jnp.einsum(
            "sd,ed->se", grad_branch, out_full, preferred_element_type=jnp.float32
        )
        grad_attended = grad_attended.reshape(slot_len, head_count, HEAD)
        grad_phi_q, grad_phi_k, grad_value = lax.map(
            partial(attend_back, allowed),
            (
                head_major(mapped_query),
                head_major(mapped_key),
                head_major(value_rows),
                head_major(grad_attended),
            ),
        )
        grad_query = feature_back(query_raw, head_major(grad_phi_q), position, table, feature_scale)
        grad_key = feature_back(key_raw, head_major(grad_phi_k), position, table, feature_scale)
        grad_mixed = jnp.stack([grad_query, grad_key, head_major(grad_value)], axis=1)
        grad_mixed = grad_mixed.reshape(slot_len, 3 * D).astype(jnp.bfloat16)
        grad_mix = jnp.einsum(
            "sd,se->de", normed_attn, grad_mixed, preferred_element_type=jnp.float32
        )
        grad_normed_attn = jnp.einsum(
            "se,de->sd", grad_mixed, mix_full, preferred_element_type=jnp.float32
        )
        _, attn_norm_pull = jax.vjp(norm_apply, inputs, gain_attn, shift_attn)
        grad_in_one, grad_gain_one, grad_bias_one = attn_norm_pull(grad_normed_attn)
        _, feed_norm_pull = jax.vjp(norm_apply, inputs, gain_feed, shift_feed)
        grad_in_two, grad_gain_two, grad_bias_two = feed_norm_pull(grad_normed_feed)
        grad_inputs.append(grad_rows.astype(jnp.float32) + grad_in_one + grad_in_two)
        attn_grads = (grad_mix, grad_out, grad_gain_one, grad_bias_one)
        feed_grads = (grad_up, grad_down, grad_gain_two, grad_bias_two)
        attn_grads = reduce_attention(attn_grads)
        feed_grads = reduce_feed(feed_grads)
        attn_total = add_tuples(attn_total, attn_grads)
        feed_total = add_tuples(feed_total, feed_grads)
    return (
        jnp.stack(output_rows),
        jnp.stack(grad_inputs),
        attn_total[0],
        attn_total[1],
        feed_total[0],
        feed_total[1],
        attn_total[2],
        attn_total[3],
        feed_total[2],
        feed_total[3],
    )


MESH_ID = pl.DeviceIdType.MESH
LOW = jnp.bfloat16
WIDE = jnp.float32


def here(nz):
    dp = lax.axis_index("dp")
    fs = lax.axis_index("fsdp")
    return dp // 2, dp % 2, fs // 2, fs % 2


class Places:
    def __init__(self, ny, nz):
        self.ny, self.nz = ny, nz
        self.y, self.x, self.z, self.c = here(nz)

    def at(self, y, x, z, c):
        return (y * 2 + x, z * 2 + c)

    def member(self, r):
        x = 1 - self.x if r & 2 else self.x
        c = 1 - self.c if r & 1 else self.c
        return x, c

    def member_id(self, r):
        x, c = self.member(r)
        return self.at(self.y, x, self.z, c)

    def yid(self):
        return self.at(1 - self.y, self.x, self.z, self.c)

    def zid(self, step):
        return self.at(self.y, self.x, (self.z + step) % self.nz, self.c)

    def zsrc(self, step):
        return (self.z + self.nz - step) % self.nz

    def signal(self):
        barrier = pltpu.get_barrier_semaphore()
        ids = [self.member_id(r) for r in (1, 2, 3)] + [self.yid()]
        ids += [self.zid(step) for step in range(1, self.nz)]
        for one in ids:
            pl.semaphore_signal(barrier, inc=1, device_id=one, device_id_type=MESH_ID)

    def meet(self):
        pl.semaphore_wait(pltpu.get_barrier_semaphore(), self.nz + 3)


class Copy:
    def __init__(self, describe):
        self.describe, self.sent = describe, False

    def start(self):
        self.describe().start()

    def wait_recv(self):
        self.describe().wait_recv()

    def wait_send(self):
        if not self.sent:
            self.describe().wait_send()
            self.sent = True


class Links:
    def __init__(self, send, recv):
        self.send, self.recv, self.count, self.open = send, recv, 0, []

    def plan(self, src, dst, device):
        i = self.count
        self.count += 1

        def describe():
            return pltpu.make_async_remote_copy(
                src() if callable(src) else src,
                dst() if callable(dst) else dst,
                self.send.at[i],
                self.recv.at[i],
                device_id=device() if callable(device) else device,
                device_id_type=MESH_ID,
            )

        return Copy(describe)

    def start(self, src, dst, device):
        copy = self.plan(src, dst, device)
        copy.start()
        self.open.append(copy)
        return copy

    def drain(self):
        for copy in self.open:
            copy.wait_send()


class Locals:
    def __init__(self, sems):
        self.sems, self.count = sems, 0

    def start(self, src, dst):
        copy = pltpu.make_async_copy(src, dst, self.sems.at[self.count])
        self.count += 1
        copy.start()
        return copy


class Line:
    def __init__(self, place):
        z = place.z
        self.place = place
        self.way = 1 - 2 * (z // 2)
        self.inner = (z // 2) * (3 - z) + (1 - z // 2) * z

    def off(self, end, inner):
        return self.place.z + self.way * ((1 - self.inner) * end + self.inner * inner)

    def near(self):
        return self.off(1, -1)

    def second(self):
        return self.off(2, 1)

    def third(self):
        return self.off(3, 2)

    def id(self, z):
        return self.place.at(self.place.y, self.place.x, z, self.place.c)

    def at_end(self, event):
        pl.when(self.inner == 0)(event)

    def at_inner(self, event):
        pl.when(self.inner == 1)(event)


class Spread:
    def __init__(self, links, line, block, own=None):
        z = line.place.z
        mine = own if own is not None else lambda: block(z)

        def here():
            return block(z)

        def second():
            return block(line.second())

        def third():
            return block(line.third())

        self.line = line
        self.sources = [line.near, line.second, line.third]
        self.beside = links.plan(mine, here, lambda: line.id(line.near()))
        self.across = links.plan(mine, here, lambda: line.id(line.second()))
        self.far = links.plan(mine, here, lambda: line.id(line.second()))
        self.hand_second = links.plan(second, second, lambda: line.id(line.near()))
        self.hand_third = links.plan(third, third, lambda: line.id(line.near()))

    def begin(self):
        self.beside.start()
        self.line.at_inner(self.across.start)
        self.line.at_end(self.far.start)

    def arrive_near(self, then=None):
        self.beside.wait_recv()
        if then:
            then[0].start()

    def arrive_inner(self, then=None):
        @self.line.at_inner
        def _():
            self.across.wait_recv()
            self.hand_second.start()
            if then:
                then[1].start()
            self.far.wait_recv()
            self.hand_third.start()
            if then:
                then[2].start()

    def arrive_end(self, then=None):
        @self.line.at_end
        def _():
            self.hand_second.wait_recv()
            if then:
                then[1].start()
            self.hand_third.wait_recv()
            if then:
                then[2].start()

    def drain(self):
        self.beside.wait_send()

        @self.line.at_inner
        def _():
            for copy in (self.across, self.hand_second, self.hand_third):
                copy.wait_send()

        self.line.at_end(self.far.wait_send)


class Direct:
    def __init__(self, links, line, block, own=None):
        place = line.place
        self.sources = [partial(place.zsrc, step) for step in range(1, place.nz)]
        mine = own if own is not None else lambda: block(place.z)
        self.copies = [
            links.plan(mine, lambda: block(place.z), partial(place.zid, step))
            for step in range(1, place.nz)
        ]

    def begin(self):
        for copy in self.copies:
            copy.start()

    def arrive_near(self, then=()):
        for k, copy in enumerate(self.copies):
            copy.wait_recv()
            if then:
                then[k].start()

    def arrive_inner(self, then=None):
        pass

    def arrive_end(self, then=None):
        pass

    def drain(self):
        for copy in self.copies:
            copy.wait_send()


class Gather:
    def __init__(self, links, place, line, block, own=None, way=Spread):
        def plane(z):
            return block(place.y, z)

        self.spread = way(links, line, plane, own)
        mine = own if own is not None else lambda: plane(place.z)
        self.cross = links.plan(mine, lambda: plane(place.z), place.yid)
        self.cross_on = [
            links.plan(lambda at=at: plane(at()), lambda at=at: plane(at()), place.yid)
            for at in self.spread.sources
        ]

    def begin(self):
        self.spread.begin()
        self.cross.start()

    def forward(self):
        self.spread.arrive_near(self.cross_on)
        self.spread.arrive_inner(self.cross_on)

    def late(self):
        self.spread.arrive_end(self.cross_on)

    def finish(self):
        for copy in [self.cross] + self.cross_on:
            copy.wait_recv()

    def drain(self):
        self.spread.drain()
        for copy in [self.cross] + self.cross_on:
            copy.wait_send()


class GatherCross:
    def __init__(self, links, place, line, block, own=None, way=Spread):
        def plane(z):
            return block(place.y, z)

        def other(z):
            return block(1 - place.y, z)

        mine = own if own is not None else lambda: plane(place.z)
        self.cross = links.plan(mine, lambda: plane(place.z), place.yid)
        self.spread = way(links, line, plane, own)
        self.spread_other = way(links, line, other)

    def begin(self):
        self.cross.start()
        self.spread.begin()

    def forward(self):
        self.cross.wait_recv()
        self.spread_other.begin()
        self.spread.arrive_near()
        self.spread.arrive_inner()

    def late(self):
        self.spread.arrive_end()
        self.spread_other.arrive_near()
        self.spread_other.arrive_inner()

    def finish(self):
        self.spread_other.arrive_end()

    def drain(self):
        self.cross.wait_send()
        self.spread.drain()
        self.spread_other.drain()


def dot_nn(a, b):
    return jnp.dot(a, b, preferred_element_type=WIDE)


def dot_nt(a, b):
    return lax.dot_general(a, b, (((1,), (1,)), ((), ())), preferred_element_type=WIDE)


def dot_tn(a, b):
    return lax.dot_general(a, b, (((0,), (0,)), ((), ())), preferred_element_type=WIDE)


def fold_rows(values):
    rows, cols = values.shape
    return jnp.sum(values.reshape(rows // 8, 8, cols), axis=0)


class Fold:
    def __init__(self, links, line, block, land):
        self.line, self.block, self.land = line, block, land

        def to(at, where, slot):
            return links.plan(lambda: block(at()), lambda: land(slot), lambda: line.id(where()))

        self.beside = to(line.near, line.near, 0)
        self.across = to(line.second, line.second, 1)
        self.far = to(line.second, line.second, 2)
        self.hand = to(line.third, line.near, 3)
        self.handed = to(line.third, line.third, 1)

    def send(self, k):
        if k == 0:
            self.line.at_inner(self.across.start)
            self.line.at_end(self.far.start)
        if k == 1:
            self.line.at_end(self.hand.start)
        if k == 2:
            self.beside.start()

    def hand_on(self):
        @self.line.at_inner
        def _():
            self.hand.wait_recv()
            block = self.block(self.line.third())
            block[...] = (block[...].astype(WIDE) + self.land(3)[...].astype(WIDE)).astype(LOW)
            self.handed.start()

    def total(self, own, emit):
        self.beside.wait_recv()

        @self.line.at_end
        def _():
            self.handed.wait_recv()
            emit(own() + self.land(0)[...].astype(WIDE) + self.land(1)[...].astype(WIDE))

        @self.line.at_inner
        def _():
            self.across.wait_recv()
            self.far.wait_recv()
            total = own() + self.land(0)[...].astype(WIDE) + self.land(1)[...].astype(WIDE)
            emit(total + self.land(2)[...].astype(WIDE))

    def drain(self):
        self.beside.wait_send()

        @self.line.at_inner
        def _():
            self.across.wait_send()
            self.handed.wait_send()

        @self.line.at_end
        def _():
            self.far.wait_send()
            self.hand.wait_send()


class Scatter:
    def __init__(self, links, place, line, theirs, mine, ybuf, zbuf):
        self.place, self.line, self.mine, self.ybuf = place, line, mine, ybuf
        self.order = [line.second, line.third, line.near, lambda: place.z]
        self.ys = [
            links.plan(lambda at=at: theirs(at()), lambda at=at: ybuf(at()), place.yid)
            for at in self.order
        ]
        self.fold = Fold(links, line, ybuf, zbuf)

    def begin(self):
        for copy in self.ys:
            copy.start()

    def turn(self, k):
        self.ys[k].wait_recv()
        if k < 3:
            at = self.order[k]()
            land = self.ybuf(at)
            land[...] = (land[...].astype(WIDE) + self.mine(at)[...].astype(WIDE)).astype(LOW)
        self.fold.send(k)

    def hand_on(self):
        self.fold.hand_on()

    def total(self, emit):
        z = self.place.z
        self.fold.total(
            lambda: self.ybuf(z)[...].astype(WIDE) + self.mine(z)[...].astype(WIDE), emit
        )

    def drain(self):
        for copy in self.ys:
            copy.wait_send()
        self.fold.drain()


class ScatterCross:
    def __init__(self, links, place, line, parts, zbuf, hold, land):
        self.place, self.parts, self.hold, self.land = place, parts, hold, land
        self.fold = Fold(links, line, parts, zbuf)
        self.cross = links.plan(lambda: hold.at[1 - place.y], lambda: land, place.yid)

    def begin(self):
        for k in range(3):
            self.fold.send(k)

    def hand_on(self):
        self.fold.hand_on()

    def turn(self):
        def emit(total):
            self.hold[...] = total.astype(LOW)

        self.fold.total(lambda: self.parts(self.place.z)[...].astype(WIDE), emit)
        self.cross.start()

    def total(self):
        self.cross.wait_recv()
        return self.hold[self.place.y].astype(WIDE) + self.land[...].astype(WIDE)

    def drain(self):
        self.cross.wait_send()
        self.fold.drain()


def layer_kernel(
    ny, nz,
    lens, tok, cot, mix_w, out_w, up_w, down_w, gain_a, bias_a, gain_f, bias_f, freq_in, scale_ref, dct_in, spread_in,
    out_rows, grad_rows, gmix_out, gout_out, gup_out, gdown_out, gains_out,
    xs, gs, nf, na, act, gp, feed, gxf, gm,
    up, down, mix, outw, small, gains, meta, table, scale, norms, freq, scale_in, dct, spread,
    gdown, ydown, zdown, ymix, zmix,
    zval, hval, yval, zout, hout, yout,
    up_send, up_recv, mix_send, mix_recv, gacc, gsum, gy, g2, gz, g3, gm_sum,
    send, recv, sems, sib_sems, own_sems, far_sems, out_free, sib_free, far_free, act_free,
):
    place = Places(ny, nz)
    y, x, z, c = place.y, place.x, place.z, place.c
    me = x * 2 + c
    micro, span, width = xs.shape[1:]
    shard = out_w.shape[0]
    feed_shard = down_w.shape[0]
    half = up.shape[-1]
    quarter = half // 2
    heads = width // HEAD // 4
    group = heads * HEAD
    none = jnp.zeros((), LOW)
    local = Locals(sems)

    def raw(n):
        return feed.at[3, 0, pl.ds(n * shard, shard)]

    def raw_load(weight, first):
        count = weight.shape[1] // width
        return [
            local.start(weight.at[:, pl.ds(n * width, width)], raw(first + n)) for n in range(count)
        ]

    norms_load = [
        local.start(src, norms.at[k]) for k, src in enumerate((gain_a, bias_a, gain_f, bias_f))
    ]
    mix_load = raw_load(mix_w, 0)
    up_load = raw_load(up_w, len(mix_load))
    out_mine = local.start(out_w, outw.at[y, z // 2, z % 2, c])
    tok_mine = local.start(tok, gp.at[0])
    cot_mine = local.start(cot, gs.at[0])
    down_mine = [
        local.start(down_w.at[:, pl.ds(k * half, half)], down.at[k, y, z]) for k in range(2)
    ]
    place.signal()
    table_loads = [
        local.start(src, dst)
        for src, dst in ((freq_in, freq), (scale_ref, scale_in), (dct_in, dct), (spread_in, spread))
    ]

    row = lax.broadcasted_iota(jnp.int32, (8, 128), 0)
    lane = lax.broadcasted_iota(jnp.int32, (8, 128), 1)
    facts = jnp.zeros((8, 128), WIDE)
    for s in range(micro):
        for k in range(lens.shape[1]):
            facts = jnp.where((row == 1 + s) & (lane == k), lens[s, k].astype(WIDE), facts)
    for copy in norms_load:
        copy.wait()
    at_row = lax.broadcasted_iota(jnp.int32, (shard, 128), 0)
    at_lane = lax.broadcasted_iota(jnp.int32, (shard, 128), 1)
    for k in range(4):
        pick = jnp.where(at_lane == at_row + k * shard, 1.0, 0.0).astype(LOW)
        facts = jnp.where(row == 0, facts + dot_nn(norms[k], pick), facts)
    small[y, x, z, c] = facts

    def up_stage(q):
        return gdown.at[:, q, pl.ds(0, shard), pl.ds(0, half)]

    def mix_stage(t, q):
        return gdown.at[0, q, pl.ds((t + 1) * shard, shard), pl.ds(half, group)]

    def raw_cols(base, first, count):
        at = first % width
        return raw(base + first // width)[:, at : at + count]

    for copy in mix_load:
        copy.wait()
    pair = group // ny
    for q in range(4):
        for t in range(3):
            for by in range(ny):
                first = t * width + ((by * 2 + q // 2) * 2 + q % 2) * pair
                mix_stage(t, q)[:, by * pair : (by + 1) * pair] = raw_cols(0, first, pair)
    for t in range(3):
        mix[t, y, x, z, c] = mix_stage(t, me)[...]
    place.meet()
    links = Links(send, recv)
    line = Line(place)

    def swap(src, dst):
        copies = []
        for r in (1, 2, 3):
            mx, mc = place.member(r)
            copies.append(links.start(src(mx * 2 + mc), dst, place.member_id(r)))
        return copies

    def landed(copies):
        for copy in copies:
            copy.wait_recv()

    small_swaps = swap(lambda q: small.at[y, x, z, c], small.at[y, x, z, c])
    mix_swaps = []
    for t in range(3):
        mix_swaps += swap(lambda q, t=t: mix_stage(t, q), mix.at[t, y, x, z, c])
    for copy in up_load:
        copy.wait()
    for q in range(4):
        for by in range(ny):
            for bz in range(nz):
                first = (((by * 2 + q // 2) * nz + bz) * 2 + q % 2) * feed_shard
                cols = slice(bz * feed_shard, (bz + 1) * feed_shard)
                up_stage(q)[by, :, cols] = raw_cols(len(mix_load), first, feed_shard)
    up[:, y, x, z, c] = up_stage(me)[...]
    up_swaps = swap(up_stage, up.at[:, y, x, z, c])
    chunks = [GatherCross(links, place, line, lambda by, bz: outw.at[by, bz // 2, bz % 2, c])]
    for t in range(3):
        chunks.append(Gather(links, place, line, lambda by, bz, t=t: mix.at[t, by, :, bz]))
    halves = [(k, pl.ds(h * quarter, quarter)) for k in range(2) for h in range(2)]
    for k, cols in halves:
        chunks.append(
            Gather(
                links, place, line,
                lambda by, bz, k=k, cols=cols: up.at[k, by, :, bz, :, :, cols],
            )
        )
    for k, cols in halves:
        way = GatherCross if (k, cols) == halves[-1] else Gather
        chunks.append(
            way(links, place, line, lambda by, bz, k=k, cols=cols: down.at[k, by, bz, :, cols])
        )
    of_mix, of_up, of_down = range(1, 4), range(4, 8), range(8, 12)
    ahead = 3
    hurried = [3]

    def turn_chunk(i):
        chunks[i].forward()
        if i and i - 1 not in hurried:
            chunks[i - 1].late()
        if i + ahead < len(chunks):
            chunks[i + ahead].begin()

    small_gather = Gather(links, place, line, lambda by, bz: small.at[by, :, bz])
    tok_sib = links.plan(gp.at[0], gp.at[1], partial(place.member_id, 1))
    tok_far = links.plan(gp.at[0], gp.at[2], partial(place.member_id, 2))
    cot_sib = links.plan(gs.at[0], gs.at[1], partial(place.member_id, 1))
    cot_far = links.plan(gs.at[0], gs.at[2], partial(place.member_id, 2))

    def send_tokens():
        tok_mine.wait()
        tok_sib.start()
        tok_far.start()

    def send_cot():
        cot_mine.wait()
        at_place = lax.broadcasted_iota(jnp.int32, (span, 1), 0)
        for s in range(micro):
            used = lens[s, 0]
            for k in range(1, lens.shape[1]):
                used = used + lens[s, k]
            gs[0, s] = jnp.where(at_place < used, gs[0, s], none)
        cot_sib.start()
        cot_far.start()

    def make_table():
        for copy in table_loads:
            copy.wait()
        raw = lax.dot_general(
            dct[...], freq[...], (((0,), (1,)), ((), ())),
            precision=lax.Precision.HIGHEST, preferred_element_type=WIDE,
        ) / math.sqrt(HEAD)
        raw = raw.astype(LOW)
        tile_row = lax.broadcasted_iota(jnp.int32, (HEAD, group), 0)
        tile_col = lax.broadcasted_iota(jnp.int32, (HEAD, group), 1)
        tiled = jnp.where(tile_col % HEAD == tile_row, 1.0, 0.0).astype(LOW)
        wide_table = dot_tn(tiled, dot_nn(raw, tiled).astype(LOW))
        block_row = lax.broadcasted_iota(jnp.int32, (group, group), 0) // HEAD
        block_col = lax.broadcasted_iota(jnp.int32, (group, group), 1) // HEAD
        table[...] = jnp.where(block_row == block_col, wide_table, 0.0).astype(LOW)
        scale[...] = lax.dot_general(
            jnp.broadcast_to(scale_in[...], (8, HEAD)), tiled.astype(WIDE), (((1,), (0,)), ((), ())),
            precision=lax.Precision.HIGHEST, preferred_element_type=WIDE,
        )

    def make_gains():
        count = ny * 2 * nz * 2
        packed = jnp.sum(jnp.where(row == 0, small[...].reshape(count, 8, 128), 0.0), axis=1)
        packed = packed.astype(LOW)
        pick_row = lax.broadcasted_iota(jnp.int32, (128, width), 0)
        pick_col = lax.broadcasted_iota(jnp.int32, (128, width), 1) % shard
        owner = lax.broadcasted_iota(jnp.int32, (count, width), 0)
        owned = lax.broadcasted_iota(jnp.int32, (count, width), 1) // shard
        for k in range(4):
            pick = jnp.where(pick_row == pick_col + k * shard, 1.0, 0.0).astype(LOW)
            part = jnp.where(owned == owner, dot_nn(packed, pick), 0.0)
            gains[k : k + 1, :] = jnp.sum(part, axis=0, keepdims=True)
        gacc[...] = jnp.zeros_like(gacc)

    def make_turns():
        places = lax.broadcasted_iota(jnp.int32, (1, span), 1).astype(WIDE)
        turn_row = lax.broadcasted_iota(jnp.int32, (ROT // 2, 1), 0)
        inverse = jnp.zeros((ROT // 2, 1), WIDE)
        for k in range(ROT // 2):
            inverse = jnp.where(turn_row == k, 10000.0 ** (-2.0 * k / ROT), inverse)
        fact_row = lax.broadcasted_iota(jnp.int32, (8, span), 0)
        for r in range(4):
            mx, mc = place.member(r)
            facts = small[y, mx, z, mc]
            for s in range(micro):
                end = jnp.zeros((1, 1), WIDE)
                segment = jnp.zeros((1, span), WIDE)
                begin = jnp.zeros((1, span), WIDE)
                for k in range(lens.shape[1]):
                    end = end + facts[1 + s : 2 + s, k : k + 1]
                    past = places >= end
                    segment = segment + jnp.where(past, 1.0, 0.0)
                    begin = jnp.where(past, end, begin)
                angle = inverse * (places - begin)
                valid = jnp.where(segment < lens.shape[1], 1.0, 0.0)
                rest = jnp.where(fact_row == 0, segment, jnp.where(fact_row == 1, 1.0, 0.0))
                rest = jnp.where(fact_row == 2, valid, rest)
                left = jnp.concatenate([jnp.cos(angle), jnp.sin(angle)], axis=0)
                for first in (0, 24, 40):
                    part = left.astype(LOW)
                    left = left - part.astype(WIDE)
                    meta[r, s, first : first + 16, :] = part
                meta[r, s, 16:24, :] = rest.astype(LOW)
                meta[r, s, 56:64, :] = jnp.zeros((8, span), LOW)

    def norm(j):
        def body(i, carry):
            s = i // (span // 128)
            rs = pl.ds(pl.multiple_of(i % (span // 128) * 128, 128), 128)
            values = gp[j, s, rs, :].astype(WIDE)
            center = values - jnp.mean(values, axis=1, keepdims=True)
            deviation = jnp.mean(center * center, axis=1, keepdims=True)
            hat = center * lax.rsqrt(deviation + epsilon)
            na[j, s, rs, :] = (hat * gains[0:1, :] + gains[1:2, :]).astype(LOW)
            nf[j, s, rs, :] = (hat * gains[2:3, :] + gains[3:4, :]).astype(LOW)
            xs[j, s, rs, :] = hat.astype(LOW)
            return carry

        lax.fori_loop(0, micro * span // 128, body, 0)

    def loop(first, last, body, events):
        def step(i, carry):
            def pump(part):
                for (at, which), event in events.items():
                    if which == part:

                        @pl.when(i == at)
                        def _(event=event):
                            event()

            body(i, pump)
            return carry

        lax.fori_loop(first, last, step, 0)

    head_lane = lax.broadcasted_iota(jnp.int32, (1, group), 1)
    of_head = [head_lane // HEAD == h for h in range(heads)]
    low_lane = lax.broadcasted_iota(jnp.int32, (1, 128), 1) % HEAD < ROT // 2
    key_at = lax.broadcasted_iota(jnp.int32, (span, span), 1)
    query_at = lax.broadcasted_iota(jnp.int32, (span, span), 0)
    wide_mix = 3 * group

    def turn(values, cosine, sine):
        parts = []
        for first in range(0, group, 128):
            part = values[:, first : first + 128]
            other = jnp.where(
                low_lane, pltpu.roll(part, 128 - ROT // 2, 1), pltpu.roll(part, ROT // 2, 1)
            )
            parts.append(part * cosine + other * sine)
        return jnp.concatenate(parts, axis=1)

    def spread_meta(j, s, first, last):
        return dot_tn(meta[j, s], spread[:, first:last])

    def attend_forward(j, s):
        rows = na[j, s]
        turns = spread_meta(j, s, 0, 384)
        cosine, sine, owner = turns[:, :128], turns[:, 128:256], turns[:, 256:384]
        owner = jnp.concatenate([owner, owner], axis=1)
        allowed = (owner == meta[j, s, 16:24, :][0:1, :].astype(WIDE)) & (key_at <= query_at)
        query, key, value = (dot_nn(rows, mix[t].reshape(width, group)) for t in range(3))
        query = turn(query, cosine, sine).astype(LOW)
        key = turn(key, cosine, sine).astype(LOW)
        value = value.astype(LOW)
        raised_query = scale[0:1, :] * jnp.exp(dot_nn(query, table[...]))
        raised_key = scale[0:1, :] * jnp.exp(dot_nn(key, table[...]))
        phi_query = raised_query.astype(LOW)
        phi_key = raised_key.astype(LOW)
        scores, totals = [], []
        numer = jnp.zeros((span, group), WIDE)
        total = jnp.zeros((span, group), WIDE)
        for h in range(heads):
            score = dot_nt(jnp.where(of_head[h], phi_query, none), phi_key)
            score = jnp.where(allowed, score, 0.0)
            totals.append(jnp.sum(score, axis=1, keepdims=True))
            scores.append(score.astype(LOW))
            numer += dot_nn(scores[h], jnp.where(of_head[h], value, none))
            total = jnp.where(of_head[h], totals[h], total)
        att = (numer / total).astype(LOW)
        gm[j, s, :, wide_mix:] = att
        return (att, cosine, sine, allowed, raised_query, raised_key, phi_query, phi_key, value,
                scores, totals, numer, total)

    def attend_back(j, s, kept):
        (att, cosine, sine, allowed, raised_query, raised_key, phi_query, phi_key, value,
         scores, totals, numer, total) = kept
        feed[j, s] = dot_nn(att, outw[:, c].reshape(group, width)).astype(LOW)
        grad_att = dot_nt(gs[j, s], outw[:, c].reshape(group, width))
        grad_numer = (grad_att / total).astype(LOW)
        product = grad_att * numer
        grad_query = jnp.zeros((span, group), WIDE)
        grad_key = jnp.zeros((span, group), WIDE)
        grad_value = jnp.zeros((span, group), WIDE)
        for h in range(heads):
            grad_total = -jnp.sum(jnp.where(of_head[h], product, 0.0), axis=1, keepdims=True)
            grad_total = grad_total / (totals[h] * totals[h])
            numer_h = jnp.where(of_head[h], grad_numer, none)
            grad_score = dot_nt(numer_h, value) + grad_total
            grad_score = jnp.where(allowed, grad_score, 0.0).astype(LOW)
            grad_query += dot_nn(grad_score, jnp.where(of_head[h], phi_key, none))
            grad_key += dot_tn(grad_score, jnp.where(of_head[h], phi_query, none))
            grad_value += dot_tn(scores[h], numer_h)
        back_query = turn(
            dot_nt((grad_query * raised_query).astype(LOW), table[...]), cosine, -sine
        )
        back_key = turn(dot_nt((grad_key * raised_key).astype(LOW), table[...]), cosine, -sine)
        parts = (back_query.astype(LOW), back_key.astype(LOW), grad_value.astype(LOW))
        grad_normed = jnp.zeros((span, width), WIDE)
        for t in range(3):
            gm[j, s, :, t * group : (t + 1) * group] = parts[t]
            grad_normed += dot_nt(parts[t], mix[t].reshape(width, group))
        gacc[0:8, :] += fold_rows(grad_normed * xs[j, s].astype(WIDE))
        gacc[8:16, :] += fold_rows(grad_normed)
        gxf[j, s] = (grad_normed * gains[0:1, :]).astype(LOW)

    def attend(j, pump):
        kept = []
        for s in range(micro):
            kept.append(attend_forward(j, s))
            pump(s)
        for s in range(micro):
            attend_back(j, s, kept[s])
            pump(micro + s)

    def hidden(k):
        def body(i, pump):
            j, s = i // micro, i % micro
            pump(0)
            h = dot_nn(nf[j, s], up[k].reshape(width, half))
            cdf = 0.5 * (1.0 + lax.erf(h * math.sqrt(0.5)))
            pdf = jnp.exp(-0.5 * h * h) * (1.0 / math.sqrt(2.0 * math.pi))
            act[j, s, :, pl.ds(k * half, half)] = (h * cdf).astype(LOW)
            gp[j, s, :, pl.ds(k * half, half)] = (cdf + h * pdf).astype(LOW)

        return body

    rest = 4 * micro * span
    blocks = width // 256

    def other_first(i):
        return (i + (1 - y) * (blocks // 2)) % blocks

    def outer(a, b, first, last, store):
        def body(i, carry):
            at = other_first(i)
            cols = pl.ds(pl.multiple_of(at * 256, 256), 256)
            store(at, dot_tn(a[:, :, :, cols].reshape(rest, 256), b().reshape(rest, -1)))
            return carry

        lax.fori_loop(first, last, body, 0)

    def keep_down(at, part):
        per = 256 // feed_shard
        for k in range(per):
            block = at * per + k
            rows = slice(k * feed_shard, (k + 1) * feed_shard)
            gdown[block // nz, block % nz] = part[rows].astype(LOW)

    def keep_up(at, part):
        na[2 + at // 2, at % 2] = part.astype(LOW)

    def up_block(ref, j, at, cols):
        size = 2 * shard
        return ref.at[j, :, pl.ds(pl.multiple_of(at * size, size), size), cols]

    def keep_mix(at, part):
        for t in range(3):
            cols = part[:, t * group : (t + 1) * group].astype(LOW)
            mix[t, at // 2, at % 2] = cols.reshape(nz, 2, shard, group)

    def outer_down(first, last):
        outer(act, lambda: gs[...], first, last, keep_down)

    def outer_up(first, last):
        outer(nf, lambda: gp[...], first, last, keep_up)

    def outer_mix(first, last):
        outer(na, lambda: gm[:, :, :, 0:wide_mix], first, last, keep_mix)

    down_sum = Scatter(
        links, place, line, lambda at: gdown.at[1 - y, at], lambda at: gdown.at[y, at],
        lambda at: ydown.at[at], lambda k: zdown.at[k],
    )
    up_sums = []
    for k in range(2):
        cols = pl.ds(k * half, half)
        up_sums.append(
            Scatter(
                links, place, line,
                lambda at, cols=cols: up_block(na, 3 - y, at, cols),
                lambda at, cols=cols: up_block(na, 2 + y, at, cols),
                lambda at, cols=cols: up_block(act, 2, at, cols),
                lambda at, cols=cols: up_block(act, 3, at, cols),
            )
        )
    two = pl.ds(0, 2)
    mix_sum = Scatter(
        links, place, line, lambda at: mix.at[two, 1 - y, :, at],
        lambda at: mix.at[two, y, :, at], lambda at: ymix.at[at], lambda k: zmix.at[k],
    )
    val_sum = ScatterCross(
        links, place, line, lambda at: mix.at[2, :, :, at], lambda k: zval.at[k], hval, yval
    )
    out_sum = ScatterCross(
        links, place, line, lambda at: outw.at[:, at // 2, at % 2, c], lambda k: zout.at[k],
        hout, yout,
    )

    out_here = outw.at[:, 1 - c, :, c]
    out_swap = links.plan(out_here, out_here, partial(place.member_id, 1))
    landed(mix_swaps[0:3])
    landed(small_swaps)
    small_gather.begin()
    out_mine.wait()
    chunks[0].begin()
    send_tokens()
    chunks[1].begin()
    landed(mix_swaps[3:6])
    chunks[2].begin()
    send_cot()
    small_gather.forward()
    small_gather.late()
    landed(mix_swaps[6:9])
    chunks[0].forward()
    make_table()
    chunks[1].forward()
    chunks[3].begin()
    landed(up_swaps)
    small_gather.finish()
    make_gains()
    make_turns()
    chunks[0].late()
    chunks[2].forward()
    chunks[1].late()
    landed([tok_sib])
    norm(1)
    chunks[3].forward()
    norm(0)
    chunks[4].begin()
    chunks[1].finish()
    chunks[0].finish()
    out_swap.start()
    chunks[5].begin()
    chunks[2].late()
    out_swap.wait_recv()
    landed([cot_sib])
    chunks[3].late()
    chunks[2].finish()
    chunks[6].begin()
    for copy in down_mine:
        copy.wait()
    chunks[3].finish()
    tok_fwd = links.plan(gp.at[2], gp.at[3], partial(place.member_id, 1))
    cot_fwd = links.plan(gs.at[2], gs.at[3], partial(place.member_id, 1))
    grad_here = outw.at[:, c, :, 1 - c]
    grad_swap = links.plan(grad_here, grad_here, partial(place.member_id, 1))
    first_up, second_up = up_sums

    def take_tokens():
        tok_far.wait_recv()
        tok_fwd.start()

    def take_cot():
        cot_far.wait_recv()
        cot_fwd.start()

    def free_out():
        chunks[0].drain()
        out_swap.wait_send()
        pl.semaphore_signal(
            out_free, inc=1, device_id=place.member_id(1), device_id_type=MESH_ID
        )

    def outer_out():
        part = dot_tn(gm[:, :, :, wide_mix:].reshape(rest, group), gs[...].reshape(rest, width))
        outw[:, c] = part.astype(LOW).reshape(ny, 2, 2, shard, width)
        pl.semaphore_wait(out_free, 1)
        grad_swap.start()

    def free_rows():
        for sem, r in ((sib_free, 1), (far_free, 2)):
            pl.semaphore_signal(sem, inc=1, device_id=place.member_id(r), device_id_type=MESH_ID)

    def await_rows():
        for sem in (sib_free, far_free):
            pl.semaphore_wait(sem, 1)

    def free_act():
        for one in [place.yid()] + [place.zid(step) for step in range(1, nz)]:
            pl.semaphore_signal(act_free, inc=1, device_id=one, device_id_type=MESH_ID)

    def sum_gains():
        gsum[...] = jnp.zeros_like(gsum)
        for k in range(4):
            gsum[k : k + 1, :] = jnp.sum(gacc[8 * k : 8 * k + 8, :], axis=0, keepdims=True)

    def drained(ones):
        for one in ones:
            one.drain()

    def rows_copy(sem, j, r, land):
        def copy(s, kind):
            buf = (feed, gxf)[kind]
            return pltpu.make_async_remote_copy(
                buf.at[j, s], land(kind, s), sem.at[0, kind, s], sem.at[1, kind, s],
                device_id=place.member_id(r), device_id_type=MESH_ID,
            )

        return copy

    sib_copy = rows_copy(sib_sems, 3, 1, lambda kind, s: gm.at[2 + kind, s])
    far_copy = rows_copy(far_sems, 2, 2, lambda kind, s: na.at[kind, s])
    own_copy = rows_copy(own_sems, 1, 1, lambda kind, s: gm.at[kind, s])

    def hand_on(j, s, value, kind):
        buf = (feed, gxf)[kind]

        @pl.when(j != 2)
        def _():
            buf[j, s] = value.astype(LOW)

        @pl.when(j == 3)
        def _():
            sib_copy(s, kind).start()

        @pl.when(j == 2)
        def _():
            sib_copy(s, kind).wait_recv()
            buf[j, s] = (value + gm[2 + kind, s].astype(WIDE)).astype(LOW)
            far_copy(s, kind).start()

        @pl.when(j == 1)
        def _():
            own_copy(s, kind).start()

    def grad_hidden(j, s):
        ga = dot_nt(gs[j, s, :, 0:half], down[0].reshape(2 * half, half))
        ga += dot_nt(gs[j, s, :, half : 2 * half], down[1].reshape(2 * half, half))
        gp[j, s] = (ga * gp[j, s].astype(WIDE)).astype(LOW)

    def rows_out_of(j, s):
        rows = act[j, s]
        sums = [dot_nn(rows, down[k].reshape(2 * half, half)) for k in range(2)]
        hand_on(j, s, jnp.concatenate(sums, axis=1) + feed[j, s].astype(WIDE), 0)

    def rows_back(j, s):
        gh = gp[j, s]
        gn = dot_nt(gh[:, :half], up[0].reshape(width, half))
        gn += dot_nt(gh[:, half:], up[1].reshape(width, half))
        gacc[16:24, :] += fold_rows(gn * xs[j, s].astype(WIDE))
        gacc[24:32, :] += fold_rows(gn)
        hand_on(j, s, gn * gains[2:3, :] + gxf[j, s].astype(WIDE), 1)

    def back_far(i, pump):
        j, s = 3 - i % 2, i // 2
        pump(0)
        rows_out_of(j, s)
        grad_hidden(j, s)
        rows_back(j, s)

    def back_own(i, pump):
        pump(0)
        grad_hidden(i // micro, i % micro)

    def rows_own(i, pump):
        j, s = 1 - i // micro, i % micro
        pump(0)
        rows_out_of(j, s)
        rows_back(j, s)

    def finish(s, carry):
        for kind in (0, 1):
            own_copy(s, kind).wait_recv()
            far_copy(s, kind).wait_recv()
        keep = spread_meta(0, s, 384, 512)[:, :1]
        values = xs[0, s].astype(WIDE)
        added = feed[0, s].astype(WIDE) + gm[0, s].astype(WIDE) + na[0, s].astype(WIDE)
        feed[0, s] = (values + keep * added).astype(LOW)
        grad = gxf[0, s].astype(WIDE) + gm[1, s].astype(WIDE) + na[1, s].astype(WIDE)
        center = values - jnp.mean(values, axis=1, keepdims=True)
        rate = lax.rsqrt(jnp.mean(center * center, axis=1, keepdims=True) + epsilon)
        hat = center * rate
        inner = jnp.mean(grad * hat, axis=1, keepdims=True)
        grad = grad - jnp.mean(grad, axis=1, keepdims=True) - hat * inner
        gxf[0, s] = (rate * grad).astype(LOW)
        return carry

    def put_up(k, qx, qc, values):
        rows = pl.ds(pl.multiple_of((k * 2 + qx) * shard, shard), shard)
        for bz in range(nz):
            first = (bz * 2 + qc) * feed_shard
            cols = pl.ds(pl.multiple_of(first, feed_shard), feed_shard)
            nf[0, 0, rows, cols] = values[:, bz * feed_shard : (bz + 1) * feed_shard]

    def put_mix(qx, qc, values):
        for t in range(3):
            for by in range(ny):
                first = ((by * 2 + qx) * 2 + qc) * pair
                cols = pl.ds(pl.multiple_of(first, pair), pair)
                nf[0, 1, t * shard : (t + 1) * shard, cols] = values[t, :, by * pair : (by + 1) * pair]

    def put_out(first, dst):
        count = dst.shape[1] // width
        return [
            local.start(nf.at[0, first, pl.ds(n * shard, shard)], dst.at[:, pl.ds(n * width, width)])
            for n in range(count)
        ]

    def share(hold, at, land):
        copies = []
        for r in (1, 2, 3):
            mx, mc = place.member(r)
            copies.append(links.start(at(hold, mx, mc), land.at[r - 1], place.member_id(r)))
        return copies

    def of_mix_share(hold, mx, mc):
        return hold.at[:, mx, mc]

    def of_up_share(hold, mx, mc):
        return hold.at[mx, pl.ds(pl.multiple_of(mc * shard, shard), shard)]

    def collect(copies, hold, at, land, put):
        put(x, c, at(hold, x, c)[...])
        for r in (1, 2, 3):
            mx, mc = place.member(r)
            copies[r - 1].wait_recv()
            put(mx, mc, land.at[r - 1][...])

    def keep_sum(hold):
        def emit(total):
            hold[...] = total.astype(LOW)

        return emit

    def finish_gains():
        totals = g3[...] + gm_sum[0] + gm_sum[1] + gm_sum[2]
        mine = ((y * 2 + x) * nz + z) * 2 + c
        pick_row = lax.broadcasted_iota(jnp.int32, (width, shard), 0) - mine * shard
        pick_col = lax.broadcasted_iota(jnp.int32, (width, shard), 1)
        gains_out[...] = lax.dot_general(
            totals, jnp.where(pick_row == pick_col, 1.0, 0.0), (((1,), (0,)), ((), ())),
            precision=lax.Precision.HIGHEST, preferred_element_type=WIDE,
        )

    chunks[4].forward()
    loop(
        0, 2, attend,
        {
            (0, 0): lambda: (chunks[7].begin(), chunks[5].forward()),
            (0, 2): lambda: (chunks[4].late(), take_tokens(), chunks[8].begin()),
            (1, 0): lambda: (chunks[5].late(), chunks[9].begin(), chunks[6].forward()),
            (1, 1): lambda: chunks[4].finish(),
            (1, 2): lambda: (chunks[6].late(), chunks[10].begin()),
        },
    )
    norm(2)
    landed([tok_fwd])
    norm(3)
    for copy in (tok_sib, tok_far, tok_fwd):
        copy.wait_send()
    chunks[5].finish()
    loop(
        0, 4 * micro, hidden(0),
        {
            (5, 0): lambda: chunks[7].forward(),
        },
    )
    chunks[8].forward()
    drained([chunks[i] for i in of_mix])
    chunks[11].begin()
    for copy in mix_swaps + up_swaps:
        copy.wait_send()
    free_out()
    loop(
        2, 4, attend,
        {
            (2, 0): lambda: (chunks[9].forward(), take_cot(), chunks[10].forward()),
            (2, 2): lambda: chunks[8].late(),
            (3, 0): lambda: (chunks[10].late(), chunks[11].forward()),
            (3, 1): lambda: (chunks[9].late(), cot_fwd.wait_recv(), chunks[7].late()),
            (3, 2): lambda: chunks[11].late(),
        },
    )
    outer_mix(0, blocks // 2)
    mix_sum.begin()
    outer_mix(blocks // 2, blocks)
    val_sum.begin()
    outer_out()
    chunks[6].finish()
    free_rows()
    chunks[7].finish()
    loop(
        0, 4 * micro, hidden(1),
        {
            (3, 0): lambda: chunks[10].finish(),
        },
    )
    landed([grad_swap])
    val_sum.hand_on()
    outer_down(0, blocks // 2)
    out_sum.begin()
    down_sum.begin()
    chunks[11].finish()
    mix_sum.turn(0)
    chunks[9].finish()
    chunks[8].finish()
    await_rows()
    loop(
        0, 2 * micro, back_far,
        {
            (1, 0): lambda: mix_sum.turn(1),
            (2, 0): lambda: (mix_sum.turn(2), outer_down(blocks // 2, blocks), mix_sum.turn(3)),
            (3, 0): lambda: out_sum.hand_on(),
        },
    )
    free_act()
    down_sum.turn(0)
    out_sum.turn()
    loop(
        0, 2 * micro, back_own,
        {
            (1, 0): lambda: val_sum.turn(),
            (2, 0): lambda: (mix_sum.hand_on(), down_sum.turn(1)),
        },
    )
    outer_up(0, blocks // 2)
    pl.semaphore_wait(act_free, nz)
    first_up.begin()
    outer_up(blocks // 2, blocks)
    down_sum.turn(2)
    down_sum.hand_on()
    loop(
        0, 2 * micro, rows_own,
        {
            (2, 0): lambda: first_up.turn(0),
            (3, 0): lambda: first_up.turn(1),
        },
    )
    links.drain()
    sum_gains()
    gain_y = links.start(gsum, gy, place.yid())
    second_up.begin()
    landed([gain_y])
    g2[...] = gsum[...] + gy[...]
    gain_zs = [links.start(g2, gz.at[step - 1], place.zid(step)) for step in range(1, nz)]
    first_up.turn(2)
    own_again = local.start(tok, xs.at[0])
    mix_sum.total(keep_sum(mix_send.at[two]))
    mix_send[2] = val_sum.total().astype(LOW)
    mix_shares = share(mix_send, of_mix_share, mix_recv)
    nf[1, 1, 0:shard, :] = out_sum.total().astype(LOW)
    written = [local.start(nf.at[1, 1, pl.ds(0, shard)], gout_out)]
    first_up.turn(3)
    down_sum.turn(3)
    drained(chunks + [small_gather])
    second_up.turn(0)
    second_up.turn(1)
    first_up.hand_on()
    second_up.turn(2)
    second_up.turn(3)
    own_again.wait()
    lax.fori_loop(0, micro, finish, 0)
    written.append(local.start(feed.at[0], out_rows))
    written.append(local.start(gxf.at[0], grad_rows))
    second_up.hand_on()
    down_sum.total(keep_sum(nf.at[1, 0, pl.ds(0, feed_shard)]))
    written.append(local.start(nf.at[1, 0, pl.ds(0, feed_shard)], gdown_out))
    first_up.total(keep_sum(up_send.at[0]))
    up_shares = [share(up_send.at[0], of_up_share, up_recv.at[0])]
    landed(gain_zs)
    g3[...] = g2[...] + sum(gz[step - 1] for step in range(1, nz))
    gain_ms = [links.start(g3, gm_sum.at[r - 1], place.member_id(r)) for r in (1, 2, 3)]
    collect(mix_shares, mix_send, of_mix_share, mix_recv, put_mix)
    written += put_out(1, gmix_out)
    second_up.total(keep_sum(up_send.at[1]))
    up_shares.append(share(up_send.at[1], of_up_share, up_recv.at[1]))
    drained([down_sum, first_up])
    collect(up_shares[0], up_send.at[0], of_up_share, up_recv.at[0], partial(put_up, 0))
    landed(gain_ms)
    finish_gains()
    drained([mix_sum, val_sum, out_sum])
    collect(up_shares[1], up_send.at[1], of_up_share, up_recv.at[1], partial(put_up, 1))
    written += put_out(0, gup_out)
    for copy in written:
        copy.wait()
    for copy in (cot_sib, cot_far, cot_fwd, grad_swap):
        copy.wait_send()
    links.drain()
    drained(chunks + up_sums + [small_gather, down_sum, mix_sum, val_sum, out_sum])
    for kind in (0, 1):
        for s in range(micro):
            sib_copy(s, kind).wait_send()
            far_copy(s, kind).wait_send()
            own_copy(s, kind).wait_send()


VMEM = pl.BlockSpec(memory_space=pltpu.VMEM)
SMEM = pl.BlockSpec(memory_space=pltpu.SMEM)
ANY = pl.BlockSpec(memory_space=pl.ANY)
SHAPE = jax.ShapeDtypeStruct
LIMIT = 59 * 2**20


def cosine_basis():
    order, sample = np.arange(HEAD)[:, None], np.arange(HEAD)[None, :]
    factor = np.where(order == 0, math.sqrt(1.0 / HEAD), math.sqrt(2.0 / HEAD))
    return (factor * np.cos(math.pi * (2 * sample + 1) * order / (2 * HEAD))).astype(np.float32)


def spread_rows():
    row = np.arange(64)[:, None]
    turn = np.where(row < 16, row, np.where((row >= 24) & (row < 56), (row - 24) % 16, -1))
    lane = np.arange(512)[None, :]
    part, dim = lane // 128, lane % HEAD
    half = ROT // 2
    cosine = (part == 0) & (dim < ROT) & (turn == dim % half)
    cosine = cosine | ((part == 0) & (dim >= ROT) & (row == 17))
    sine = (part == 1) & (dim < ROT) & (turn == half + dim % half)
    rest = ((part == 2) & (row == 16)) | ((part == 3) & (row == 18))
    sign = np.where((part == 1) & (dim < half), -1.0, 1.0)
    return np.where(cosine | sine | rest, sign, 0.0).astype(jnp.bfloat16)


def widen_kernel(
    rows, grads, cot, gains, mix, out, up, down,
    rows_out, grads_out, gain_one, bias_one, gain_two, bias_two, mix_out, out_out, up_out, down_out,
    rows_low, grads_low, cot_low, grads_wide, mix_low, mix_wide, out_low, out_wide,
    up_low, up_wide, down_low, down_wide, loaded, stored,
):
    parts = [(s, h) for s in range(rows.shape[0]) for h in range(2)]
    half = rows.shape[1] // 2
    weights = [
        (mix, mix_low, mix_wide, mix_out),
        (up, up_low, up_wide, up_out),
        (down, down_low, down_wide, down_out),
        (out, out_low, out_wide, out_out),
    ]
    copies = Locals(loaded)
    stores = Locals(stored)
    loads, written = [], []
    row_loads = [copies.start(rows.at[s], rows_low.at[s]) for s in range(rows.shape[0])]
    for s, h in parts:
        at = pl.ds(h * half, half)
        loads.append(
            (
                copies.start(grads.at[s, at], grads_low.at[s, at]),
                copies.start(cot.at[s, at], cot_low.at[s, at]),
            )
        )
    weight_loads = [copies.start(src, low) for src, low, _, _ in weights]
    for s, load in enumerate(row_loads):
        load.wait()
        written.append(stores.start(rows_low.at[s], rows_out.at[s]))
    for k, ref in enumerate((gain_one, bias_one, gain_two, bias_two)):
        ref[...] = gains[k : k + 1, :]
    for (s, h), pair in zip(parts, loads):
        for copy in pair:
            copy.wait()
        at = pl.ds(h * half, half)
        grads_wide[s, at] = cot_low[s, at].astype(WIDE) + grads_low[s, at].astype(WIDE)
        written.append(stores.start(grads_wide.at[s, at], grads_out.at[s, at]))
    for load, (_, low, wide, dst) in zip(weight_loads, weights):
        load.wait()
        wide[...] = low[...].astype(WIDE)
        written.append(stores.start(wide, dst))
    for copy in written:
        copy.wait()


def per_device_group(
    ny,
    nz,
    tokens,
    lengths,
    mix_weight,
    out_weight,
    up_weight,
    down_weight,
    attn_gain,
    attn_bias,
    feed_gain,
    feed_bias,
    feature_freq,
    feature_scale,
    cotangent,
):
    micro, span, width = tokens.shape
    shard = mix_weight.shape[0]
    feed_shard = down_weight.shape[0]
    group = width // 4
    hidden = feed_shard * ny * nz
    half = hidden // 2
    norms = [one[None] for one in (attn_gain, attn_bias, feed_gain, feed_bias)]

    dma = pltpu.SemaphoreType.DMA
    whole = pltpu.VMEM((4, micro, span, width), LOW)

    def low(*shape):
        return pltpu.VMEM(shape, LOW)

    def wide(*shape):
        return pltpu.VMEM(shape, WIDE)

    out_rows, grad_rows, gmix, gout, gup, gdown, gains = pl.pallas_call(
        partial(layer_kernel, ny, nz),
        out_shape=[
            SHAPE((micro, span, width), LOW),
            SHAPE((micro, span, width), LOW),
            SHAPE(mix_weight.shape, LOW),
            SHAPE(out_weight.shape, LOW),
            SHAPE(up_weight.shape, LOW),
            SHAPE(down_weight.shape, LOW),
            SHAPE((8, shard), WIDE),
        ],
        in_specs=[SMEM] + [ANY] * 14,
        out_specs=[ANY] * 6 + [VMEM],
        scratch_shapes=[whole] * 9
        + [
            low(2, ny, 2, nz, 2, shard, half),
            low(2, ny, nz, feed_shard, half),
            low(3, ny, 2, nz, 2, shard, group),
            low(ny, nz // 2, 2, 2, shard, width),
            wide(ny, 2, nz, 2, 8, 128),
            wide(8, width),
            low(4, micro, 64, span),
            low(group, group),
            wide(8, group),
            low(4, 1, shard),
            wide(HEAD, HEAD),
            wide(1, HEAD),
            wide(HEAD, HEAD),
            low(64, 512),
            low(ny, nz, feed_shard, width),
            low(nz, feed_shard, width),
            low(4, feed_shard, width),
            low(nz, 2, 2, 2, shard, group),
            low(4, 2, 2, 2, shard, group),
            low(4, ny, 2, 2, shard, group),
            low(ny, 2, 2, shard, group),
            low(2, 2, shard, group),
            low(4, ny, shard, width),
            low(ny, shard, width),
            low(shard, width),
            low(2, 2, 2 * shard, half),
            low(2, 3, shard, half),
            low(3, 2, 2, shard, group),
            low(3, 3, shard, group),
            wide(32, width),
            wide(8, width),
            wide(8, width),
            wide(8, width),
            wide(nz - 1, 8, width),
            wide(8, width),
            wide(3, 8, width),
            dma((240,)),
            dma((240,)),
            dma((36,)),
            dma((2, 2, 2)),
            dma((2, 2, 2)),
            dma((2, 2, 2)),
            pltpu.SemaphoreType.REGULAR,
            pltpu.SemaphoreType.REGULAR,
            pltpu.SemaphoreType.REGULAR,
            pltpu.SemaphoreType.REGULAR,
        ],
        name="layer",
        cost_estimate=pl.CostEstimate(flops=45 * 10**9, bytes_accessed=20 * 10**6, transcendentals=0),
        compiler_params=pltpu.CompilerParams(
            collective_id=0, has_side_effects=True, vmem_limit_bytes=LIMIT
        ),
    )(
        lengths[:, 0], tokens, cotangent, mix_weight, out_weight, up_weight, down_weight, *norms,
        feature_freq, feature_scale[None], cosine_basis(), spread_rows(),
    )
    shapes = [w.shape for w in (mix_weight, out_weight, up_weight, down_weight)]
    one = SHAPE((1, shard), WIDE)
    results = pl.pallas_call(
        widen_kernel,
        out_shape=[SHAPE(out_rows.shape, LOW), SHAPE(out_rows.shape, WIDE), one, one, one, one]
        + [SHAPE(shape, WIDE) for shape in shapes],
        in_specs=[ANY] * 3 + [VMEM] + [ANY] * 4,
        out_specs=[ANY] * 2 + [VMEM] * 4 + [ANY] * 4,
        scratch_shapes=[low(*out_rows.shape)] * 3
        + [wide(*out_rows.shape)]
        + [kind(*shape) for shape in shapes[:2] for kind in (low, wide)]
        + [kind(*shape) for shape in shapes[2:] for kind in (low, wide)]
        + [dma((16,)), dma((16,))],
        name="widen",
    )(out_rows, grad_rows, cotangent, gains, gmix, gout, gup, gdown)
    rows, grads, *norm_grads = results[:6]
    return (rows, grads, *results[6:], *(part.reshape(shard) for part in norm_grads))


def solution(mesh):
    ny, nz = mesh.shape["dp"] // 2, mesh.shape["fsdp"] // 2
    grouped = ny == 2 and nz == 4 and D // mesh.size % 32 == 0
    body = partial(per_device_group, ny, nz) if grouped else per_device_plain
    rows = P(("dp", "fsdp"), None)
    vector = P(("dp", "fsdp"))
    slots = P(None, ("dp", "fsdp"), None)
    return jax.shard_map(
        body,
        mesh=mesh,
        in_specs=(slots, slots, *[rows] * 4, *[vector] * 4, P(), P(), slots),
        out_specs=(slots, slots, *[rows] * 4, *[vector] * 4),
        check_vma=False,
    )
```

```python
from functools import partial
import math

import jax
import jax.numpy as jnp
import numpy as np
from jax import lax
from jax.experimental import pallas as pl
from jax.experimental.pallas import tpu as pltpu
from jax.sharding import PartitionSpec as P

D = 1024
HEAD = 64
ROT = 16


epsilon = 1e-05
exact_precision = lax.Precision.HIGHEST


def dct_matrix(width):
    order = jnp.arange(width, dtype=jnp.float32)[:, None]
    sample = jnp.arange(width, dtype=jnp.float32)[None, :]
    factor = jnp.where(order == 0, jnp.sqrt(1.0 / width), jnp.sqrt(2.0 / width))
    return factor * jnp.cos(math.pi * (2.0 * sample + 1.0) * order / (2.0 * width))


def feature_table(feature_freq):
    table = jnp.dot(dct_matrix(HEAD).T, feature_freq.T, precision=exact_precision) / math.sqrt(HEAD)
    return table.astype(jnp.bfloat16)


def slot_layout(span_table, slot_len):
    seg_ends = jnp.cumsum(span_table, axis=-1)
    seg_starts = seg_ends - span_table
    places = jnp.arange(slot_len, dtype=jnp.int32)
    segment = jnp.sum((places[:, None] >= seg_ends[..., None, :]).astype(jnp.int32), axis=-1)
    numbers = jnp.arange(span_table.shape[-1], dtype=jnp.int32)
    matched = segment[..., None] == numbers
    begin_at = jnp.sum(jnp.where(matched, seg_starts[..., None, :], 0), axis=-1)
    begin_at = begin_at + jnp.where(segment == span_table.shape[-1], seg_ends[..., -1:], 0)
    position = (places - begin_at).astype(jnp.float32)
    valid = (segment < span_table.shape[-1]).astype(jnp.float32)
    return (segment, position, valid)


def rotate(raw_heads, position):
    half_rot = ROT // 2
    inverse = 10000.0 ** (-2.0 * jnp.arange(half_rot, dtype=jnp.float32) / ROT)
    angle = position[..., None] * inverse
    cosine_wave = jnp.cos(angle)[..., None, :]
    sine = jnp.sin(angle)[..., None, :]
    first = raw_heads[..., :half_rot]
    second = raw_heads[..., half_rot:ROT]
    return jnp.concatenate(
        [
            first * cosine_wave - second * sine,
            second * cosine_wave + first * sine,
            raw_heads[..., ROT:],
        ],
        axis=-1,
    )


def feature_map(raw_heads, position, table, feature_scale):
    rotated_rows = rotate(raw_heads, position).astype(jnp.bfloat16)
    pre = jnp.einsum("shd,df->shf", rotated_rows, table, preferred_element_type=jnp.float32)
    return feature_scale * jnp.exp(pre)


def feature_back(raw_heads, grad_phi, position, table, feature_scale):
    phi = feature_map(raw_heads, position, table, feature_scale)
    grad_pre = (grad_phi * phi).astype(jnp.bfloat16)
    grad_turned = jnp.einsum("shf,df->shd", grad_pre, table, preferred_element_type=jnp.float32)
    _, turn_pull = jax.vjp(lambda values: rotate(values, position), raw_heads)
    return turn_pull(grad_turned)[0]


def norm_apply(inputs, gain, shift):
    center = inputs - jnp.mean(inputs, axis=-1, keepdims=True)
    spread = jnp.mean(center * center, axis=-1, keepdims=True)
    return center * lax.rsqrt(spread + epsilon) * gain + shift


def head_major(values):
    return jnp.swapaxes(values, 0, 1)


def attend_head(allowed, pieces):
    mapped_query, mapped_key, value_rows = pieces
    score_matrix = jnp.einsum(
        "qf,kf->qk", mapped_query, mapped_key, preferred_element_type=jnp.float32
    )
    score_matrix = jnp.where(allowed, score_matrix, 0.0)
    totals = jnp.sum(score_matrix, axis=1)
    numerator = jnp.dot(
        score_matrix.astype(jnp.bfloat16), value_rows, preferred_element_type=jnp.float32
    )
    return numerator / totals[:, None]


def attend_back(allowed, pieces):
    mapped_query, mapped_key, value_rows, grad_heads = pieces
    score_matrix = jnp.einsum(
        "qf,kf->qk", mapped_query, mapped_key, preferred_element_type=jnp.float32
    )
    score_matrix = jnp.where(allowed, score_matrix, 0.0)
    totals = jnp.sum(score_matrix, axis=1)
    scores_low = score_matrix.astype(jnp.bfloat16)
    numerator = jnp.dot(scores_low, value_rows, preferred_element_type=jnp.float32)
    grad_numer = (grad_heads / totals[:, None]).astype(jnp.bfloat16)
    grad_totals = -jnp.sum(grad_heads * numerator, axis=1) / (totals * totals)
    grad_scores = jnp.einsum(
        "qd,kd->qk", grad_numer, value_rows, preferred_element_type=jnp.float32
    )
    grad_scores = jnp.where(allowed, grad_scores + grad_totals[:, None], 0.0).astype(jnp.bfloat16)
    grad_query = jnp.dot(grad_scores, mapped_key, preferred_element_type=jnp.float32)
    grad_key = jnp.einsum(
        "qk,qf->kf", grad_scores, mapped_query, preferred_element_type=jnp.float32
    )
    grad_value = jnp.einsum("qk,qd->kd", scores_low, grad_numer, preferred_element_type=jnp.float32)
    return (grad_query, grad_key, grad_value)


def fetch_attention(shards):
    return (
        lax.all_gather(shards[0], ("dp", "fsdp"), axis=0, tiled=True),
        lax.all_gather(shards[1], ("dp", "fsdp"), axis=0, tiled=True),
        lax.all_gather(shards[2], ("dp", "fsdp"), axis=0, tiled=True),
        lax.all_gather(shards[3], ("dp", "fsdp"), axis=0, tiled=True),
    )


def fetch_feed(shards):
    return (
        lax.all_gather(shards[0], ("dp", "fsdp"), axis=0, tiled=True),
        lax.all_gather(shards[1], ("dp", "fsdp"), axis=0, tiled=True),
        lax.all_gather(shards[2], ("dp", "fsdp"), axis=0, tiled=True),
        lax.all_gather(shards[3], ("dp", "fsdp"), axis=0, tiled=True),
    )


def reduce_attention(grads):
    return (
        lax.psum_scatter(grads[0], ("dp", "fsdp"), scatter_dimension=0, tiled=True),
        lax.psum_scatter(grads[1], ("dp", "fsdp"), scatter_dimension=0, tiled=True),
        lax.psum_scatter(grads[2], ("dp", "fsdp"), scatter_dimension=0, tiled=True),
        lax.psum_scatter(grads[3], ("dp", "fsdp"), scatter_dimension=0, tiled=True),
    )


def reduce_feed(grads):
    return (
        lax.psum_scatter(grads[0], ("dp", "fsdp"), scatter_dimension=0, tiled=True),
        lax.psum_scatter(grads[1], ("dp", "fsdp"), scatter_dimension=0, tiled=True),
        lax.psum_scatter(grads[2], ("dp", "fsdp"), scatter_dimension=0, tiled=True),
        lax.psum_scatter(grads[3], ("dp", "fsdp"), scatter_dimension=0, tiled=True),
    )


def add_tuples(running, update):
    if running is None:
        return tuple(update)
    return tuple(jax.tree.map(jnp.add, tuple(running), tuple(update)))


def per_device_plain(
    tokens,
    lengths,
    mix_weight,
    out_weight,
    up_weight,
    down_weight,
    attn_gain,
    attn_bias,
    feed_gain,
    feed_bias,
    feature_freq,
    feature_scale,
    cotangent,
):
    table = feature_table(feature_freq)
    slot_len = tokens.shape[1]
    head_count = D // HEAD
    attn_shards = (mix_weight, out_weight, attn_gain, attn_bias)
    feed_shards = (up_weight, down_weight, feed_gain, feed_bias)
    places = jnp.arange(slot_len, dtype=jnp.int32)
    output_rows = []
    grad_inputs = []
    attn_total = None
    feed_total = None
    for micro_index in range(tokens.shape[0]):
        attn_full = fetch_attention(attn_shards)
        feed_full = fetch_feed(feed_shards)
        mix_full, out_full, gain_one, bias_one = attn_full
        up_full, down_full, gain_two, bias_two = feed_full
        gain_attn = gain_one.astype(jnp.float32)
        shift_attn = bias_one.astype(jnp.float32)
        gain_feed = gain_two.astype(jnp.float32)
        shift_feed = bias_two.astype(jnp.float32)
        inputs = tokens[micro_index].astype(jnp.float32)
        segment, position, valid = slot_layout(lengths[micro_index, 0], slot_len)
        allowed = (segment[:, None] == segment[None, :]) & (places[None, :] <= places[:, None])
        normed_attn = norm_apply(inputs, gain_attn, shift_attn).astype(jnp.bfloat16)
        normed_feed = norm_apply(inputs, gain_feed, shift_feed).astype(jnp.bfloat16)
        mixed = jnp.dot(normed_attn, mix_full, preferred_element_type=jnp.float32)
        mixed = mixed.reshape(slot_len, 3, head_count, HEAD)
        query_raw = mixed[:, 0]
        key_raw = mixed[:, 1]
        value_rows = mixed[:, 2].astype(jnp.bfloat16)
        mapped_query = feature_map(query_raw, position, table, feature_scale).astype(jnp.bfloat16)
        mapped_key = feature_map(key_raw, position, table, feature_scale).astype(jnp.bfloat16)
        attended = lax.map(
            partial(attend_head, allowed),
            (head_major(mapped_query), head_major(mapped_key), head_major(value_rows)),
        )
        attended = head_major(attended).reshape(slot_len, D).astype(jnp.bfloat16)
        attn_rows = jnp.dot(attended, out_full, preferred_element_type=jnp.float32)
        hidden = jnp.dot(normed_feed, up_full, preferred_element_type=jnp.float32)
        active = jax.nn.gelu(hidden, approximate=False).astype(jnp.bfloat16)
        feed_rows = jnp.dot(active, down_full, preferred_element_type=jnp.float32)
        result = inputs + valid[:, None] * (attn_rows + feed_rows)
        output_rows.append(result.astype(jnp.bfloat16))
        attn_full = fetch_attention(attn_shards)
        feed_full = fetch_feed(feed_shards)
        mix_full, out_full, gain_one, bias_one = attn_full
        up_full, down_full, gain_two, bias_two = feed_full
        grad_rows = cotangent[micro_index]
        grad_branch = jnp.where(valid[:, None] > 0.0, grad_rows, jnp.zeros_like(grad_rows))
        grad_down = jnp.einsum("sf,sd->fd", active, grad_branch, preferred_element_type=jnp.float32)
        grad_out = jnp.einsum(
            "sd,se->de", attended, grad_branch, preferred_element_type=jnp.float32
        )
        grad_active = jnp.einsum(
            "sd,fd->sf", grad_branch, down_full, preferred_element_type=jnp.float32
        )
        _, gelu_pull = jax.vjp(partial(jax.nn.gelu, approximate=False), hidden)
        grad_hidden = gelu_pull(grad_active)[0].astype(jnp.bfloat16)
        grad_up = jnp.einsum(
            "sd,sf->df", normed_feed, grad_hidden, preferred_element_type=jnp.float32
        )
        grad_normed_feed = jnp.einsum(
            "sf,df->sd", grad_hidden, up_full, preferred_element_type=jnp.float32
        )
        grad_attended = jnp.einsum(
            "sd,ed->se", grad_branch, out_full, preferred_element_type=jnp.float32
        )
        grad_attended = grad_attended.reshape(slot_len, head_count, HEAD)
        grad_phi_q, grad_phi_k, grad_value = lax.map(
            partial(attend_back, allowed),
            (
                head_major(mapped_query),
                head_major(mapped_key),
                head_major(value_rows),
                head_major(grad_attended),
            ),
        )
        grad_query = feature_back(query_raw, head_major(grad_phi_q), position, table, feature_scale)
        grad_key = feature_back(key_raw, head_major(grad_phi_k), position, table, feature_scale)
        grad_mixed = jnp.stack([grad_query, grad_key, head_major(grad_value)], axis=1)
        grad_mixed = grad_mixed.reshape(slot_len, 3 * D).astype(jnp.bfloat16)
        grad_mix = jnp.einsum(
            "sd,se->de", normed_attn, grad_mixed, preferred_element_type=jnp.float32
        )
        grad_normed_attn = jnp.einsum(
            "se,de->sd", grad_mixed, mix_full, preferred_element_type=jnp.float32
        )
        _, attn_norm_pull = jax.vjp(norm_apply, inputs, gain_attn, shift_attn)
        grad_in_one, grad_gain_one, grad_bias_one = attn_norm_pull(grad_normed_attn)
        _, feed_norm_pull = jax.vjp(norm_apply, inputs, gain_feed, shift_feed)
        grad_in_two, grad_gain_two, grad_bias_two = feed_norm_pull(grad_normed_feed)
        grad_inputs.append(grad_rows.astype(jnp.float32) + grad_in_one + grad_in_two)
        attn_grads = (grad_mix, grad_out, grad_gain_one, grad_bias_one)
        feed_grads = (grad_up, grad_down, grad_gain_two, grad_bias_two)
        attn_grads = reduce_attention(attn_grads)
        feed_grads = reduce_feed(feed_grads)
        attn_total = add_tuples(attn_total, attn_grads)
        feed_total = add_tuples(feed_total, feed_grads)
    return (
        jnp.stack(output_rows),
        jnp.stack(grad_inputs),
        attn_total[0],
        attn_total[1],
        feed_total[0],
        feed_total[1],
        attn_total[2],
        attn_total[3],
        feed_total[2],
        feed_total[3],
    )


MESH_ID = pl.DeviceIdType.MESH
LOW = jnp.bfloat16
WIDE = jnp.float32


def here(nz):
    dp = lax.axis_index("dp")
    fs = lax.axis_index("fsdp")
    return dp // 2, dp % 2, fs // 2, fs % 2


class Places:
    def __init__(self, ny, nz):
        self.ny, self.nz = ny, nz
        self.y, self.x, self.z, self.c = here(nz)

    def at(self, y, x, z, c):
        return (y * 2 + x, z * 2 + c)

    def member(self, r):
        x = 1 - self.x if r & 2 else self.x
        c = 1 - self.c if r & 1 else self.c
        return x, c

    def member_id(self, r):
        x, c = self.member(r)
        return self.at(self.y, x, self.z, c)

    def yid(self):
        return self.at(1 - self.y, self.x, self.z, self.c)

    def zid(self, step):
        return self.at(self.y, self.x, (self.z + step) % self.nz, self.c)

    def zsrc(self, step):
        return (self.z + self.nz - step) % self.nz

    def signal(self):
        barrier = pltpu.get_barrier_semaphore()
        ids = [self.member_id(r) for r in (1, 2, 3)] + [self.yid()]
        ids += [self.zid(step) for step in range(1, self.nz)]
        for one in ids:
            pl.semaphore_signal(barrier, inc=1, device_id=one, device_id_type=MESH_ID)

    def meet(self):
        pl.semaphore_wait(pltpu.get_barrier_semaphore(), self.nz + 3)


class Copy:
    def __init__(self, describe):
        self.describe, self.sent = describe, False

    def start(self):
        self.describe().start()

    def wait_recv(self):
        self.describe().wait_recv()

    def wait_send(self):
        if not self.sent:
            self.describe().wait_send()
            self.sent = True


class Links:
    def __init__(self, send, recv):
        self.send, self.recv, self.count, self.open = send, recv, 0, []

    def plan(self, src, dst, device):
        i = self.count
        self.count += 1

        def describe():
            return pltpu.make_async_remote_copy(
                src() if callable(src) else src,
                dst() if callable(dst) else dst,
                self.send.at[i],
                self.recv.at[i],
                device_id=device() if callable(device) else device,
                device_id_type=MESH_ID,
            )

        return Copy(describe)

    def start(self, src, dst, device):
        copy = self.plan(src, dst, device)
        copy.start()
        self.open.append(copy)
        return copy

    def drain(self):
        for copy in self.open:
            copy.wait_send()


class Locals:
    def __init__(self, sems):
        self.sems, self.count = sems, 0

    def start(self, src, dst):
        copy = pltpu.make_async_copy(src, dst, self.sems.at[self.count])
        self.count += 1
        copy.start()
        return copy


class Line:
    def __init__(self, place):
        z = place.z
        self.place = place
        self.way = 1 - 2 * (z // 2)
        self.inner = (z // 2) * (3 - z) + (1 - z // 2) * z

    def off(self, end, inner):
        return self.place.z + self.way * ((1 - self.inner) * end + self.inner * inner)

    def near(self):
        return self.off(1, -1)

    def second(self):
        return self.off(2, 1)

    def third(self):
        return self.off(3, 2)

    def id(self, z):
        return self.place.at(self.place.y, self.place.x, z, self.place.c)

    def at_end(self, event):
        pl.when(self.inner == 0)(event)

    def at_inner(self, event):
        pl.when(self.inner == 1)(event)


class Spread:
    def __init__(self, links, line, block, own=None):
        z = line.place.z
        mine = own if own is not None else lambda: block(z)

        def here():
            return block(z)

        def second():
            return block(line.second())

        def third():
            return block(line.third())

        self.line = line
        self.sources = [line.near, line.second, line.third]
        self.beside = links.plan(mine, here, lambda: line.id(line.near()))
        self.across = links.plan(mine, here, lambda: line.id(line.second()))
        self.far = links.plan(mine, here, lambda: line.id(line.second()))
        self.hand_second = links.plan(second, second, lambda: line.id(line.near()))
        self.hand_third = links.plan(third, third, lambda: line.id(line.near()))

    def begin(self):
        self.beside.start()
        self.line.at_inner(self.across.start)
        self.line.at_end(self.far.start)

    def arrive_near(self, then=None):
        self.beside.wait_recv()
        if then:
            then[0].start()

    def arrive_inner(self, then=None):
        @self.line.at_inner
        def _():
            self.across.wait_recv()
            self.hand_second.start()
            if then:
                then[1].start()
            self.far.wait_recv()
            self.hand_third.start()
            if then:
                then[2].start()

    def arrive_end(self, then=None):
        @self.line.at_end
        def _():
            self.hand_second.wait_recv()
            if then:
                then[1].start()
            self.hand_third.wait_recv()
            if then:
                then[2].start()

    def drain(self):
        self.beside.wait_send()

        @self.line.at_inner
        def _():
            for copy in (self.across, self.hand_second, self.hand_third):
                copy.wait_send()

        self.line.at_end(self.far.wait_send)


class Direct:
    def __init__(self, links, line, block, own=None):
        place = line.place
        self.sources = [partial(place.zsrc, step) for step in range(1, place.nz)]
        mine = own if own is not None else lambda: block(place.z)
        self.copies = [
            links.plan(mine, lambda: block(place.z), partial(place.zid, step))
            for step in range(1, place.nz)
        ]

    def begin(self):
        for copy in self.copies:
            copy.start()

    def arrive_near(self, then=()):
        for k, copy in enumerate(self.copies):
            copy.wait_recv()
            if then:
                then[k].start()

    def arrive_inner(self, then=None):
        pass

    def arrive_end(self, then=None):
        pass

    def drain(self):
        for copy in self.copies:
            copy.wait_send()


class Gather:
    def __init__(self, links, place, line, block, own=None, way=Spread):
        def plane(z):
            return block(place.y, z)

        self.spread = way(links, line, plane, own)
        mine = own if own is not None else lambda: plane(place.z)
        self.cross = links.plan(mine, lambda: plane(place.z), place.yid)
        self.cross_on = [
            links.plan(lambda at=at: plane(at()), lambda at=at: plane(at()), place.yid)
            for at in self.spread.sources
        ]

    def begin(self):
        self.spread.begin()
        self.cross.start()

    def forward(self):
        self.spread.arrive_near(self.cross_on)
        self.spread.arrive_inner(self.cross_on)

    def late(self):
        self.spread.arrive_end(self.cross_on)

    def finish(self):
        for copy in [self.cross] + self.cross_on:
            copy.wait_recv()

    def drain(self):
        self.spread.drain()
        for copy in [self.cross] + self.cross_on:
            copy.wait_send()


class GatherCross:
    def __init__(self, links, place, line, block, own=None, way=Spread):
        def plane(z):
            return block(place.y, z)

        def other(z):
            return block(1 - place.y, z)

        mine = own if own is not None else lambda: plane(place.z)
        self.cross = links.plan(mine, lambda: plane(place.z), place.yid)
        self.spread = way(links, line, plane, own)
        self.spread_other = way(links, line, other)

    def begin(self):
        self.cross.start()
        self.spread.begin()

    def forward(self):
        self.cross.wait_recv()
        self.spread_other.begin()
        self.spread.arrive_near()
        self.spread.arrive_inner()

    def late(self):
        self.spread.arrive_end()
        self.spread_other.arrive_near()
        self.spread_other.arrive_inner()

    def finish(self):
        self.spread_other.arrive_end()

    def drain(self):
        self.cross.wait_send()
        self.spread.drain()
        self.spread_other.drain()


def dot_nn(a, b):
    return jnp.dot(a, b, preferred_element_type=WIDE)


def dot_nt(a, b):
    return lax.dot_general(a, b, (((1,), (1,)), ((), ())), preferred_element_type=WIDE)


def dot_tn(a, b):
    return lax.dot_general(a, b, (((0,), (0,)), ((), ())), preferred_element_type=WIDE)


def fold_rows(values):
    rows, cols = values.shape
    return jnp.sum(values.reshape(rows // 8, 8, cols), axis=0)


class Fold:
    def __init__(self, links, line, block, land):
        self.line, self.block, self.land = line, block, land

        def to(at, where, slot):
            return links.plan(lambda: block(at()), lambda: land(slot), lambda: line.id(where()))

        self.beside = to(line.near, line.near, 0)
        self.across = to(line.second, line.second, 1)
        self.far = to(line.second, line.second, 2)
        self.hand = to(line.third, line.near, 3)
        self.handed = to(line.third, line.third, 1)

    def send(self, k):
        if k == 0:
            self.line.at_inner(self.across.start)
            self.line.at_end(self.far.start)
        if k == 1:
            self.line.at_end(self.hand.start)
        if k == 2:
            self.beside.start()

    def hand_on(self):
        @self.line.at_inner
        def _():
            self.hand.wait_recv()
            block = self.block(self.line.third())
            block[...] = (block[...].astype(WIDE) + self.land(3)[...].astype(WIDE)).astype(LOW)
            self.handed.start()

    def total(self, own, emit):
        self.beside.wait_recv()

        @self.line.at_end
        def _():
            self.handed.wait_recv()
            emit(own() + self.land(0)[...].astype(WIDE) + self.land(1)[...].astype(WIDE))

        @self.line.at_inner
        def _():
            self.across.wait_recv()
            self.far.wait_recv()
            total = own() + self.land(0)[...].astype(WIDE) + self.land(1)[...].astype(WIDE)
            emit(total + self.land(2)[...].astype(WIDE))

    def drain(self):
        self.beside.wait_send()

        @self.line.at_inner
        def _():
            self.across.wait_send()
            self.handed.wait_send()

        @self.line.at_end
        def _():
            self.far.wait_send()
            self.hand.wait_send()


class Scatter:
    def __init__(self, links, place, line, theirs, mine, ybuf, zbuf):
        self.place, self.line, self.mine, self.ybuf = place, line, mine, ybuf
        self.order = [line.second, line.third, line.near, lambda: place.z]
        self.ys = [
            links.plan(lambda at=at: theirs(at()), lambda at=at: ybuf(at()), place.yid)
            for at in self.order
        ]
        self.fold = Fold(links, line, ybuf, zbuf)

    def begin(self):
        for copy in self.ys:
            copy.start()

    def turn(self, k):
        self.ys[k].wait_recv()
        if k < 3:
            at = self.order[k]()
            land = self.ybuf(at)
            land[...] = (land[...].astype(WIDE) + self.mine(at)[...].astype(WIDE)).astype(LOW)
        self.fold.send(k)

    def hand_on(self):
        self.fold.hand_on()

    def total(self, emit):
        z = self.place.z
        self.fold.total(
            lambda: self.ybuf(z)[...].astype(WIDE) + self.mine(z)[...].astype(WIDE), emit
        )

    def drain(self):
        for copy in self.ys:
            copy.wait_send()
        self.fold.drain()


class ScatterCross:
    def __init__(self, links, place, line, parts, zbuf, hold, land):
        self.place, self.parts, self.hold, self.land = place, parts, hold, land
        self.fold = Fold(links, line, parts, zbuf)
        self.cross = links.plan(lambda: hold.at[1 - place.y], lambda: land, place.yid)

    def begin(self):
        for k in range(3):
            self.fold.send(k)

    def hand_on(self):
        self.fold.hand_on()

    def turn(self):
        def emit(total):
            self.hold[...] = total.astype(LOW)

        self.fold.total(lambda: self.parts(self.place.z)[...].astype(WIDE), emit)
        self.cross.start()

    def total(self):
        self.cross.wait_recv()
        return self.hold[self.place.y].astype(WIDE) + self.land[...].astype(WIDE)

    def drain(self):
        self.cross.wait_send()
        self.fold.drain()


def layer_kernel(
    ny, nz,
    lens, tok, cot, mix_w, out_w, up_w, down_w, gain_a, bias_a, gain_f, bias_f, freq_in, scale_ref, dct_in, spread_in,
    out_rows, grad_rows, gmix_out, gout_out, gup_out, gdown_out, gains_out,
    xs, gs, nf, na, act, gp, feed, gxf, gm,
    up, down, mix, outw, small, gains, meta, table, scale, norms, freq, scale_in, dct, spread,
    gdown, ydown, zdown, ymix, zmix,
    zval, hval, yval, zout, hout, yout,
    up_send, up_recv, mix_send, mix_recv, gacc, gsum, gy, g2, gz, g3, gm_sum,
    send, recv, sems, sib_sems, own_sems, far_sems, out_free, sib_free, far_free, act_free,
):
    place = Places(ny, nz)
    y, x, z, c = place.y, place.x, place.z, place.c
    me = x * 2 + c
    micro, span, width = xs.shape[1:]
    shard = out_w.shape[0]
    feed_shard = down_w.shape[0]
    half = up.shape[-1]
    quarter = half // 2
    heads = width // HEAD // 4
    group = heads * HEAD
    none = jnp.zeros((), LOW)
    local = Locals(sems)

    def raw(n):
        return feed.at[3, 0, pl.ds(n * shard, shard)]

    def raw_load(weight, first):
        count = weight.shape[1] // width
        return [
            local.start(weight.at[:, pl.ds(n * width, width)], raw(first + n)) for n in range(count)
        ]

    norms_load = [
        local.start(src, norms.at[k]) for k, src in enumerate((gain_a, bias_a, gain_f, bias_f))
    ]
    mix_load = raw_load(mix_w, 0)
    up_load = raw_load(up_w, len(mix_load))
    out_mine = local.start(out_w, outw.at[y, z // 2, z % 2, c])
    tok_mine = local.start(tok, gp.at[0])
    cot_mine = local.start(cot, gs.at[0])
    down_mine = [
        local.start(down_w.at[:, pl.ds(k * half, half)], down.at[k, y, z]) for k in range(2)
    ]
    place.signal()
    table_loads = [
        local.start(src, dst)
        for src, dst in ((freq_in, freq), (scale_ref, scale_in), (dct_in, dct), (spread_in, spread))
    ]

    row = lax.broadcasted_iota(jnp.int32, (8, 128), 0)
    lane = lax.broadcasted_iota(jnp.int32, (8, 128), 1)
    facts = jnp.zeros((8, 128), WIDE)
    for s in range(micro):
        for k in range(lens.shape[1]):
            facts = jnp.where((row == 1 + s) & (lane == k), lens[s, k].astype(WIDE), facts)
    for copy in norms_load:
        copy.wait()
    at_row = lax.broadcasted_iota(jnp.int32, (shard, 128), 0)
    at_lane = lax.broadcasted_iota(jnp.int32, (shard, 128), 1)
    for k in range(4):
        pick = jnp.where(at_lane == at_row + k * shard, 1.0, 0.0).astype(LOW)
        facts = jnp.where(row == 0, facts + dot_nn(norms[k], pick), facts)
    small[y, x, z, c] = facts

    def up_stage(q):
        return gdown.at[:, q, pl.ds(0, shard), pl.ds(0, half)]

    def mix_stage(t, q):
        return gdown.at[0, q, pl.ds((t + 1) * shard, shard), pl.ds(half, group)]

    def raw_cols(base, first, count):
        at = first % width
        return raw(base + first // width)[:, at : at + count]

    for copy in mix_load:
        copy.wait()
    pair = group // ny
    for q in range(4):
        for t in range(3):
            for by in range(ny):
                first = t * width + ((by * 2 + q // 2) * 2 + q % 2) * pair
                mix_stage(t, q)[:, by * pair : (by + 1) * pair] = raw_cols(0, first, pair)
    for t in range(3):
        mix[t, y, x, z, c] = mix_stage(t, me)[...]
    place.meet()
    links = Links(send, recv)
    line = Line(place)

    def swap(src, dst):
        copies = []
        for r in (1, 2, 3):
            mx, mc = place.member(r)
            copies.append(links.start(src(mx * 2 + mc), dst, place.member_id(r)))
        return copies

    def landed(copies):
        for copy in copies:
            copy.wait_recv()

    small_swaps = swap(lambda q: small.at[y, x, z, c], small.at[y, x, z, c])
    mix_swaps = []
    for t in range(3):
        mix_swaps += swap(lambda q, t=t: mix_stage(t, q), mix.at[t, y, x, z, c])
    for copy in up_load:
        copy.wait()
    for q in range(4):
        for by in range(ny):
            for bz in range(nz):
                first = (((by * 2 + q // 2) * nz + bz) * 2 + q % 2) * feed_shard
                cols = slice(bz * feed_shard, (bz + 1) * feed_shard)
                up_stage(q)[by, :, cols] = raw_cols(len(mix_load), first, feed_shard)
    up[:, y, x, z, c] = up_stage(me)[...]
    up_swaps = swap(up_stage, up.at[:, y, x, z, c])
    chunks = [GatherCross(links, place, line, lambda by, bz: outw.at[by, bz // 2, bz % 2, c])]
    for t in range(3):
        chunks.append(Gather(links, place, line, lambda by, bz, t=t: mix.at[t, by, :, bz]))
    halves = [(k, pl.ds(h * quarter, quarter)) for k in range(2) for h in range(2)]
    for k, cols in halves:
        chunks.append(
            Gather(
                links, place, line,
                lambda by, bz, k=k, cols=cols: up.at[k, by, :, bz, :, :, cols],
            )
        )
    for k, cols in halves:
        way = GatherCross if (k, cols) == halves[-1] else Gather
        chunks.append(
            way(links, place, line, lambda by, bz, k=k, cols=cols: down.at[k, by, bz, :, cols])
        )
    of_mix, of_up, of_down = range(1, 4), range(4, 8), range(8, 12)
    ahead = 3
    hurried = [3]

    def turn_chunk(i):
        chunks[i].forward()
        if i and i - 1 not in hurried:
            chunks[i - 1].late()
        if i + ahead < len(chunks):
            chunks[i + ahead].begin()

    small_gather = Gather(links, place, line, lambda by, bz: small.at[by, :, bz])
    tok_sib = links.plan(gp.at[0], gp.at[1], partial(place.member_id, 1))
    tok_far = links.plan(gp.at[0], gp.at[2], partial(place.member_id, 2))
    cot_sib = links.plan(gs.at[0], gs.at[1], partial(place.member_id, 1))
    cot_far = links.plan(gs.at[0], gs.at[2], partial(place.member_id, 2))

    def send_tokens():
        tok_mine.wait()
        tok_sib.start()
        tok_far.start()

    def send_cot():
        cot_mine.wait()
        at_place = lax.broadcasted_iota(jnp.int32, (span, 1), 0)
        for s in range(micro):
            used = lens[s, 0]
            for k in range(1, lens.shape[1]):
                used = used + lens[s, k]
            gs[0, s] = jnp.where(at_place < used, gs[0, s], none)
        cot_sib.start()
        cot_far.start()

    def make_table():
        for copy in table_loads:
            copy.wait()
        raw = lax.dot_general(
            dct[...], freq[...], (((0,), (1,)), ((), ())),
            precision=lax.Precision.HIGHEST, preferred_element_type=WIDE,
        ) / math.sqrt(HEAD)
        raw = raw.astype(LOW)
        tile_row = lax.broadcasted_iota(jnp.int32, (HEAD, group), 0)
        tile_col = lax.broadcasted_iota(jnp.int32, (HEAD, group), 1)
        tiled = jnp.where(tile_col % HEAD == tile_row, 1.0, 0.0).astype(LOW)
        wide_table = dot_tn(tiled, dot_nn(raw, tiled).astype(LOW))
        block_row = lax.broadcasted_iota(jnp.int32, (group, group), 0) // HEAD
        block_col = lax.broadcasted_iota(jnp.int32, (group, group), 1) // HEAD
        table[...] = jnp.where(block_row == block_col, wide_table, 0.0).astype(LOW)
        scale[...] = lax.dot_general(
            jnp.broadcast_to(scale_in[...], (8, HEAD)), tiled.astype(WIDE), (((1,), (0,)), ((), ())),
            precision=lax.Precision.HIGHEST, preferred_element_type=WIDE,
        )

    def make_gains():
        count = ny * 2 * nz * 2
        packed = jnp.sum(jnp.where(row == 0, small[...].reshape(count, 8, 128), 0.0), axis=1)
        packed = packed.astype(LOW)
        pick_row = lax.broadcasted_iota(jnp.int32, (128, width), 0)
        pick_col = lax.broadcasted_iota(jnp.int32, (128, width), 1) % shard
        owner = lax.broadcasted_iota(jnp.int32, (count, width), 0)
        owned = lax.broadcasted_iota(jnp.int32, (count, width), 1) // shard
        for k in range(4):
            pick = jnp.where(pick_row == pick_col + k * shard, 1.0, 0.0).astype(LOW)
            part = jnp.where(owned == owner, dot_nn(packed, pick), 0.0)
            gains[k : k + 1, :] = jnp.sum(part, axis=0, keepdims=True)
        gacc[...] = jnp.zeros_like(gacc)

    def make_turns():
        places = lax.broadcasted_iota(jnp.int32, (1, span), 1).astype(WIDE)
        turn_row = lax.broadcasted_iota(jnp.int32, (ROT // 2, 1), 0)
        inverse = jnp.zeros((ROT // 2, 1), WIDE)
        for k in range(ROT // 2):
            inverse = jnp.where(turn_row == k, 10000.0 ** (-2.0 * k / ROT), inverse)
        fact_row = lax.broadcasted_iota(jnp.int32, (8, span), 0)
        for r in range(4):
            mx, mc = place.member(r)
            facts = small[y, mx, z, mc]
            for s in range(micro):
                end = jnp.zeros((1, 1), WIDE)
                segment = jnp.zeros((1, span), WIDE)
                begin = jnp.zeros((1, span), WIDE)
                for k in range(lens.shape[1]):
                    end = end + facts[1 + s : 2 + s, k : k + 1]
                    past = places >= end
                    segment = segment + jnp.where(past, 1.0, 0.0)
                    begin = jnp.where(past, end, begin)
                angle = inverse * (places - begin)
                valid = jnp.where(segment < lens.shape[1], 1.0, 0.0)
                rest = jnp.where(fact_row == 0, segment, jnp.where(fact_row == 1, 1.0, 0.0))
                rest = jnp.where(fact_row == 2, valid, rest)
                left = jnp.concatenate([jnp.cos(angle), jnp.sin(angle)], axis=0)
                for first in (0, 24, 40):
                    part = left.astype(LOW)
                    left = left - part.astype(WIDE)
                    meta[r, s, first : first + 16, :] = part
                meta[r, s, 16:24, :] = rest.astype(LOW)
                meta[r, s, 56:64, :] = jnp.zeros((8, span), LOW)

    def norm(j):
        def body(i, carry):
            s = i // (span // 128)
            rs = pl.ds(pl.multiple_of(i % (span // 128) * 128, 128), 128)
            values = gp[j, s, rs, :].astype(WIDE)
            center = values - jnp.mean(values, axis=1, keepdims=True)
            deviation = jnp.mean(center * center, axis=1, keepdims=True)
            hat = center * lax.rsqrt(deviation + epsilon)
            na[j, s, rs, :] = (hat * gains[0:1, :] + gains[1:2, :]).astype(LOW)
            nf[j, s, rs, :] = (hat * gains[2:3, :] + gains[3:4, :]).astype(LOW)
            xs[j, s, rs, :] = hat.astype(LOW)
            return carry

        lax.fori_loop(0, micro * span // 128, body, 0)

    def loop(first, last, body, events):
        def step(i, carry):
            def pump(part):
                for (at, which), event in events.items():
                    if which == part:

                        @pl.when(i == at)
                        def _(event=event):
                            event()

            body(i, pump)
            return carry

        lax.fori_loop(first, last, step, 0)

    head_lane = lax.broadcasted_iota(jnp.int32, (1, group), 1)
    of_head = [head_lane // HEAD == h for h in range(heads)]
    low_lane = lax.broadcasted_iota(jnp.int32, (1, 128), 1) % HEAD < ROT // 2
    key_at = lax.broadcasted_iota(jnp.int32, (span, span), 1)
    query_at = lax.broadcasted_iota(jnp.int32, (span, span), 0)
    wide_mix = 3 * group

    def turn(values, cosine, sine):
        parts = []
        for first in range(0, group, 128):
            part = values[:, first : first + 128]
            other = jnp.where(
                low_lane, pltpu.roll(part, 128 - ROT // 2, 1), pltpu.roll(part, ROT // 2, 1)
            )
            parts.append(part * cosine + other * sine)
        return jnp.concatenate(parts, axis=1)

    def spread_meta(j, s, first, last):
        return dot_tn(meta[j, s], spread[:, first:last])

    def attend_forward(j, s):
        rows = na[j, s]
        turns = spread_meta(j, s, 0, 384)
        cosine, sine, owner = turns[:, :128], turns[:, 128:256], turns[:, 256:384]
        owner = jnp.concatenate([owner, owner], axis=1)
        allowed = (owner == meta[j, s, 16:24, :][0:1, :].astype(WIDE)) & (key_at <= query_at)
        query, key, value = (dot_nn(rows, mix[t].reshape(width, group)) for t in range(3))
        query = turn(query, cosine, sine).astype(LOW)
        key = turn(key, cosine, sine).astype(LOW)
        value = value.astype(LOW)
        raised_query = scale[0:1, :] * jnp.exp(dot_nn(query, table[...]))
        raised_key = scale[0:1, :] * jnp.exp(dot_nn(key, table[...]))
        phi_query = raised_query.astype(LOW)
        phi_key = raised_key.astype(LOW)
        scores, totals = [], []
        total = jnp.zeros((span, group), WIDE)
        for h in range(heads):
            score = dot_nt(jnp.where(of_head[h], phi_query, none), phi_key)
            score = jnp.where(allowed, score, 0.0)
            totals.append(jnp.sum(score, axis=1, keepdims=True))
            scores.append(score.astype(LOW))
            total = jnp.where(of_head[h], totals[h], total)
        values = jnp.concatenate([jnp.where(one, value, none) for one in of_head], axis=0)
        numer = dot_nn(jnp.concatenate(scores, axis=1), values)
        att = (numer / total).astype(LOW)
        gm[j, s, :, wide_mix:] = att
        return (att, cosine, sine, allowed, raised_query, raised_key, phi_query, phi_key, value,
                scores, totals, numer, total)

    def attend_back(j, s, kept):
        (att, cosine, sine, allowed, raised_query, raised_key, phi_query, phi_key, value,
         scores, totals, numer, total) = kept
        feed[j, s] = dot_nn(att, outw[:, c].reshape(group, width)).astype(LOW)
        grad_att = dot_nt(gs[j, s], outw[:, c].reshape(group, width))
        grad_numer = (grad_att / total).astype(LOW)
        product = grad_att * numer
        grad_scores, numers = [], []
        for h in range(heads):
            grad_total = -jnp.sum(jnp.where(of_head[h], product, 0.0), axis=1, keepdims=True)
            grad_total = grad_total / (totals[h] * totals[h])
            numers.append(jnp.where(of_head[h], grad_numer, none))
            grad_score = dot_nt(numers[h], value) + grad_total
            grad_scores.append(jnp.where(allowed, grad_score, 0.0).astype(LOW))
        keys = jnp.concatenate([jnp.where(one, phi_key, none) for one in of_head], axis=0)
        queries = jnp.concatenate([jnp.where(one, phi_query, none) for one in of_head], axis=0)
        grad_query = dot_nn(jnp.concatenate(grad_scores, axis=1), keys)
        grad_key = dot_tn(jnp.concatenate(grad_scores, axis=0), queries)
        grad_value = dot_tn(jnp.concatenate(scores, axis=0), jnp.concatenate(numers, axis=0))
        back_query = turn(
            dot_nt((grad_query * raised_query).astype(LOW), table[...]), cosine, -sine
        )
        back_key = turn(dot_nt((grad_key * raised_key).astype(LOW), table[...]), cosine, -sine)
        parts = (back_query.astype(LOW), back_key.astype(LOW), grad_value.astype(LOW))
        for t in range(3):
            gm[j, s, :, t * group : (t + 1) * group] = parts[t]
        weights = jnp.concatenate([mix[t].reshape(width, group) for t in range(3)], axis=1)
        grad_normed = dot_nt(jnp.concatenate(parts, axis=1), weights)
        gacc[0:8, :] += fold_rows(grad_normed * xs[j, s].astype(WIDE))
        gacc[8:16, :] += fold_rows(grad_normed)
        gxf[j, s] = (grad_normed * gains[0:1, :]).astype(LOW)

    def attend(j, pump):
        kept = []
        for s in range(micro):
            kept.append(attend_forward(j, s))
            pump(s)
        for s in range(micro):
            attend_back(j, s, kept[s])
            pump(micro + s)

    def hidden(k):
        def body(i, pump):
            j, s = i // micro, i % micro
            pump(0)
            h = dot_nn(nf[j, s], up[k].reshape(width, half))
            cdf = 0.5 * (1.0 + lax.erf(h * math.sqrt(0.5)))
            pdf = jnp.exp(-0.5 * h * h) * (1.0 / math.sqrt(2.0 * math.pi))
            act[j, s, :, pl.ds(k * half, half)] = (h * cdf).astype(LOW)
            gp[j, s, :, pl.ds(k * half, half)] = (cdf + h * pdf).astype(LOW)

        return body

    rest = 4 * micro * span
    blocks = width // 256

    def other_first(i):
        return (i + (1 - y) * (blocks // 2)) % blocks

    def outer(a, b, first, last, store):
        def body(i, carry):
            at = other_first(i)
            cols = pl.ds(pl.multiple_of(at * 256, 256), 256)
            store(at, dot_tn(a[:, :, :, cols].reshape(rest, 256), b().reshape(rest, -1)))
            return carry

        lax.fori_loop(first, last, body, 0)

    def keep_down(at, part):
        per = 256 // feed_shard
        for k in range(per):
            block = at * per + k
            rows = slice(k * feed_shard, (k + 1) * feed_shard)
            gdown[block // nz, block % nz] = part[rows].astype(LOW)

    def keep_up(at, part):
        na[2 + at // 2, at % 2] = part.astype(LOW)

    def up_block(ref, j, at, cols):
        size = 2 * shard
        return ref.at[j, :, pl.ds(pl.multiple_of(at * size, size), size), cols]

    def keep_mix(at, part):
        for t in range(3):
            cols = part[:, t * group : (t + 1) * group].astype(LOW)
            mix[t, at // 2, at % 2] = cols.reshape(nz, 2, shard, group)

    def outer_down(first, last):
        outer(act, lambda: gs[...], first, last, keep_down)

    def outer_up(first, last):
        outer(nf, lambda: gp[...], first, last, keep_up)

    def outer_mix(first, last):
        outer(na, lambda: gm[:, :, :, 0:wide_mix], first, last, keep_mix)

    down_sum = Scatter(
        links, place, line, lambda at: gdown.at[1 - y, at], lambda at: gdown.at[y, at],
        lambda at: ydown.at[at], lambda k: zdown.at[k],
    )
    up_sums = []
    for k in range(2):
        cols = pl.ds(k * half, half)
        up_sums.append(
            Scatter(
                links, place, line,
                lambda at, cols=cols: up_block(na, 3 - y, at, cols),
                lambda at, cols=cols: up_block(na, 2 + y, at, cols),
                lambda at, cols=cols: up_block(act, 2, at, cols),
                lambda at, cols=cols: up_block(act, 3, at, cols),
            )
        )
    two = pl.ds(0, 2)
    mix_sum = Scatter(
        links, place, line, lambda at: mix.at[two, 1 - y, :, at],
        lambda at: mix.at[two, y, :, at], lambda at: ymix.at[at], lambda k: zmix.at[k],
    )
    val_sum = ScatterCross(
        links, place, line, lambda at: mix.at[2, :, :, at], lambda k: zval.at[k], hval, yval
    )
    out_sum = ScatterCross(
        links, place, line, lambda at: outw.at[:, at // 2, at % 2, c], lambda k: zout.at[k],
        hout, yout,
    )

    out_here = outw.at[:, 1 - c, :, c]
    out_swap = links.plan(out_here, out_here, partial(place.member_id, 1))
    landed(mix_swaps[0:3])
    landed(small_swaps)
    small_gather.begin()
    out_mine.wait()
    chunks[0].begin()
    send_tokens()
    chunks[1].begin()
    landed(mix_swaps[3:6])
    chunks[2].begin()
    send_cot()
    small_gather.forward()
    small_gather.late()
    landed(mix_swaps[6:9])
    chunks[0].forward()
    make_table()
    chunks[1].forward()
    chunks[3].begin()
    landed(up_swaps)
    small_gather.finish()
    make_gains()
    make_turns()
    chunks[0].late()
    chunks[2].forward()
    chunks[1].late()
    landed([tok_sib])
    norm(1)
    chunks[3].forward()
    norm(0)
    chunks[4].begin()
    chunks[1].finish()
    chunks[0].finish()
    out_swap.start()
    chunks[5].begin()
    chunks[2].late()
    out_swap.wait_recv()
    landed([cot_sib])
    chunks[3].late()
    chunks[2].finish()
    chunks[6].begin()
    for copy in down_mine:
        copy.wait()
    chunks[3].finish()
    tok_fwd = links.plan(gp.at[2], gp.at[3], partial(place.member_id, 1))
    cot_fwd = links.plan(gs.at[2], gs.at[3], partial(place.member_id, 1))
    grad_here = outw.at[:, c, :, 1 - c]
    grad_swap = links.plan(grad_here, grad_here, partial(place.member_id, 1))
    first_up, second_up = up_sums

    def take_tokens():
        tok_far.wait_recv()
        tok_fwd.start()

    def take_cot():
        cot_far.wait_recv()
        cot_fwd.start()

    def free_out():
        chunks[0].drain()
        out_swap.wait_send()
        pl.semaphore_signal(
            out_free, inc=1, device_id=place.member_id(1), device_id_type=MESH_ID
        )

    def outer_out():
        part = dot_tn(gm[:, :, :, wide_mix:].reshape(rest, group), gs[...].reshape(rest, width))
        outw[:, c] = part.astype(LOW).reshape(ny, 2, 2, shard, width)
        pl.semaphore_wait(out_free, 1)
        grad_swap.start()

    def free_rows():
        for sem, r in ((sib_free, 1), (far_free, 2)):
            pl.semaphore_signal(sem, inc=1, device_id=place.member_id(r), device_id_type=MESH_ID)

    def await_rows():
        for sem in (sib_free, far_free):
            pl.semaphore_wait(sem, 1)

    def free_act():
        for one in [place.yid()] + [place.zid(step) for step in range(1, nz)]:
            pl.semaphore_signal(act_free, inc=1, device_id=one, device_id_type=MESH_ID)

    def sum_gains():
        gsum[...] = jnp.zeros_like(gsum)
        for k in range(4):
            gsum[k : k + 1, :] = jnp.sum(gacc[8 * k : 8 * k + 8, :], axis=0, keepdims=True)

    def drained(ones):
        for one in ones:
            one.drain()

    def rows_copy(sem, j, r, land):
        def copy(s, kind):
            buf = (feed, gxf)[kind]
            return pltpu.make_async_remote_copy(
                buf.at[j, s], land(kind, s), sem.at[0, kind, s], sem.at[1, kind, s],
                device_id=place.member_id(r), device_id_type=MESH_ID,
            )

        return copy

    sib_copy = rows_copy(sib_sems, 3, 1, lambda kind, s: gm.at[2 + kind, s])
    far_copy = rows_copy(far_sems, 2, 2, lambda kind, s: na.at[kind, s])
    own_copy = rows_copy(own_sems, 1, 1, lambda kind, s: gm.at[kind, s])

    def hand_on(j, s, value, kind):
        buf = (feed, gxf)[kind]

        @pl.when(j != 2)
        def _():
            buf[j, s] = value.astype(LOW)

        @pl.when(j == 3)
        def _():
            sib_copy(s, kind).start()

        @pl.when(j == 2)
        def _():
            sib_copy(s, kind).wait_recv()
            buf[j, s] = (value + gm[2 + kind, s].astype(WIDE)).astype(LOW)
            far_copy(s, kind).start()

        @pl.when(j == 1)
        def _():
            own_copy(s, kind).start()

    def grad_hidden(j, s):
        ga = dot_nt(gs[j, s, :, 0:half], down[0].reshape(2 * half, half))
        ga += dot_nt(gs[j, s, :, half : 2 * half], down[1].reshape(2 * half, half))
        gp[j, s] = (ga * gp[j, s].astype(WIDE)).astype(LOW)

    def rows_out_of(j, s):
        rows = act[j, s]
        sums = [dot_nn(rows, down[k].reshape(2 * half, half)) for k in range(2)]
        hand_on(j, s, jnp.concatenate(sums, axis=1) + feed[j, s].astype(WIDE), 0)

    def rows_back(j, s):
        gh = gp[j, s]
        gn = dot_nt(gh[:, :half], up[0].reshape(width, half))
        gn += dot_nt(gh[:, half:], up[1].reshape(width, half))
        gacc[16:24, :] += fold_rows(gn * xs[j, s].astype(WIDE))
        gacc[24:32, :] += fold_rows(gn)
        hand_on(j, s, gn * gains[2:3, :] + gxf[j, s].astype(WIDE), 1)

    def back_far(i, pump):
        j, s = 3 - i % 2, i // 2
        pump(0)
        rows_out_of(j, s)
        grad_hidden(j, s)
        rows_back(j, s)

    def back_own(i, pump):
        pump(0)
        grad_hidden(i // micro, i % micro)

    def rows_own(i, pump):
        j, s = 1 - i // micro, i % micro
        pump(0)
        rows_out_of(j, s)
        rows_back(j, s)

    def finish(s, carry):
        for kind in (0, 1):
            own_copy(s, kind).wait_recv()
            far_copy(s, kind).wait_recv()
        keep = spread_meta(0, s, 384, 512)[:, :1]
        values = xs[0, s].astype(WIDE)
        added = feed[0, s].astype(WIDE) + gm[0, s].astype(WIDE) + na[0, s].astype(WIDE)
        feed[0, s] = (values + keep * added).astype(LOW)
        grad = gxf[0, s].astype(WIDE) + gm[1, s].astype(WIDE) + na[1, s].astype(WIDE)
        center = values - jnp.mean(values, axis=1, keepdims=True)
        rate = lax.rsqrt(jnp.mean(center * center, axis=1, keepdims=True) + epsilon)
        hat = center * rate
        inner = jnp.mean(grad * hat, axis=1, keepdims=True)
        grad = grad - jnp.mean(grad, axis=1, keepdims=True) - hat * inner
        gxf[0, s] = (rate * grad).astype(LOW)
        return carry

    def put_up(k, qx, qc, values):
        rows = pl.ds(pl.multiple_of((k * 2 + qx) * shard, shard), shard)
        for bz in range(nz):
            first = (bz * 2 + qc) * feed_shard
            cols = pl.ds(pl.multiple_of(first, feed_shard), feed_shard)
            nf[0, 0, rows, cols] = values[:, bz * feed_shard : (bz + 1) * feed_shard]

    def put_mix(qx, qc, values):
        for t in range(3):
            for by in range(ny):
                first = ((by * 2 + qx) * 2 + qc) * pair
                cols = pl.ds(pl.multiple_of(first, pair), pair)
                nf[0, 1, t * shard : (t + 1) * shard, cols] = values[t, :, by * pair : (by + 1) * pair]

    def put_out(first, dst):
        count = dst.shape[1] // width
        return [
            local.start(nf.at[0, first, pl.ds(n * shard, shard)], dst.at[:, pl.ds(n * width, width)])
            for n in range(count)
        ]

    def share(hold, at, land):
        copies = []
        for r in (1, 2, 3):
            mx, mc = place.member(r)
            copies.append(links.start(at(hold, mx, mc), land.at[r - 1], place.member_id(r)))
        return copies

    def of_mix_share(hold, mx, mc):
        return hold.at[:, mx, mc]

    def of_up_share(hold, mx, mc):
        return hold.at[mx, pl.ds(pl.multiple_of(mc * shard, shard), shard)]

    def collect(copies, hold, at, land, put):
        put(x, c, at(hold, x, c)[...])
        for r in (1, 2, 3):
            mx, mc = place.member(r)
            copies[r - 1].wait_recv()
            put(mx, mc, land.at[r - 1][...])

    def keep_sum(hold):
        def emit(total):
            hold[...] = total.astype(LOW)

        return emit

    def finish_gains():
        totals = g3[...] + gm_sum[0] + gm_sum[1] + gm_sum[2]
        mine = ((y * 2 + x) * nz + z) * 2 + c
        pick_row = lax.broadcasted_iota(jnp.int32, (width, shard), 0) - mine * shard
        pick_col = lax.broadcasted_iota(jnp.int32, (width, shard), 1)
        gains_out[...] = lax.dot_general(
            totals, jnp.where(pick_row == pick_col, 1.0, 0.0), (((1,), (0,)), ((), ())),
            precision=lax.Precision.HIGHEST, preferred_element_type=WIDE,
        )

    chunks[4].forward()
    loop(
        0, 2, attend,
        {
            (0, 0): lambda: (chunks[7].begin(), chunks[5].forward()),
            (0, 2): lambda: (chunks[4].late(), take_tokens(), chunks[8].begin()),
            (1, 0): lambda: (chunks[5].late(), chunks[9].begin(), chunks[6].forward()),
            (1, 1): lambda: chunks[4].finish(),
            (1, 2): lambda: (chunks[6].late(), chunks[10].begin()),
        },
    )
    norm(2)
    landed([tok_fwd])
    norm(3)
    for copy in (tok_sib, tok_far, tok_fwd):
        copy.wait_send()
    chunks[5].finish()
    loop(
        0, 4 * micro, hidden(0),
        {
            (5, 0): lambda: chunks[7].forward(),
        },
    )
    chunks[8].forward()
    drained([chunks[i] for i in of_mix])
    chunks[11].begin()
    for copy in mix_swaps + up_swaps:
        copy.wait_send()
    free_out()
    loop(
        2, 4, attend,
        {
            (2, 0): lambda: (chunks[9].forward(), take_cot(), chunks[10].forward()),
            (2, 2): lambda: chunks[8].late(),
            (3, 0): lambda: (chunks[10].late(), chunks[11].forward()),
            (3, 1): lambda: (chunks[9].late(), cot_fwd.wait_recv(), chunks[7].late()),
            (3, 2): lambda: chunks[11].late(),
        },
    )
    outer_mix(0, blocks // 2)
    mix_sum.begin()
    outer_mix(blocks // 2, blocks)
    val_sum.begin()
    outer_out()
    chunks[6].finish()
    free_rows()
    chunks[7].finish()
    loop(
        0, 4 * micro, hidden(1),
        {
            (3, 0): lambda: chunks[10].finish(),
        },
    )
    landed([grad_swap])
    val_sum.hand_on()
    outer_down(0, blocks // 2)
    out_sum.begin()
    down_sum.begin()
    chunks[11].finish()
    mix_sum.turn(0)
    chunks[9].finish()
    chunks[8].finish()
    await_rows()
    loop(
        0, 2 * micro, back_far,
        {
            (1, 0): lambda: mix_sum.turn(1),
            (2, 0): lambda: (mix_sum.turn(2), outer_down(blocks // 2, blocks), mix_sum.turn(3)),
            (3, 0): lambda: out_sum.hand_on(),
        },
    )
    free_act()
    down_sum.turn(0)
    out_sum.turn()
    loop(
        0, 2 * micro, back_own,
        {
            (1, 0): lambda: val_sum.turn(),
            (2, 0): lambda: (mix_sum.hand_on(), down_sum.turn(1)),
        },
    )
    outer_up(0, blocks // 2)
    pl.semaphore_wait(act_free, nz)
    first_up.begin()
    outer_up(blocks // 2, blocks)
    down_sum.turn(2)
    down_sum.hand_on()
    loop(
        0, 2 * micro, rows_own,
        {
            (2, 0): lambda: first_up.turn(0),
            (3, 0): lambda: first_up.turn(1),
        },
    )
    links.drain()
    sum_gains()
    gain_y = links.start(gsum, gy, place.yid())
    second_up.begin()
    landed([gain_y])
    g2[...] = gsum[...] + gy[...]
    gain_zs = [links.start(g2, gz.at[step - 1], place.zid(step)) for step in range(1, nz)]
    first_up.turn(2)
    own_again = local.start(tok, xs.at[0])
    mix_sum.total(keep_sum(mix_send.at[two]))
    mix_send[2] = val_sum.total().astype(LOW)
    mix_shares = share(mix_send, of_mix_share, mix_recv)
    nf[1, 1, 0:shard, :] = out_sum.total().astype(LOW)
    written = [local.start(nf.at[1, 1, pl.ds(0, shard)], gout_out)]
    first_up.turn(3)
    down_sum.turn(3)
    drained(chunks + [small_gather])
    second_up.turn(0)
    second_up.turn(1)
    first_up.hand_on()
    second_up.turn(2)
    second_up.turn(3)
    own_again.wait()
    lax.fori_loop(0, micro, finish, 0)
    written.append(local.start(feed.at[0], out_rows))
    written.append(local.start(gxf.at[0], grad_rows))
    second_up.hand_on()
    down_sum.total(keep_sum(nf.at[1, 0, pl.ds(0, feed_shard)]))
    written.append(local.start(nf.at[1, 0, pl.ds(0, feed_shard)], gdown_out))
    first_up.total(keep_sum(up_send.at[0]))
    up_shares = [share(up_send.at[0], of_up_share, up_recv.at[0])]
    landed(gain_zs)
    g3[...] = g2[...] + sum(gz[step - 1] for step in range(1, nz))
    gain_ms = [links.start(g3, gm_sum.at[r - 1], place.member_id(r)) for r in (1, 2, 3)]
    collect(mix_shares, mix_send, of_mix_share, mix_recv, put_mix)
    written += put_out(1, gmix_out)
    second_up.total(keep_sum(up_send.at[1]))
    up_shares.append(share(up_send.at[1], of_up_share, up_recv.at[1]))
    drained([down_sum, first_up])
    collect(up_shares[0], up_send.at[0], of_up_share, up_recv.at[0], partial(put_up, 0))
    landed(gain_ms)
    finish_gains()
    drained([mix_sum, val_sum, out_sum])
    collect(up_shares[1], up_send.at[1], of_up_share, up_recv.at[1], partial(put_up, 1))
    written += put_out(0, gup_out)
    for copy in written:
        copy.wait()
    for copy in (cot_sib, cot_far, cot_fwd, grad_swap):
        copy.wait_send()
    links.drain()
    drained(chunks + up_sums + [small_gather, down_sum, mix_sum, val_sum, out_sum])
    for kind in (0, 1):
        for s in range(micro):
            sib_copy(s, kind).wait_send()
            far_copy(s, kind).wait_send()
            own_copy(s, kind).wait_send()


VMEM = pl.BlockSpec(memory_space=pltpu.VMEM)
SMEM = pl.BlockSpec(memory_space=pltpu.SMEM)
ANY = pl.BlockSpec(memory_space=pl.ANY)
SHAPE = jax.ShapeDtypeStruct
LIMIT = 59 * 2**20


def cosine_basis():
    order, sample = np.arange(HEAD)[:, None], np.arange(HEAD)[None, :]
    factor = np.where(order == 0, math.sqrt(1.0 / HEAD), math.sqrt(2.0 / HEAD))
    return (factor * np.cos(math.pi * (2 * sample + 1) * order / (2 * HEAD))).astype(np.float32)


def spread_rows():
    row = np.arange(64)[:, None]
    turn = np.where(row < 16, row, np.where((row >= 24) & (row < 56), (row - 24) % 16, -1))
    lane = np.arange(512)[None, :]
    part, dim = lane // 128, lane % HEAD
    half = ROT // 2
    cosine = (part == 0) & (dim < ROT) & (turn == dim % half)
    cosine = cosine | ((part == 0) & (dim >= ROT) & (row == 17))
    sine = (part == 1) & (dim < ROT) & (turn == half + dim % half)
    rest = ((part == 2) & (row == 16)) | ((part == 3) & (row == 18))
    sign = np.where((part == 1) & (dim < half), -1.0, 1.0)
    return np.where(cosine | sine | rest, sign, 0.0).astype(jnp.bfloat16)


def widen_kernel(
    rows, grads, cot, gains, mix, out, up, down,
    rows_out, grads_out, gain_one, bias_one, gain_two, bias_two, mix_out, out_out, up_out, down_out,
    rows_low, grads_low, cot_low, grads_wide, mix_low, mix_wide, out_low, out_wide,
    up_low, up_wide, down_low, down_wide, loaded, stored,
):
    parts = [(s, h) for s in range(rows.shape[0]) for h in range(2)]
    half = rows.shape[1] // 2
    weights = [
        (mix, mix_low, mix_wide, mix_out),
        (up, up_low, up_wide, up_out),
        (down, down_low, down_wide, down_out),
        (out, out_low, out_wide, out_out),
    ]
    copies = Locals(loaded)
    stores = Locals(stored)
    loads, written = [], []
    row_loads = [copies.start(rows.at[s], rows_low.at[s]) for s in range(rows.shape[0])]
    for s, h in parts:
        at = pl.ds(h * half, half)
        loads.append(
            (
                copies.start(grads.at[s, at], grads_low.at[s, at]),
                copies.start(cot.at[s, at], cot_low.at[s, at]),
            )
        )
    weight_loads = [copies.start(src, low) for src, low, _, _ in weights]
    for s, load in enumerate(row_loads):
        load.wait()
        written.append(stores.start(rows_low.at[s], rows_out.at[s]))
    for k, ref in enumerate((gain_one, bias_one, gain_two, bias_two)):
        ref[...] = gains[k : k + 1, :]
    for (s, h), pair in zip(parts, loads):
        for copy in pair:
            copy.wait()
        at = pl.ds(h * half, half)
        grads_wide[s, at] = cot_low[s, at].astype(WIDE) + grads_low[s, at].astype(WIDE)
        written.append(stores.start(grads_wide.at[s, at], grads_out.at[s, at]))
    for load, (_, low, wide, dst) in zip(weight_loads, weights):
        load.wait()
        wide[...] = low[...].astype(WIDE)
        written.append(stores.start(wide, dst))
    for copy in written:
        copy.wait()


def per_device_group(
    ny,
    nz,
    tokens,
    lengths,
    mix_weight,
    out_weight,
    up_weight,
    down_weight,
    attn_gain,
    attn_bias,
    feed_gain,
    feed_bias,
    feature_freq,
    feature_scale,
    cotangent,
):
    micro, span, width = tokens.shape
    shard = mix_weight.shape[0]
    feed_shard = down_weight.shape[0]
    group = width // 4
    hidden = feed_shard * ny * nz
    half = hidden // 2
    norms = [one[None] for one in (attn_gain, attn_bias, feed_gain, feed_bias)]

    dma = pltpu.SemaphoreType.DMA
    whole = pltpu.VMEM((4, micro, span, width), LOW)

    def low(*shape):
        return pltpu.VMEM(shape, LOW)

    def wide(*shape):
        return pltpu.VMEM(shape, WIDE)

    out_rows, grad_rows, gmix, gout, gup, gdown, gains = pl.pallas_call(
        partial(layer_kernel, ny, nz),
        out_shape=[
            SHAPE((micro, span, width), LOW),
            SHAPE((micro, span, width), LOW),
            SHAPE(mix_weight.shape, LOW),
            SHAPE(out_weight.shape, LOW),
            SHAPE(up_weight.shape, LOW),
            SHAPE(down_weight.shape, LOW),
            SHAPE((8, shard), WIDE),
        ],
        in_specs=[SMEM] + [ANY] * 14,
        out_specs=[ANY] * 6 + [VMEM],
        scratch_shapes=[whole] * 9
        + [
            low(2, ny, 2, nz, 2, shard, half),
            low(2, ny, nz, feed_shard, half),
            low(3, ny, 2, nz, 2, shard, group),
            low(ny, nz // 2, 2, 2, shard, width),
            wide(ny, 2, nz, 2, 8, 128),
            wide(8, width),
            low(4, micro, 64, span),
            low(group, group),
            wide(8, group),
            low(4, 1, shard),
            wide(HEAD, HEAD),
            wide(1, HEAD),
            wide(HEAD, HEAD),
            low(64, 512),
            low(ny, nz, feed_shard, width),
            low(nz, feed_shard, width),
            low(4, feed_shard, width),
            low(nz, 2, 2, 2, shard, group),
            low(4, 2, 2, 2, shard, group),
            low(4, ny, 2, 2, shard, group),
            low(ny, 2, 2, shard, group),
            low(2, 2, shard, group),
            low(4, ny, shard, width),
            low(ny, shard, width),
            low(shard, width),
            low(2, 2, 2 * shard, half),
            low(2, 3, shard, half),
            low(3, 2, 2, shard, group),
            low(3, 3, shard, group),
            wide(32, width),
            wide(8, width),
            wide(8, width),
            wide(8, width),
            wide(nz - 1, 8, width),
            wide(8, width),
            wide(3, 8, width),
            dma((240,)),
            dma((240,)),
            dma((36,)),
            dma((2, 2, 2)),
            dma((2, 2, 2)),
            dma((2, 2, 2)),
            pltpu.SemaphoreType.REGULAR,
            pltpu.SemaphoreType.REGULAR,
            pltpu.SemaphoreType.REGULAR,
            pltpu.SemaphoreType.REGULAR,
        ],
        name="layer",
        cost_estimate=pl.CostEstimate(flops=45 * 10**9, bytes_accessed=20 * 10**6, transcendentals=0),
        compiler_params=pltpu.CompilerParams(
            collective_id=0, has_side_effects=True, vmem_limit_bytes=LIMIT
        ),
    )(
        lengths[:, 0], tokens, cotangent, mix_weight, out_weight, up_weight, down_weight, *norms,
        feature_freq, feature_scale[None], cosine_basis(), spread_rows(),
    )
    shapes = [w.shape for w in (mix_weight, out_weight, up_weight, down_weight)]
    one = SHAPE((1, shard), WIDE)
    results = pl.pallas_call(
        widen_kernel,
        out_shape=[SHAPE(out_rows.shape, LOW), SHAPE(out_rows.shape, WIDE), one, one, one, one]
        + [SHAPE(shape, WIDE) for shape in shapes],
        in_specs=[ANY] * 3 + [VMEM] + [ANY] * 4,
        out_specs=[ANY] * 2 + [VMEM] * 4 + [ANY] * 4,
        scratch_shapes=[low(*out_rows.shape)] * 3
        + [wide(*out_rows.shape)]
        + [kind(*shape) for shape in shapes[:2] for kind in (low, wide)]
        + [kind(*shape) for shape in shapes[2:] for kind in (low, wide)]
        + [dma((16,)), dma((16,))],
        name="widen",
    )(out_rows, grad_rows, cotangent, gains, gmix, gout, gup, gdown)
    rows, grads, *norm_grads = results[:6]
    return (rows, grads, *results[6:], *(part.reshape(shard) for part in norm_grads))


def solution(mesh):
    ny, nz = mesh.shape["dp"] // 2, mesh.shape["fsdp"] // 2
    grouped = ny == 2 and nz == 4 and D // mesh.size % 32 == 0
    body = partial(per_device_group, ny, nz) if grouped else per_device_plain
    rows = P(("dp", "fsdp"), None)
    vector = P(("dp", "fsdp"))
    slots = P(None, ("dp", "fsdp"), None)
    return jax.shard_map(
        body,
        mesh=mesh,
        in_specs=(slots, slots, *[rows] * 4, *[vector] * 4, P(), P(), slots),
        out_specs=(slots, slots, *[rows] * 4, *[vector] * 4),
        check_vma=False,
    )
```
